32 devices in a mesh: section: 4 (over y, x), dp: 8 (over z, core).
Axes of the slice: x: 2, y: 2, z: 4, core: 2. Of those that a mesh axis runs over, the one named last changes fastest.
Arguments:
- clean: bfloat16 [32, 16, 16, 384], P('dp'), may hold values from -12 to 12
- noise: bfloat16 [32, 16, 16, 384], P('dp'), may hold values from -6 to 6
- stamps: int32 [32], P('dp'), may hold values from 0 to 999
- enc_weight: bfloat16 [4, 3, 3, 384, 384], P('section'), may hold values from -0.109375 to 0.109375
- dec_weight: bfloat16 [4, 3, 3, 768, 384], P('section'), may hold values from -0.078125 to 0.078125
Outputs:
- enc_grad: float32 [4, 3, 3, 384, 384], P('section', None, None, 'dp')
- dec_grad: float32 [4, 3, 3, 768, 384], P('section', None, None, 'dp')
The draws below stay inside these ranges and needn't reach their ends.
All inputs are finite; a program needn't handle non-finite values.
Results may differ from the reference program's by a relative error of at most 0.0035.
Values sent between devices are 32-bit elements; how exact they have to be, the bound alone decides.
No kernel may reach another device: no remote copies, remote signals or barrier semaphores. Data moves between devices by JAX's collectives and lax.ppermute only.
A program may use at most 128 MiB of HBM per device.

```python
import math
import jax
import jax.numpy as jnp
from jax import lax

C = 384
GROUPS = 32
RES = 16
BATCH = 32
N_SECTION = 4


def draw_clean(key, part):
    base_key, scale_key = jax.random.split(key)
    scales = 0.3 * jnp.exp(jax.random.uniform(scale_key, (BATCH, 1, 1, C), jnp.float32, 0.0, math.log(10.0)))
    base_values = jnp.clip(jax.random.normal(base_key, (BATCH, RES, RES, C), jnp.float32), -4.0, 4.0)
    return (base_values * scales).astype(jnp.bfloat16)


def place_ends(result, key, smallest, largest):
    place = [jax.random.randint(jax.random.fold_in(key, axis), (), 0, length) for axis, length in enumerate(result.shape)]
    longest = result.shape.index(max(result.shape))
    next_to = place[:longest] + [(place[longest] + 1) % result.shape[longest]] + place[longest + 1:]
    return result.at[tuple(place)].set(smallest).at[tuple(next_to)].set(largest)


def block_scale(stream_key, dims, cuts, smallest, high):
    def one(position, parts):
        heights = jax.random.uniform(jax.random.fold_in(jax.random.fold_in(stream_key, 6), position), (parts,), jnp.float32, smallest / len(cuts), high / len(cuts))
        return jnp.repeat(jnp.exp(heights), dims[position] // parts).reshape((-1,) + (1,) * (len(dims) - position - 1))

    loudness = one(*cuts[0])
    for cut in cuts[1:]:
        loudness = loudness * one(*cut)
    return loudness


def bell_draw(own_key, shape, spread, reach, pieces=(), kind=jnp.bfloat16):
    array = spread * jax.random.normal(own_key, shape, jnp.float32)
    if pieces:
        array = array * block_scale(own_key, shape, pieces, -0.22, 0.18)
    return jnp.clip(array, -reach, reach).astype(kind)


def setup_inputs(seed: int = 0) -> dict:
    key_list = jax.random.split(jax.random.key(seed), 6)
    return {
        "clean": draw_clean(jax.random.fold_in(key_list[5], 71), 0),
        "noise": bell_draw(key_list[1], (BATCH, RES, RES, C), 1.0, 6.0, ((0, 8),)),
        "stamps": place_ends(jax.random.randint(key_list[2], (BATCH,), 0, 1000), jax.random.fold_in(key_list[2], 1), 0, 999).astype(jnp.int32),
        "enc_weight": bell_draw(key_list[3], (N_SECTION, 3, 3, C, C), (9 * C) ** -0.5, 0.109375, ((0, 4),)),
        "dec_weight": bell_draw(key_list[4], (N_SECTION, 3, 3, 2 * C, C), (18 * C) ** -0.5, 0.078125, ((0, 4),)),
    }


def embed(stamps_in, channels):
    half_width = channels // 2
    frequency = jnp.exp(-math.log(10000.0) * jnp.arange(half_width, dtype=jnp.float32) / half_width)
    angles = stamps_in.astype(jnp.float32)[:, None] * frequency[None, :]
    return jnp.concatenate([jnp.sin(angles), jnp.cos(angles)], axis=1)

def activate(inputs_f32, stamps_in):
    batch_rows, height, breadth, channels = inputs_f32.shape
    grouped = inputs_f32.reshape(batch_rows, height * breadth, GROUPS, channels // GROUPS)
    group_mean = lax.optimization_barrier(jnp.mean(grouped, axis=(1, 3), keepdims=True))
    centered = grouped - group_mean
    group_var = lax.optimization_barrier(jnp.mean(centered * centered, axis=(1, 3), keepdims=True))
    normed = (centered * lax.rsqrt(group_var + 1e-05)).reshape(inputs_f32.shape)
    modulate = 1.0 + 0.5 * embed(stamps_in, channels)[:, None, None, :]
    return jax.nn.silu(normed * modulate)

def conv_apply(activations, weight):
    batch_rows, height, breadth, channels = activations.shape
    padded = jnp.pad(activations, ((0, 0), (1, 1), (1, 1), (0, 0)))
    summed = jnp.zeros((batch_rows * height * breadth, weight.shape[3]), jnp.float32)
    for row_off in range(3):
        for col_off in range(3):
            window = padded[:, row_off:row_off + height, col_off:col_off + breadth, :].reshape(-1, channels)
            summed = summed + jnp.dot(window, weight[row_off, col_off], preferred_element_type=jnp.float32)
    return summed.reshape(batch_rows, height, breadth, weight.shape[3])

def conv_back(cotangent, weight):
    batch_rows, height, breadth, outputs = cotangent.shape
    padded = jnp.pad(cotangent.astype(jnp.bfloat16), ((0, 0), (1, 1), (1, 1), (0, 0)))
    summed = jnp.zeros((batch_rows * height * breadth, weight.shape[2]), jnp.float32)
    for row_off in range(3):
        for col_off in range(3):
            window = padded[:, 2 - row_off:2 - row_off + height, 2 - col_off:2 - col_off + breadth, :].reshape(-1, outputs)
            summed = summed + lax.dot_general(window, weight[row_off, col_off], (((1,), (1,)), ((), ())), preferred_element_type=jnp.float32)
    return summed.reshape(batch_rows, height, breadth, weight.shape[2])

def conv_weight_grad(activations, cotangent):
    batch_rows, height, breadth, channels = activations.shape
    padded = jnp.pad(activations, ((0, 0), (1, 1), (1, 1), (0, 0)))
    flat_cot = cotangent.astype(jnp.bfloat16).reshape(-1, cotangent.shape[3])
    kernel_rows = []
    for row_off in range(3):
        kernel_cols = []
        for col_off in range(3):
            window = padded[:, row_off:row_off + height, col_off:col_off + breadth, :].reshape(-1, channels)
            kernel_cols.append(lax.dot_general(window, flat_cot, (((0,), (0,)), ((), ())), preferred_element_type=jnp.float32))
        kernel_rows.append(jnp.stack(kernel_cols))
    return jnp.stack(kernel_rows)

def block_forward(inputs, residual, weight, stamps_in):
    activations = activate(inputs.astype(jnp.float32), stamps_in).astype(jnp.bfloat16)
    return residual.astype(jnp.float32) + conv_apply(activations, weight)

def block_backward(inputs, weight, stamps_in, cotangent):
    activated, pullback = jax.vjp(lambda inner_field: activate(inner_field, stamps_in), inputs.astype(jnp.float32))
    activations = activated.astype(jnp.bfloat16)
    weight_grad = conv_weight_grad(activations, cotangent)
    input_grad = pullback(conv_back(cotangent, weight))[0]
    return (input_grad, weight_grad)

def noise_levels(stamps_in):
    phase = (stamps_in.astype(jnp.float32) / 1000.0 + 0.008) / 1.008 * (math.pi / 2.0)
    signal = jnp.cos(phase) ** 2
    return (jnp.sqrt(signal), jnp.sqrt(1.0 - signal))

def reference(clean, noise, stamps, enc_weight, dec_weight):
    keep_level, spread_level = noise_levels(stamps)
    state_now = keep_level[:, None, None, None] * clean.astype(jnp.float32) + spread_level[:, None, None, None] * noise.astype(jnp.float32)
    enc_inputs = []
    skips = []
    for block_id in range(N_SECTION):
        enc_inputs.append(state_now)
        state_now = block_forward(state_now, state_now, enc_weight[block_id], stamps)
        skips.append(state_now)
    dec_inputs = [state_now] * N_SECTION
    for block_id in reversed(range(N_SECTION)):
        dec_inputs[block_id] = state_now
        joined = jnp.concatenate([state_now, skips[block_id]], axis=3)
        state_now = block_forward(joined, state_now, dec_weight[block_id], stamps)
    factor = 1.0 / math.sqrt(BATCH * RES * RES)
    flowing = factor * (state_now - noise.astype(jnp.float32))
    dec_grads = []
    skip_grads = []
    for block_id in range(N_SECTION):
        joined = jnp.concatenate([dec_inputs[block_id], skips[block_id]], axis=3)
        input_grad, weight_grad = block_backward(joined, dec_weight[block_id], stamps, flowing)
        dec_grads.append(weight_grad)
        skip_grads.append(input_grad[..., C:])
        flowing = input_grad[..., :C] + flowing
    enc_grads = [dec_grads[0]] * N_SECTION
    for block_id in reversed(range(N_SECTION)):
        merged = flowing + skip_grads[block_id]
        input_grad, weight_grad = block_backward(enc_inputs[block_id], enc_weight[block_id], stamps, merged)
        enc_grads[block_id] = weight_grad
        flowing = input_grad + merged
    return (jnp.stack(enc_grads), jnp.stack(dec_grads))
```

```python
import functools
import math

import jax
import jax.numpy as jnp
from jax import lax
from jax.experimental import pallas as pl
from jax.experimental.pallas import tpu as pltpu
from jax.sharding import PartitionSpec as P

GROUPS = 32
F32 = jnp.float32
BF16 = jnp.bfloat16
ENC_FWD, DEC_FWD, DEC_BWD, ENC_BWD = 1, 2, 3, 4
VMEM_LIMIT = 40 * 1024 * 1024


def embed(stamps_in, channels):
    half_width = channels // 2
    frequency = jnp.exp(-math.log(10000.0) * jnp.arange(half_width, dtype=jnp.float32) / half_width)
    angles = stamps_in.astype(jnp.float32)[:, None] * frequency[None, :]
    return jnp.concatenate([jnp.sin(angles), jnp.cos(angles)], axis=1)


def noise_levels(stamps_in):
    phase = (stamps_in.astype(jnp.float32) / 1000.0 + 0.008) / 1.008 * (math.pi / 2.0)
    signal = jnp.cos(phase) ** 2
    return (jnp.sqrt(signal), jnp.sqrt(1.0 - signal))


def stage_of(position, sections):
    lap, step = divmod(position, sections)
    section = step if lap % 2 == 0 else sections - 1 - step
    return section, lap + 1


def make_schedule(sections, samples):
    stages = 4 * sections
    ticks = []
    for tick in range(stages + 2 * (samples - 1)):
        work, moves = {}, []
        for sample in range(samples):
            position = tick - 2 * sample
            if not 0 <= position < stages:
                continue
            section, op = stage_of(position, sections)
            assert section not in work
            work[section] = (op, sample)
            if position + 1 < stages:
                target, _ = stage_of(position + 1, sections)
                if target != section:
                    moves.append((section, target))
        ticks.append((work, moves))
    return ticks


def schedule_table(ticks, sections):
    table = []
    for section in range(sections):
        row = []
        for work, _ in ticks:
            op, sample = work.get(section, (0, 0))
            first, last = section == 0, section == sections - 1
            from_here = (
                (op == ENC_FWD and first)
                or (op == DEC_FWD and last)
                or (op == DEC_BWD and first)
                or (op == ENC_BWD and last)
            )
            to_here = (
                op == ENC_FWD or (op == DEC_FWD and first) or (op == DEC_BWD and last)
            )
            row += [op, sample, int(from_here), int(to_here)]
        table.append(row)
    return table


def group_sums(vectors, members):
    channels = vectors[0].shape[1]
    row = lax.broadcasted_iota(jnp.int32, (16, channels), 0)
    stacked = jnp.zeros((16, channels), F32)
    for index, vector in enumerate(vectors):
        high = vector.astype(BF16).astype(F32)
        rest = vector - high
        middle = rest.astype(BF16).astype(F32)
        for part_index, part in enumerate((high, middle, rest - middle)):
            stacked = jnp.where(row == 3 * index + part_index, part, stacked)
    summed = jnp.dot(stacked.astype(BF16), members, preferred_element_type=F32)
    return [
        summed[3 * i : 3 * i + 1] + summed[3 * i + 1 : 3 * i + 2] + summed[3 * i + 2 : 3 * i + 3]
        for i in range(len(vectors))
    ]


def spread_columns(field, breadth, windows_ref):
    pixels, channels = field.shape
    column = lax.broadcasted_iota(jnp.int32, (pixels, channels), 0) & (breadth - 1)
    before = jnp.where(column == 0, 0.0, pltpu.roll(field, 1, 0))
    after = jnp.where(column == breadth - 1, 0.0, pltpu.roll(field, pixels - 1, 0))
    edge = jnp.zeros((breadth, channels), BF16)
    for index, shifted in enumerate((before, field, after)):
        lanes = slice(index * channels, (index + 1) * channels)
        windows_ref[0:breadth, lanes] = edge
        windows_ref[breadth : breadth + pixels, lanes] = shifted.astype(BF16)
        windows_ref[breadth + pixels : 2 * breadth + pixels, lanes] = edge


def convolve(windows_ref, weight_ref, pixels, breadth):
    taps, channels, outputs = weight_ref.shape
    total = None
    for row in range(3):
        part = jnp.dot(
            windows_ref[row * breadth : row * breadth + pixels, :],
            weight_ref[3 * row : 3 * row + 3].reshape(3 * channels, outputs),
            preferred_element_type=F32,
        )
        total = part if total is None else total + part
    return total


def convolve_back(windows_ref, weight_ref, pixels, breadth):
    taps, channels, outputs = weight_ref.shape
    total = None
    for row in range(3):
        for col in range(3):
            part = lax.dot_general(
                windows_ref[
                    (2 - row) * breadth : (2 - row) * breadth + pixels,
                    (2 - col) * outputs : (3 - col) * outputs,
                ],
                weight_ref[3 * row + col],
                (((1,), (1,)), ((), ())),
                preferred_element_type=F32,
            )
            total = part if total is None else total + part
    return total


def stage_kernel(
    tick,
    aside,
    sections,
    breadth,
    factor,
    has_forward,
    has_backward,
    table,
    arriving,
    modulation,
    members,
    enc_weight,
    dec_weight,
    noise,
    _kept,
    _side,
    _normed,
    _scale,
    _acts,
    _cots,
    leaving,
    kept,
    side,
    normed,
    scale,
    acts,
    cots,
    x_buf,
    e_buf,
    n_buf,
    h_buf,
    r_buf,
    a_buf,
    y_buf,
    m_buf,
    w_buf,
    windows,
    sems,
):
    pixels, channels = x_buf.shape
    op = table[4 * tick]
    slot = table[4 * tick + 1]
    from_here = table[4 * tick + 2]
    to_here = table[4 * tick + 3]
    is_enc = jnp.logical_or(op == ENC_FWD, op == ENC_BWD)

    def copy(source, target, sem):
        return pltpu.make_async_copy(source, target, sems.at[sem])

    group_size = channels // GROUPS
    if aside:
        kind = 2
        inverse_count = 1.0 / (pixels * 2 * group_size)
    else:
        kind = jnp.where(is_enc, 0, 1)
        inverse_count = jnp.where(
            is_enc, 1.0 / (pixels * group_size), 1.0 / (pixels * 2 * group_size)
        ).astype(F32)

    def start_weight():
        if aside:
            copy(dec_weight.at[:, channels : 2 * channels, :], w_buf, 0).start()
            copy(members.at[1], m_buf, 1).start()
        else:

            @pl.when(is_enc)
            def _():
                copy(enc_weight, w_buf, 0).start()

            @pl.when(jnp.logical_not(is_enc))
            def _():
                copy(dec_weight.at[:, 0:channels, :], w_buf, 0).start()

            copy(members.at[kind], m_buf, 1).start()

    def start_input():
        if aside:
            copy(kept.at[slot], x_buf, 2).start()
        else:

            @pl.when(from_here == 1)
            def _():
                copy(kept.at[slot], x_buf, 2).start()

            @pl.when(from_here == 0)
            def _():
                copy(arriving, x_buf, 2).start()

    def forward():
        start_input()
        start_weight()
        is_dec = op == DEC_FWD
        if not aside:

            @pl.when(is_dec)
            def _():
                copy(side.at[slot], e_buf, 3).start()

                @pl.when(to_here == 1)
                def _():
                    copy(noise.at[slot], n_buf, 4).start()

        copy(kept.at[slot], x_buf, 2).wait()
        copy(members.at[0], m_buf, 1).wait()
        x = x_buf[...]
        total = jnp.sum(x, axis=0, keepdims=True)
        own_mean = total * (1.0 / pixels)
        own_dev = x - own_mean
        own_square = jnp.sum(own_dev * own_dev, axis=0, keepdims=True)
        (group_total,) = group_sums([total], m_buf[...])
        mean = group_total * inverse_count
        apart = own_mean - mean
        (group_square,) = group_sums([own_square + pixels * (apart * apart)], m_buf[...])
        inverse_std = lax.rsqrt(group_square * inverse_count + 1e-05)
        unit = (x - mean) * inverse_std
        value = unit * modulation[kind, slot]
        active = value / (1.0 + jnp.exp(-value))
        h_buf[...] = unit
        r_buf[...] = inverse_std
        a_buf[...] = active.astype(BF16)
        spread_columns(active, breadth, windows)
        copy(h_buf, normed.at[kind, slot], 5).start()
        copy(r_buf, scale.at[kind, slot], 6).start()
        copy(a_buf, acts.at[kind, slot], 7).start()
        copy(enc_weight, w_buf, 0).wait()
        y = convolve(windows, w_buf, pixels, breadth)
        if aside:
            y_buf[...] = y
            out = copy(y_buf, side.at[slot], 8)
            out.start()
            out.wait()
        else:
            y = y + x_buf[...]
            y_buf[...] = y

            @pl.when(is_dec)
            def _():
                copy(side.at[slot], e_buf, 3).wait()
                y_buf[...] = y_buf[...] + e_buf[...]

                @pl.when(to_here == 1)
                def _():
                    copy(noise.at[slot], n_buf, 4).wait()
                    y_buf[...] = factor * (y_buf[...] - n_buf[...].astype(F32))

            send_result()
        copy(h_buf, normed.at[kind, slot], 5).wait()
        copy(r_buf, scale.at[kind, slot], 6).wait()
        copy(a_buf, acts.at[kind, slot], 7).wait()

    def send_result():
        out = copy(y_buf, leaving, 8)
        out.start()

        @pl.when(to_here == 1)
        def _():
            stay = copy(y_buf, kept.at[slot], 9)
            stay.start()
            stay.wait()

        out.wait()

    def backward():
        start_weight()
        which = 1 if aside else 1 - jnp.where(is_enc, 1, 0)
        if aside:
            copy(cots.at[1, slot], a_buf, 7).start()
        else:
            start_input()

            @pl.when(is_enc)
            def _():
                copy(side.at[slot], e_buf, 3).start()

        copy(normed.at[kind, slot], h_buf, 5).start()
        copy(scale.at[kind, slot], r_buf, 6).start()
        if aside:
            copy(cots.at[1, slot], a_buf, 7).wait()
            spread_columns(a_buf[...].astype(F32), breadth, windows)
        else:
            copy(kept.at[slot], x_buf, 2).wait()

            @pl.when(is_enc)
            def _():
                copy(side.at[slot], e_buf, 3).wait()
                x_buf[...] = x_buf[...] + e_buf[...]

            g = x_buf[...]
            a_buf[...] = g.astype(BF16)
            copy(a_buf, cots.at[which, slot], 7).start()
            spread_columns(g, breadth, windows)
        copy(enc_weight, w_buf, 0).wait()
        down = convolve_back(windows, w_buf, pixels, breadth)
        copy(normed.at[kind, slot], h_buf, 5).wait()
        copy(scale.at[kind, slot], r_buf, 6).wait()
        copy(members.at[0], m_buf, 1).wait()
        unit = h_buf[...]
        mod = modulation[kind, slot]
        value = unit * mod
        gate = 1.0 / (1.0 + jnp.exp(-value))
        slope = gate * (1.0 + value * (1.0 - gate))
        d_unit = down * slope * mod
        sums = group_sums(
            [
                jnp.sum(d_unit, axis=0, keepdims=True),
                jnp.sum(d_unit * unit, axis=0, keepdims=True),
            ],
            m_buf[...],
        )
        shift, stretch = sums[0] * inverse_count, sums[1] * inverse_count
        result = r_buf[...] * (d_unit - shift - unit * stretch)
        if aside:
            y_buf[...] = result
            out = copy(y_buf, side.at[slot], 8)
            out.start()
            out.wait()
        else:
            y_buf[...] = result + x_buf[...]
            send_result()
            copy(a_buf, cots.at[which, slot], 7).wait()

    if has_forward:
        pl.when(op == ENC_FWD if aside else jnp.logical_or(op == ENC_FWD, op == DEC_FWD))(forward)
    if has_backward:
        pl.when(op == DEC_BWD if aside else op >= DEC_BWD)(backward)


def call_stage(tick, aside, sections, breadth, factor, ops, table, arriving, consts, state):
    samples, pixels, channels = state[0].shape
    any_spec = pl.BlockSpec(memory_space=pl.ANY)
    vmem = pl.BlockSpec(memory_space=pltpu.VMEM)
    smem = pl.BlockSpec(memory_space=pltpu.SMEM)
    block = jax.ShapeDtypeStruct((pixels, channels), F32)
    n_state = len(state)
    fresh = state[1] is None or not isinstance(state[1], jax.Array)
    if aside:
        has_forward, has_backward = ENC_FWD in ops, DEC_BWD in ops
    else:
        has_forward = ENC_FWD in ops or DEC_FWD in ops
        has_backward = DEC_BWD in ops or ENC_BWD in ops
    modulation, members, enc_weight, dec_weight, noise = consts
    body = functools.partial(
        stage_kernel, tick, aside, sections, breadth, factor, has_forward, has_backward
    )
    given = [table, arriving, modulation, members, enc_weight, dec_weight, noise]
    first_state = len(given)
    present = [i for i, leaf in enumerate(state) if not isinstance(leaf, jax.ShapeDtypeStruct)]

    def kernel(*refs):
        head = list(refs[:first_state])
        tail = list(refs[first_state + len(present) :])
        if aside:
            tail = [None] + tail
        body(*head, *([None] * n_state), *tail)

    state_shapes = [jax.ShapeDtypeStruct(leaf.shape, leaf.dtype) for leaf in state]
    shift = 0 if aside else 1
    outs = pl.pallas_call(
        kernel,
        out_shape=([] if aside else [block]) + state_shapes,
        in_specs=[smem, any_spec, vmem] + [any_spec] * (4 + len(present)),
        out_specs=[any_spec] * (n_state + shift),
        scratch_shapes=[
            pltpu.VMEM((pixels, channels), F32),
            pltpu.VMEM((pixels, channels), F32),
            pltpu.VMEM((pixels, channels), BF16),
            pltpu.VMEM((pixels, channels), F32),
            pltpu.VMEM((1, channels), F32),
            pltpu.VMEM((pixels, channels), BF16),
            pltpu.VMEM((pixels, channels), F32),
            pltpu.VMEM((channels, channels), BF16),
            pltpu.VMEM(enc_weight.shape, BF16),
            pltpu.VMEM((pixels + 2 * breadth, 3 * channels), BF16),
            pltpu.SemaphoreType.DMA((10,)),
        ],
        input_output_aliases={first_state + j: i + shift for j, i in enumerate(present)},
        compiler_params=pltpu.CompilerParams(vmem_limit_bytes=VMEM_LIMIT),
        cost_estimate=pl.CostEstimate(
            flops=2 * 9 * pixels * channels * channels,
            bytes_accessed=10 * pixels * channels * 4,
            transcendentals=0,
        ),
    )(*given, *[state[i] for i in present])
    outs = list(outs)
    if aside:
        return None, outs
    return outs[0], outs[1:]


def weight_grad_kernel(breadth, acts, cots, out, flipped, windows):
    halves, samples, pixels, channels = acts.shape
    tap = pl.program_id(0)

    @pl.when(tap == 0)
    def _():
        for half in range(halves):
            for sample in range(samples):
                flipped[
                    half * channels : (half + 1) * channels, sample * pixels : (sample + 1) * pixels
                ] = acts[half, sample].astype(F32).T.astype(BF16)
        edge = jnp.zeros((breadth, channels), BF16)
        column = lax.broadcasted_iota(jnp.int32, (pixels, channels), 0) & (breadth - 1)
        for sample in range(samples):
            field = cots[0, sample].astype(F32)
            before = jnp.where(column == 0, 0.0, pltpu.roll(field, 1, 0))
            after = jnp.where(column == breadth - 1, 0.0, pltpu.roll(field, pixels - 1, 0))
            for index, shifted in enumerate((before, field, after)):
                windows[index, sample, 0:breadth, :] = edge
                windows[index, sample, breadth : breadth + pixels, :] = shifted.astype(BF16)
                windows[index, sample, breadth + pixels : 2 * breadth + pixels, :] = edge

    row, col = tap // 3, tap % 3
    start = pl.multiple_of((2 - row) * breadth, breadth)
    total = None
    for sample in range(samples):
        part = jnp.dot(
            flipped[:, sample * pixels : (sample + 1) * pixels],
            windows[2 - col, sample, pl.ds(start, pixels), :],
            preferred_element_type=F32,
        )
        total = part if total is None else total + part
    out[0] = total


def weight_grad(acts, cots, halves, breadth):
    _, samples, pixels, channels = acts.shape
    first_half = 0 if halves == 1 else 1
    which = 0 if halves == 1 else 1
    acts = acts[first_half : first_half + halves]
    return pl.pallas_call(
        functools.partial(weight_grad_kernel, breadth),
        grid=(9,),
        out_shape=jax.ShapeDtypeStruct((9, halves * channels, channels), F32),
        in_specs=[
            pl.BlockSpec((halves, samples, pixels, channels), lambda tap: (0, 0, 0, 0)),
            pl.BlockSpec((1, samples, pixels, channels), lambda tap: (which, 0, 0, 0)),
        ],
        out_specs=pl.BlockSpec((1, halves * channels, channels), lambda tap: (tap, 0, 0)),
        scratch_shapes=[
            pltpu.VMEM((halves * channels, samples * pixels), BF16),
            pltpu.VMEM((3, samples, pixels + 2 * breadth, channels), BF16),
        ],
        compiler_params=pltpu.CompilerParams(vmem_limit_bytes=VMEM_LIMIT),
        cost_estimate=pl.CostEstimate(
            flops=2 * 9 * samples * pixels * channels * channels * halves,
            bytes_accessed=9 * halves * channels * channels * 4,
            transcendentals=0,
        ),
    )(acts, cots)


def shards(clean, noise, stamps, enc_weight, dec_weight):
    sections = lax.axis_size("section")
    section_index = lax.axis_index("section")
    samples, height, breadth, channels = clean.shape
    pixels = height * breadth
    factor = 1.0 / math.sqrt(samples * lax.axis_size("dp") * pixels)

    ticks = make_schedule(sections, samples)
    table = jnp.asarray(schedule_table(ticks, sections), jnp.int32)[section_index]

    keep_level, spread_level = noise_levels(stamps)
    noise = noise.reshape(samples, pixels, channels)
    noisy = keep_level[:, None, None] * clean.reshape(noise.shape).astype(F32) + spread_level[
        :, None, None
    ] * noise.astype(F32)

    wide = embed(stamps, 2 * channels)
    modulation = 1.0 + 0.5 * jnp.stack(
        [embed(stamps, channels), wide[:, :channels], wide[:, channels:]]
    )
    modulation = modulation[:, :, None, :]
    channel = jnp.arange(channels)
    group_size = channels // GROUPS
    members = jnp.stack(
        [
            (channel[:, None] // size == channel[None, :] // size).astype(BF16)
            for size in (group_size, 2 * group_size)
        ]
    )
    enc_kernel = enc_weight.reshape(9, channels, channels)
    dec_kernel = dec_weight.reshape(9, 2 * channels, channels)
    consts = (modulation, members, enc_kernel, dec_kernel, noise)

    fresh = jax.ShapeDtypeStruct
    state = [
        noisy,
        fresh((samples, pixels, channels), F32),
        fresh((3, samples, pixels, channels), F32),
        fresh((3, samples, 1, channels), F32),
        fresh((3, samples, pixels, channels), BF16),
        fresh((2, samples, pixels, channels), BF16),
    ]
    arriving = noisy[0]
    dec_done = max(
        tick for tick, (work, _) in enumerate(ticks) if any(w[0] == DEC_BWD for w in work.values())
    )
    dec_share = None
    for tick, (work, moves) in enumerate(ticks):
        ops = {op for op, _ in work.values()}
        leaving, state = call_stage(
            tick, False, sections, breadth, factor, ops, table, arriving, consts, state
        )
        if moves:
            arriving = lax.ppermute(leaving, "section", moves)
        if ops & {ENC_FWD, DEC_BWD}:
            _, state = call_stage(
                tick, True, sections, breadth, factor, ops, table, arriving_before(leaving), consts, state
            )
        if tick == dec_done:
            dec_grad = weight_grad(state[4], state[5], 2, breadth)
            dec_share = lax.psum_scatter(
                dec_grad.reshape((1, 3, 3, 2 * channels, channels)),
                "dp",
                scatter_dimension=3,
                tiled=True,
            )
    enc_grad = weight_grad(state[4], state[5], 1, breadth)
    enc_share = lax.psum_scatter(
        enc_grad.reshape((1, 3, 3, channels, channels)), "dp", scatter_dimension=3, tiled=True
    )
    return (enc_share, dec_share)


def arriving_before(leaving):
    return leaving


def solution(mesh):
    placed = (
        P("dp", None, None, None),
        P("dp", None, None, None),
        P("dp"),
        P("section", None, None, None, None),
        P("section", None, None, None, None),
    )
    return jax.shard_map(
        shards,
        mesh=mesh,
        in_specs=placed,
        out_specs=(P("section", None, None, "dp", None), P("section", None, None, "dp", None)),
        check_vma=False,
    )
```

```python
import functools
import math

import jax
import jax.numpy as jnp
import ml_dtypes
import numpy as np
from jax import lax
from jax.experimental import pallas as pl
from jax.experimental.pallas import tpu as pltpu
from jax.sharding import PartitionSpec as P

GROUPS = 32
F32 = jnp.float32
BF16 = jnp.bfloat16
ENC_FWD, DEC_FWD, DEC_BWD, ENC_BWD = 1, 2, 3, 4
VMEM_LIMIT = 40 * 1024 * 1024
STAGE_VMEM = 8 * 1024 * 1024


def embed(stamps_in, channels):
    half_width = channels // 2
    frequency = jnp.exp(-math.log(10000.0) * jnp.arange(half_width, dtype=jnp.float32) / half_width)
    angles = stamps_in.astype(jnp.float32)[:, None] * frequency[None, :]
    return jnp.concatenate([jnp.sin(angles), jnp.cos(angles)], axis=1)


def noise_levels(stamps_in):
    phase = (stamps_in.astype(jnp.float32) / 1000.0 + 0.008) / 1.008 * (math.pi / 2.0)
    signal = jnp.cos(phase) ** 2
    return (jnp.sqrt(signal), jnp.sqrt(1.0 - signal))


def stage_of(position, sections):
    lap, step = divmod(position, sections)
    section = step if lap % 2 == 0 else sections - 1 - step
    return section, lap + 1


def make_schedule(sections, samples):
    stages = 4 * sections
    ticks = []
    for tick in range(stages + 2 * (samples - 1)):
        work, moves = {}, []
        for sample in range(samples):
            position = tick - 2 * sample
            if not 0 <= position < stages:
                continue
            section, op = stage_of(position, sections)
            assert section not in work
            work[section] = (op, sample)
            if position + 1 < stages:
                target, _ = stage_of(position + 1, sections)
                if target != section:
                    moves.append((section, target))
        ticks.append((work, moves))
    return ticks


def group_sums(vectors, members):
    channels = vectors[0].shape[1]
    row = lax.broadcasted_iota(jnp.int32, (16, channels), 0)
    stacked = jnp.zeros((16, channels), F32)
    for index, vector in enumerate(vectors):
        high = vector.astype(BF16).astype(F32)
        rest = vector - high
        middle = rest.astype(BF16).astype(F32)
        for part_index, part in enumerate((high, middle, rest - middle)):
            stacked = jnp.where(row == 3 * index + part_index, part, stacked)
    summed = jnp.dot(stacked.astype(BF16), members, preferred_element_type=F32)
    return [
        summed[3 * i : 3 * i + 1] + summed[3 * i + 1 : 3 * i + 2] + summed[3 * i + 2 : 3 * i + 3]
        for i in range(len(vectors))
    ]


def spread_columns(field, breadth, windows_ref):
    pixels, channels = field.shape
    column = lax.broadcasted_iota(jnp.int32, (pixels, channels), 0) & (breadth - 1)
    before = jnp.where(column == 0, 0.0, pltpu.roll(field, 1, 0))
    after = jnp.where(column == breadth - 1, 0.0, pltpu.roll(field, pixels - 1, 0))
    edge = jnp.zeros((breadth, channels), BF16)
    for index, shifted in enumerate((before, field, after)):
        lanes = slice(index * channels, (index + 1) * channels)
        windows_ref[0:breadth, lanes] = edge
        windows_ref[breadth : breadth + pixels, lanes] = shifted.astype(BF16)
        windows_ref[breadth + pixels : 2 * breadth + pixels, lanes] = edge


def convolve(windows_ref, weight_ref, pixels, breadth):
    taps, channels, outputs = weight_ref.shape
    total = None
    for row in range(3):
        part = jnp.dot(
            windows_ref[row * breadth : row * breadth + pixels, :],
            weight_ref[3 * row : 3 * row + 3].reshape(3 * channels, outputs),
            preferred_element_type=F32,
        )
        total = part if total is None else total + part
    return total


def chosen(index, values):
    result = jnp.int32(values[0])
    for position, value in enumerate(values):
        if value != values[0]:
            result = jnp.where(index == position, value, result)
    return result


def local_input(op, section, sections):
    return (op in (ENC_FWD, DEC_BWD) and section == 0) or (
        op in (DEC_FWD, ENC_BWD) and section == sections - 1
    )


def local_result(op, section, sections):
    return (
        op == ENC_FWD
        or (op == DEC_FWD and section == 0)
        or (op == DEC_BWD and section == sections - 1)
    )


STATE = ("kept", "side", "normed", "scale", "acts", "cots")


def stage_kernel(work, aside, sections, breadth, factor, refs):
    pixels, channels = refs["kept"].shape[1:]
    section = lax.axis_index("section")
    jobs = [work.get(s, (0, 0)) for s in range(sections)]
    ops = {op for op, _ in jobs}
    op = chosen(section, [job[0] for job in jobs])
    slot = chosen(section, [job[1] for job in jobs])
    from_here = chosen(section, [int(local_input(job[0], s, sections)) for s, job in enumerate(jobs)])
    to_here = chosen(section, [int(local_result(job[0], s, sections)) for s, job in enumerate(jobs)])
    kept, side, normed, scale = (refs[name] for name in ("kept", "side", "normed", "scale"))
    acts, cots, windows = (refs[name] for name in ("acts", "cots", "windows"))
    members, modulation = (refs[name] for name in ("members", "modulation"))
    group_size = channels // GROUPS
    fewer, more = 1.0 / (pixels * group_size), 1.0 / (pixels * 2 * group_size)

    def pick(is_dec):
        if aside:
            return 2, 1, F32(more)
        kind = jnp.where(is_dec, 1, 0)
        return kind, kind, jnp.where(is_dec, F32(more), F32(fewer))

    def load_input():
        if aside or "arriving" not in refs:
            return kept[slot]
        if not any(local_input(job[0], s, sections) for s, job in enumerate(jobs)):
            return refs["arriving"][...]
        return jnp.where(from_here == 1, kept[slot], refs["arriving"][...])

    def forward():
        is_dec = op == DEC_FWD
        kind, which, inverse_count = pick(is_dec)
        x = load_input()
        if not aside:
            refs["leaving"][...] = x
        total = jnp.sum(x, axis=0, keepdims=True)
        own_mean = total * (1.0 / pixels)
        own_dev = x - own_mean
        own_square = jnp.sum(own_dev * own_dev, axis=0, keepdims=True)
        (group_total,) = group_sums([total], members[which])
        mean = group_total * inverse_count
        apart = own_mean - mean
        (group_square,) = group_sums([own_square + pixels * (apart * apart)], members[which])
        inverse_std = lax.rsqrt(group_square * inverse_count + 1e-05)
        unit = (x - mean) * inverse_std
        value = unit * modulation[kind, slot]
        active = value / (1.0 + jnp.exp(-value))
        normed[kind, slot] = unit
        scale[kind, slot] = inverse_std
        acts[kind, slot] = active.astype(BF16)
        spread_columns(active, breadth, windows)
        y = convolve(windows, refs["weights"].at[kind], pixels, breadth)
        if aside:
            side[slot] = y
            return
        leaving = refs["leaving"]
        leaving[...] = leaving[...] + y
        if DEC_FWD in ops:

            @pl.when(is_dec)
            def _():
                leaving[...] = leaving[...] + side[slot]

                @pl.when(to_here == 1)
                def _():
                    leaving[...] = factor * (leaving[...] - refs["noise"][slot].astype(F32))

        keep_result()

    def keep_result():
        if any(local_result(job[0], s, sections) for s, job in enumerate(jobs)):

            @pl.when(to_here == 1)
            def _():
                kept[slot] = refs["leaving"][...]

    def backward():
        is_dec = op == DEC_BWD
        kind, which, inverse_count = pick(is_dec)
        if aside:
            spread_columns(cots[1, slot].astype(F32), breadth, windows)
        else:
            leaving = refs["leaving"]
            leaving[...] = load_input()
            if ENC_BWD in ops:

                @pl.when(op == ENC_BWD)
                def _():
                    leaving[...] = leaving[...] + side[slot]

            g = leaving[...]
            cots[kind, slot] = g.astype(BF16)
            spread_columns(g, breadth, windows)
        down = convolve(windows, refs["flipped"].at[kind], pixels, breadth)
        unit = normed[kind, slot]
        mod = modulation[kind, slot]
        value = unit * mod
        gate = 1.0 / (1.0 + jnp.exp(-value))
        slope = gate * (1.0 + value * (1.0 - gate))
        d_unit = down * slope * mod
        sums = group_sums(
            [
                jnp.sum(d_unit, axis=0, keepdims=True),
                jnp.sum(d_unit * unit, axis=0, keepdims=True),
            ],
            members[which],
        )
        shift, stretch = sums[0] * inverse_count, sums[1] * inverse_count
        result = scale[kind, slot] * (d_unit - shift - unit * stretch)
        if aside:
            side[slot] = result
        else:
            leaving[...] = leaving[...] + result
            keep_result()

    if aside:
        if ENC_FWD in ops:
            pl.when(op == ENC_FWD)(forward)
        if DEC_BWD in ops:
            pl.when(op == DEC_BWD)(backward)
    else:
        if ops & {ENC_FWD, DEC_FWD}:
            pl.when(jnp.logical_or(op == ENC_FWD, op == DEC_FWD))(forward)
        if ops & {DEC_BWD, ENC_BWD}:
            pl.when(op >= DEC_BWD)(backward)


def call_stage(work, aside, sections, breadth, factor, arriving, consts, state):
    ops = {op for op, _ in work.values()}
    samples, pixels, channels = state["kept"].shape
    vmem = pl.BlockSpec(memory_space=pltpu.VMEM)
    forward = ENC_FWD in ops if aside else bool(ops & {ENC_FWD, DEC_FWD})
    backward = DEC_BWD in ops if aside else bool(ops & {DEC_BWD, ENC_BWD})
    given = {name: consts[name] for name in ("modulation", "members")}
    if forward:
        given["weights"] = consts["weights"]
    if backward:
        given["flipped"] = consts["flipped"]
    if DEC_FWD in ops and not aside:
        given["noise"] = consts["noise"]
    if not aside and any(not local_input(op, s, sections) for s, (op, _) in work.items()):
        given["arriving"] = arriving
    present = [n for n in STATE if not isinstance(state[n], jax.ShapeDtypeStruct)]
    out_shape = {} if aside else {"leaving": jax.ShapeDtypeStruct((pixels, channels), F32)}
    for name in STATE:
        out_shape[name] = jax.ShapeDtypeStruct(state[name].shape, state[name].dtype)
    out_names = list(out_shape)

    def kernel(*refs):
        named = dict(zip(given, refs))
        named.update(zip(out_names, refs[len(given) + len(present) :]))
        named["windows"] = refs[-1]
        stage_kernel(work, aside, sections, breadth, factor, named)

    outs = pl.pallas_call(
        kernel,
        out_shape=list(out_shape.values()),
        in_specs=[vmem] * (len(given) + len(present)),
        out_specs=[vmem] * len(out_shape),
        scratch_shapes=[pltpu.VMEM((pixels + 2 * breadth, 3 * channels), BF16)],
        input_output_aliases={
            len(given) + i: out_names.index(name) for i, name in enumerate(present)
        },
        compiler_params=pltpu.CompilerParams(vmem_limit_bytes=STAGE_VMEM),
        cost_estimate=pl.CostEstimate(
            flops=2 * 9 * pixels * channels * channels,
            bytes_accessed=4 * pixels * channels,
            transcendentals=0,
        ),
    )(*given.values(), *[state[n] for n in present])
    named = dict(zip(out_names, outs))
    return named.pop("leaving", None), named


def prepare_kernel(levels, clean, noise, enc_weight, dec_weight, noisy, weights, sems):
    channels = enc_weight.shape[2]
    copies = [
        pltpu.make_async_copy(enc_weight, weights.at[0], sems.at[0]),
        pltpu.make_async_copy(dec_weight.at[:, 0:channels, :], weights.at[1], sems.at[1]),
        pltpu.make_async_copy(
            dec_weight.at[:, channels : 2 * channels, :], weights.at[2], sems.at[2]
        ),
    ]
    for one in copies:
        one.start()
    for sample in range(clean.shape[0]):
        noisy[sample] = levels[0, sample] * clean[sample].astype(F32) + levels[
            1, sample
        ] * noise[sample].astype(F32)
    for one in copies:
        one.wait()


def prepare(levels, clean, noise, enc_weight, dec_weight):
    vmem = pl.BlockSpec(memory_space=pltpu.VMEM)
    any_spec = pl.BlockSpec(memory_space=pl.ANY)
    return pl.pallas_call(
        prepare_kernel,
        out_shape=[
            jax.ShapeDtypeStruct(clean.shape, F32),
            jax.ShapeDtypeStruct((3,) + enc_weight.shape, BF16),
        ],
        in_specs=[vmem] * 3 + [any_spec] * 2,
        out_specs=[vmem] * 2,
        scratch_shapes=[pltpu.SemaphoreType.DMA((3,))],
        compiler_params=pltpu.CompilerParams(vmem_limit_bytes=VMEM_LIMIT),
    )(levels, clean, noise, enc_weight, dec_weight)


def flip_kernel(core, weights, *refs):
    flipped = refs[-1]
    taps = weights.shape[1]

    @pl.when(lax.axis_index("dp") % 2 == core)
    def _():
        def one(tap, carry):
            for kind in range(3):
                flipped[kind, taps - 1 - tap] = weights[kind, tap].astype(F32).T.astype(BF16)
            return carry

        lax.fori_loop(0, taps, one, 0)


def flip(core, weights, flipped):
    vmem = pl.BlockSpec(memory_space=pltpu.VMEM)
    return pl.pallas_call(
        functools.partial(flip_kernel, core),
        out_shape=jax.ShapeDtypeStruct(weights.shape, BF16),
        in_specs=[vmem] * (1 if flipped is None else 2),
        out_specs=vmem,
        input_output_aliases={} if flipped is None else {1: 0},
        compiler_params=pltpu.CompilerParams(vmem_limit_bytes=STAGE_VMEM),
    )(weights, *([] if flipped is None else [flipped]))


def weight_grad_kernel(breadth, kinds, which, acts, cots, out, flipped, windows):
    _, samples, pixels, channels = acts.shape
    tap = pl.program_id(0)

    @pl.when(tap == 0)
    def _():
        for half, kind in enumerate(kinds):
            for sample in range(samples):
                flipped[
                    half * channels : (half + 1) * channels, sample * pixels : (sample + 1) * pixels
                ] = acts[kind, sample].astype(F32).T.astype(BF16)
        edge = jnp.zeros((breadth, channels), BF16)
        column = lax.broadcasted_iota(jnp.int32, (pixels, channels), 0) & (breadth - 1)
        for sample in range(samples):
            field = cots[which, sample].astype(F32)
            before = jnp.where(column == 0, 0.0, pltpu.roll(field, 1, 0))
            after = jnp.where(column == breadth - 1, 0.0, pltpu.roll(field, pixels - 1, 0))
            for index, shifted in enumerate((before, field, after)):
                windows[index, sample, 0:breadth, :] = edge
                windows[index, sample, breadth : breadth + pixels, :] = shifted.astype(BF16)
                windows[index, sample, breadth + pixels : 2 * breadth + pixels, :] = edge

    row, col = tap // 3, tap % 3
    start = pl.multiple_of((2 - row) * breadth, breadth)
    total = None
    for sample in range(samples):
        part = jnp.dot(
            flipped[:, sample * pixels : (sample + 1) * pixels],
            windows[2 - col, sample, pl.ds(start, pixels), :],
            preferred_element_type=F32,
        )
        total = part if total is None else total + part
    out[0] = total


def weight_grad(acts, cots, kinds, which, breadth):
    _, samples, pixels, channels = acts.shape
    halves = len(kinds)
    return pl.pallas_call(
        functools.partial(weight_grad_kernel, breadth, kinds, which),
        grid=(9,),
        out_shape=jax.ShapeDtypeStruct((9, halves * channels, channels), F32),
        in_specs=[
            pl.BlockSpec(acts.shape, lambda tap: (0, 0, 0, 0)),
            pl.BlockSpec(cots.shape, lambda tap: (0, 0, 0, 0)),
        ],
        out_specs=pl.BlockSpec((1, halves * channels, channels), lambda tap: (tap, 0, 0)),
        scratch_shapes=[
            pltpu.VMEM((halves * channels, samples * pixels), BF16),
            pltpu.VMEM((3, samples, pixels + 2 * breadth, channels), BF16),
        ],
        compiler_params=pltpu.CompilerParams(vmem_limit_bytes=VMEM_LIMIT),
        cost_estimate=pl.CostEstimate(
            flops=2 * 9 * samples * pixels * channels * channels * halves,
            bytes_accessed=9 * halves * channels * channels * 4,
            transcendentals=0,
        ),
    )(acts, cots)


def member_matrices(channels):
    channel = np.arange(channels)
    size = channels // GROUPS
    return np.stack(
        [channel[:, None] // n == channel[None, :] // n for n in (size, 2 * size)]
    ).astype(ml_dtypes.bfloat16)


def shards(clean, noise, stamps, enc_weight, dec_weight):
    sections = lax.axis_size("section")
    samples, height, breadth, channels = clean.shape
    pixels = height * breadth
    factor = 1.0 / math.sqrt(samples * lax.axis_size("dp") * pixels)
    ticks = make_schedule(sections, samples)

    levels = jnp.stack(noise_levels(stamps))
    levels = jnp.broadcast_to(levels[:, :, None, None], (2, samples, 1, channels))
    noise = noise.reshape(samples, pixels, channels)
    noisy, weights = prepare(
        levels,
        clean.reshape(noise.shape),
        noise,
        enc_weight.reshape(9, channels, channels),
        dec_weight.reshape(9, 2 * channels, channels),
    )
    wide = embed(stamps, 2 * channels)
    modulation = 1.0 + 0.5 * jnp.stack(
        [embed(stamps, channels), wide[:, :channels], wide[:, channels:]]
    )
    consts = {
        "modulation": modulation[:, :, None, :],
        "members": jnp.asarray(member_matrices(channels)),
        "weights": weights,
        "noise": noise,
    }
    consts["flipped"] = flip(1, weights, None)

    fresh = jax.ShapeDtypeStruct
    state = {
        "kept": noisy,
        "side": fresh((samples, pixels, channels), F32),
        "normed": fresh((3, samples, pixels, channels), F32),
        "scale": fresh((3, samples, 1, channels), F32),
        "acts": fresh((3, samples, pixels, channels), BF16),
        "cots": fresh((2, samples, pixels, channels), BF16),
    }
    state["kept"], consts["flipped"] = lax.optimization_barrier(
        (state["kept"], consts["flipped"])
    )
    arriving = None
    dec_done = max(
        tick for tick, (work, _) in enumerate(ticks) if any(w[0] == DEC_BWD for w in work.values())
    )
    for tick, (work, moves) in enumerate(ticks):
        ops = {op for op, _ in work.values()}
        leaving, state = call_stage(
            work, False, sections, breadth, factor, arriving, consts, state
        )
        if moves:
            arriving = lax.ppermute(leaving, "section", moves)
        if tick == 0:
            state["kept"], consts["weights"] = lax.optimization_barrier(
                (state["kept"], consts["weights"])
            )
            consts["flipped"] = flip(0, consts["weights"], consts["flipped"])
        if ops & {ENC_FWD, DEC_BWD}:
            _, state = call_stage(work, True, sections, breadth, factor, None, consts, state)
        if tick == dec_done:
            dec_grad = weight_grad(state["acts"], state["cots"], (1, 2), 1, breadth)
            dec_share = lax.psum_scatter(
                dec_grad.reshape((1, 3, 3, 2 * channels, channels)),
                "dp",
                scatter_dimension=3,
                tiled=True,
            )
    enc_grad = weight_grad(state["acts"], state["cots"], (0,), 0, breadth)
    enc_grad, dec_share = lax.optimization_barrier((enc_grad, dec_share))
    enc_share = lax.psum_scatter(
        enc_grad.reshape((1, 3, 3, channels, channels)), "dp", scatter_dimension=3, tiled=True
    )
    return (enc_share, dec_share)


def solution(mesh):
    placed = (
        P("dp", None, None, None),
        P("dp", None, None, None),
        P("dp"),
        P("section", None, None, None, None),
        P("section", None, None, None, None),
    )
    return jax.shard_map(
        shards,
        mesh=mesh,
        in_specs=placed,
        out_specs=(P("section", None, None, "dp", None), P("section", None, None, "dp", None)),
        check_vma=False,
    )
```

```python
import functools
import math

import jax
import jax.numpy as jnp
import ml_dtypes
import numpy as np
from jax import lax
from jax.experimental import pallas as pl
from jax.experimental.pallas import tpu as pltpu
from jax.sharding import PartitionSpec as P

GROUPS = 32
F32 = jnp.float32
BF16 = jnp.bfloat16
ENC_FWD, DEC_FWD, DEC_BWD, ENC_BWD = 1, 2, 3, 4
STAGE_VMEM = 8 * 1024 * 1024
GRAD_VMEM = 20 * 1024 * 1024


def embed(stamps_in, channels):
    half_width = channels // 2
    frequency = jnp.exp(-math.log(10000.0) * jnp.arange(half_width, dtype=jnp.float32) / half_width)
    angles = stamps_in.astype(jnp.float32)[:, None] * frequency[None, :]
    return jnp.concatenate([jnp.sin(angles), jnp.cos(angles)], axis=1)


def noise_levels(stamps_in):
    phase = (stamps_in.astype(jnp.float32) / 1000.0 + 0.008) / 1.008 * (math.pi / 2.0)
    signal = jnp.cos(phase) ** 2
    return (jnp.sqrt(signal), jnp.sqrt(1.0 - signal))


def stage_of(position, sections):
    lap, step = divmod(position, sections)
    section = step if lap % 2 == 0 else sections - 1 - step
    return section, lap + 1


def make_schedule(sections, samples):
    stages = 4 * sections
    ticks = []
    for tick in range(stages + 2 * (samples - 1)):
        work, moves = {}, []
        for sample in range(samples):
            position = tick - 2 * sample
            if not 0 <= position < stages:
                continue
            section, op = stage_of(position, sections)
            assert section not in work
            work[section] = (op, sample)
            if position + 1 < stages:
                target, _ = stage_of(position + 1, sections)
                if target != section:
                    moves.append((section, target))
        ticks.append((work, moves))
    return ticks


def group_sums(vectors, members):
    channels = vectors[0].shape[1]
    row = lax.broadcasted_iota(jnp.int32, (16, channels), 0)
    stacked = jnp.zeros((16, channels), F32)
    for index, vector in enumerate(vectors):
        high = vector.astype(BF16).astype(F32)
        rest = vector - high
        middle = rest.astype(BF16).astype(F32)
        for part_index, part in enumerate((high, middle, rest - middle)):
            stacked = jnp.where(row == 3 * index + part_index, part, stacked)
    summed = jnp.dot(stacked.astype(BF16), members, preferred_element_type=F32)
    return [
        summed[3 * i : 3 * i + 1] + summed[3 * i + 1 : 3 * i + 2] + summed[3 * i + 2 : 3 * i + 3]
        for i in range(len(vectors))
    ]


def spread_columns(field, breadth, windows_ref):
    pixels, channels = field.shape
    column = lax.broadcasted_iota(jnp.int32, (pixels, channels), 0) & (breadth - 1)
    before = jnp.where(column == 0, 0.0, pltpu.roll(field, 1, 0))
    after = jnp.where(column == breadth - 1, 0.0, pltpu.roll(field, pixels - 1, 0))
    edge = jnp.zeros((breadth, channels), BF16)
    for index, shifted in enumerate((before, field, after)):
        lanes = slice(index * channels, (index + 1) * channels)
        windows_ref[0:breadth, lanes] = edge
        windows_ref[breadth : breadth + pixels, lanes] = shifted.astype(BF16)
        windows_ref[breadth + pixels : 2 * breadth + pixels, lanes] = edge


def convolve(windows_ref, weight_ref, first, pixels, breadth):
    outputs = weight_ref.shape[2]
    channels = windows_ref.shape[1] // 3
    total = None
    for row in range(3):
        part = jnp.dot(
            windows_ref[row * breadth : row * breadth + pixels, :],
            weight_ref[3 * row : 3 * row + 3, first : first + channels, :].reshape(
                3 * channels, outputs
            ),
            preferred_element_type=F32,
        )
        total = part if total is None else total + part
    return total


def chosen(index, values):
    result = jnp.int32(values[0])
    for position, value in enumerate(values):
        if value != values[0]:
            result = jnp.where(index == position, value, result)
    return result


def local_input(op, section, sections):
    return (op in (ENC_FWD, DEC_BWD) and section == 0) or (
        op in (DEC_FWD, ENC_BWD) and section == sections - 1
    )


def local_result(op, section, sections):
    return (
        op == ENC_FWD
        or (op == DEC_FWD and section == 0)
        or (op == DEC_BWD and section == sections - 1)
    )


STATE = ("kept", "side", "normed", "scale", "acts", "cots")


def stage_kernel(work, aside, sections, breadth, factor, refs):
    pixels, channels = refs["kept"].shape[1:]
    section = lax.axis_index("section")
    jobs = [work.get(s, (0, 0)) for s in range(sections)]
    ops = {op for op, _ in jobs}
    op = chosen(section, [job[0] for job in jobs])
    slot = chosen(section, [job[1] for job in jobs])
    to_here = chosen(
        section, [int(local_result(job[0], s, sections)) for s, job in enumerate(jobs)]
    )
    kept, side, normed, scale = (refs[name] for name in ("kept", "side", "normed", "scale"))
    acts, cots, windows = (refs[name] for name in ("acts", "cots", "windows"))
    members, modulation = (refs[name] for name in ("members", "modulation"))
    group_size = channels // GROUPS
    fewer, more = 1.0 / (pixels * group_size), 1.0 / (pixels * 2 * group_size)

    def pick(is_dec):
        if aside:
            return 2, 1, F32(more)
        kind = jnp.where(is_dec, 1, 0)
        return kind, kind, jnp.where(is_dec, F32(more), F32(fewer))

    def load_input():
        leaving = refs["leaving"]
        cases = {}
        for s, (job_op, _) in enumerate(jobs):
            if job_op:
                local = local_input(job_op, s, sections)
                case = "noisy" if local and job_op == ENC_FWD else "kept" if local else "arriving"
                cases.setdefault(case, []).append(s)

        def fill(case):
            if case == "noisy":
                leaving[...] = refs["levels"][0, slot] * refs["clean"][slot].astype(F32) + refs[
                    "levels"
                ][1, slot] * refs["noise"][slot].astype(F32)
            elif case == "kept":
                leaving[...] = kept[slot]
            else:
                leaving[...] = refs["arriving"][...]

        for case, places in cases.items():
            here = functools.reduce(jnp.logical_or, [section == s for s in places])
            pl.when(here)(functools.partial(fill, case))
        return leaving[...]

    def forward():
        is_dec = op == DEC_FWD
        kind, which, inverse_count = pick(is_dec)
        x = kept[slot] if aside else load_input()
        total = jnp.sum(x, axis=0, keepdims=True)
        own_mean = total * (1.0 / pixels)
        own_dev = x - own_mean
        own_square = jnp.sum(own_dev * own_dev, axis=0, keepdims=True)
        (group_total,) = group_sums([total], members[which])
        mean = group_total * inverse_count
        apart = own_mean - mean
        (group_square,) = group_sums([own_square + pixels * (apart * apart)], members[which])
        inverse_std = lax.rsqrt(group_square * inverse_count + 1e-05)
        unit = (x - mean) * inverse_std
        value = unit * modulation[kind, slot]
        active = value / (1.0 + jnp.exp(-value))
        normed[kind, slot] = unit
        scale[kind, slot] = inverse_std
        acts[kind, slot] = active.astype(BF16)
        spread_columns(active, breadth, windows)
        if aside:
            side[slot] = convolve(windows, refs["dec_weight"], channels, pixels, breadth)
            return
        leaving = refs["leaving"]
        if ENC_FWD in ops:

            @pl.when(op == ENC_FWD)
            def _():
                leaving[...] += convolve(windows, refs["enc_weight"], 0, pixels, breadth)

        if DEC_FWD in ops:

            @pl.when(is_dec)
            def _():
                own = convolve(windows, refs["dec_weight"], 0, pixels, breadth)
                leaving[...] += own + side[slot]

                @pl.when(to_here == 1)
                def _():
                    leaving[...] = factor * (leaving[...] - refs["noise"][slot].astype(F32))

        keep_result()

    def keep_result():
        if any(local_result(job[0], s, sections) for s, job in enumerate(jobs)):

            @pl.when(to_here == 1)
            def _():
                kept[slot] = refs["leaving"][...]

    def backward():
        is_dec = op == DEC_BWD
        kind, which, inverse_count = pick(is_dec)
        if aside:
            spread_columns(cots[1, slot].astype(F32), breadth, windows)
        else:
            leaving = refs["leaving"]
            load_input()
            if ENC_BWD in ops:

                @pl.when(op == ENC_BWD)
                def _():
                    leaving[...] = leaving[...] + side[slot]

            g = leaving[...]
            cots[kind, slot] = g.astype(BF16)
            spread_columns(g, breadth, windows)
        down = convolve(windows, refs["flipped"].at[kind], 0, pixels, breadth)
        unit = normed[kind, slot]
        mod = modulation[kind, slot]
        value = unit * mod
        gate = 1.0 / (1.0 + jnp.exp(-value))
        slope = gate * (1.0 + value * (1.0 - gate))
        d_unit = down * slope * mod
        sums = group_sums(
            [
                jnp.sum(d_unit, axis=0, keepdims=True),
                jnp.sum(d_unit * unit, axis=0, keepdims=True),
            ],
            members[which],
        )
        shift, stretch = sums[0] * inverse_count, sums[1] * inverse_count
        result = scale[kind, slot] * (d_unit - shift - unit * stretch)
        if aside:
            side[slot] = result
        else:
            leaving[...] = leaving[...] + result
            keep_result()

    if aside:
        if ENC_FWD in ops:
            pl.when(op == ENC_FWD)(forward)
        if DEC_BWD in ops:
            pl.when(op == DEC_BWD)(backward)
    else:
        if ops & {ENC_FWD, DEC_FWD}:
            pl.when(jnp.logical_or(op == ENC_FWD, op == DEC_FWD))(forward)
        if ops & {DEC_BWD, ENC_BWD}:
            pl.when(op >= DEC_BWD)(backward)


def call_stage(work, aside, sections, breadth, factor, arriving, consts, state):
    ops = {op for op, _ in work.values()}
    _, pixels, channels = state["kept"].shape
    vmem = pl.BlockSpec(memory_space=pltpu.VMEM)
    forward = ENC_FWD in ops if aside else bool(ops & {ENC_FWD, DEC_FWD})
    backward = DEC_BWD in ops if aside else bool(ops & {DEC_BWD, ENC_BWD})
    given = {name: consts[name] for name in ("modulation", "members")}
    if ENC_FWD in ops and not aside:
        given["enc_weight"] = consts["enc_weight"]
    if DEC_FWD in ops or (aside and forward):
        given["dec_weight"] = consts["dec_weight"]
    if backward:
        given["flipped"] = consts["flipped"]
    starting = not aside and work.get(0, (0, 0))[0] == ENC_FWD
    if starting:
        given["levels"] = consts["levels"]
        given["clean"] = consts["clean"]
    if starting or (DEC_FWD in ops and not aside):
        given["noise"] = consts["noise"]
    if not aside and any(not local_input(op, s, sections) for s, (op, _) in work.items()):
        given["arriving"] = arriving
    present = [n for n in STATE if not isinstance(state[n], jax.ShapeDtypeStruct)]
    out_shape = {} if aside else {"leaving": jax.ShapeDtypeStruct((pixels, channels), F32)}
    for name in STATE:
        out_shape[name] = jax.ShapeDtypeStruct(state[name].shape, state[name].dtype)
    out_names = list(out_shape)

    def kernel(*refs):
        named = dict(zip(given, refs))
        named.update(zip(out_names, refs[len(given) + len(present) :]))
        named["windows"] = refs[-1]
        stage_kernel(work, aside, sections, breadth, factor, named)

    outs = pl.pallas_call(
        kernel,
        out_shape=list(out_shape.values()),
        in_specs=[vmem] * (len(given) + len(present)),
        out_specs=[vmem] * len(out_shape),
        scratch_shapes=[pltpu.VMEM((pixels + 2 * breadth, 3 * channels), BF16)],
        input_output_aliases={
            len(given) + i: out_names.index(name) for i, name in enumerate(present)
        },
        compiler_params=pltpu.CompilerParams(vmem_limit_bytes=STAGE_VMEM),
        cost_estimate=pl.CostEstimate(
            flops=2 * 9 * pixels * channels * channels,
            bytes_accessed=4 * pixels * channels,
            transcendentals=0,
        ),
    )(*given.values(), *[state[n] for n in present])
    named = dict(zip(out_names, outs))
    return named.pop("leaving", None), named


def flip_kernel(core, enc_weight, dec_weight, *refs):
    flipped = refs[-1]
    taps, channels, _ = enc_weight.shape

    @pl.when(lax.axis_index("dp") % 2 == core)
    def _():
        def one(tap, carry):
            for kind, tile in enumerate(
                (
                    enc_weight[tap],
                    dec_weight[tap, 0:channels, :],
                    dec_weight[tap, channels : 2 * channels, :],
                )
            ):
                flipped[kind, taps - 1 - tap] = tile.astype(F32).T.astype(BF16)
            return carry

        lax.fori_loop(0, taps, one, 0)


def flip(core, enc_weight, dec_weight, flipped):
    vmem = pl.BlockSpec(memory_space=pltpu.VMEM)
    return pl.pallas_call(
        functools.partial(flip_kernel, core),
        out_shape=jax.ShapeDtypeStruct((3,) + enc_weight.shape, BF16),
        in_specs=[vmem] * (2 if flipped is None else 3),
        out_specs=vmem,
        input_output_aliases={} if flipped is None else {2: 0},
        compiler_params=pltpu.CompilerParams(vmem_limit_bytes=STAGE_VMEM),
    )(enc_weight, dec_weight, *([] if flipped is None else [flipped]))


def weight_grad_kernel(breadth, kinds, which, span, chunks, resumed, acts, cots, *refs):
    before = refs[0:2] if resumed else None
    outs = refs[2:4] if resumed else refs[0:2]
    flipped, windows, ready, sems, loaded, load_sems = refs[4 if resumed else 2 :]
    _, _, pixels, channels = acts.shape
    core = lax.axis_index("dp") % 2
    halves = len(kinds)
    rows = halves * channels // chunks // 2

    def load(tap, slot):
        return [
            pltpu.make_async_copy(
                before[i].at[:, tap], loaded.at[slot, i], load_sems.at[slot, i]
            )
            for i in range(2)
        ]

    def store(tap, slot):
        return [
            pltpu.make_async_copy(ready.at[slot, i], outs[i].at[:, tap], sems.at[slot, i])
            for i in range(2)
        ]

    if resumed:
        for one in load(0, 0):
            one.start()
    for order, sample in enumerate(span):
        for half, kind in enumerate(kinds):
            flipped[
                half * channels : (half + 1) * channels, order * pixels : (order + 1) * pixels
            ] = acts[kind, sample].astype(F32).T.astype(BF16)
        spread_columns(cots[which, sample].astype(F32), breadth, windows.at[order])

    def one_tap(tap, carry):
        slot = lax.rem(tap, 2)
        row, col = tap // 3, lax.rem(tap, 3)
        start = pl.multiple_of((2 - row) * breadth, breadth)
        lane = pl.multiple_of((2 - col) * channels, 128)
        total = None
        for order in range(len(span)):
            part = jnp.dot(
                flipped[:, order * pixels : (order + 1) * pixels],
                windows[order, pl.ds(start, pixels), pl.ds(lane, channels)],
                preferred_element_type=F32,
            )
            total = part if total is None else total + part
        if resumed:
            for one in load(tap, slot):
                one.wait()

            @pl.when(tap < 8)
            def _():
                for one in load(tap + 1, 1 - slot):
                    one.start()

        @pl.when(tap >= 2)
        def _():
            for one in store(tap, slot):
                one.wait()

        pieces = total.reshape(chunks, 2, rows, channels)
        kept = jnp.where(core == 0, pieces[:, 0], pieces[:, 1])
        given = jnp.where(core == 0, pieces[:, 1], pieces[:, 0])
        if resumed:
            kept = kept + loaded[slot, 0]
            given = given + loaded[slot, 1]
        ready[slot, 0] = kept
        ready[slot, 1] = given
        for one in store(tap, slot):
            one.start()
        return carry

    lax.fori_loop(0, 9, one_tap, 0)
    for tap in (7, 8):
        for one in store(tap, tap % 2):
            one.wait()


def weight_grad(acts, cots, kinds, which, span, before, breadth):
    _, samples, pixels, channels = acts.shape
    halves = len(kinds)
    chunks = lax.axis_size("dp") // 2
    rows = halves * channels // chunks // 2
    vmem = pl.BlockSpec(memory_space=pltpu.VMEM)
    any_spec = pl.BlockSpec(memory_space=pl.ANY)
    shape = jax.ShapeDtypeStruct((chunks, 9, rows, channels), F32)
    resumed = before is not None
    return pl.pallas_call(
        functools.partial(
            weight_grad_kernel, breadth, kinds, which, tuple(span), chunks, resumed
        ),
        out_shape=[shape, shape],
        in_specs=[vmem, vmem] + ([any_spec] * 2 if resumed else []),
        out_specs=[any_spec, any_spec],
        scratch_shapes=[
            pltpu.VMEM((halves * channels, len(span) * pixels), BF16),
            pltpu.VMEM((len(span), pixels + 2 * breadth, 3 * channels), BF16),
            pltpu.VMEM((2, 2, chunks, rows, channels), F32),
            pltpu.SemaphoreType.DMA((2, 2)),
            pltpu.VMEM((2, 2, chunks, rows, channels) if resumed else (8, 128), F32),
            pltpu.SemaphoreType.DMA((2, 2)),
        ],
        compiler_params=pltpu.CompilerParams(vmem_limit_bytes=GRAD_VMEM),
        cost_estimate=pl.CostEstimate(
            flops=2 * 9 * len(span) * pixels * channels * channels * halves,
            bytes_accessed=9 * halves * channels * channels * 4,
            transcendentals=0,
        ),
    )(acts, cots, *(before if resumed else ()))


def member_matrices(channels):
    channel = np.arange(channels)
    size = channels // GROUPS
    return np.stack(
        [channel[:, None] // n == channel[None, :] // n for n in (size, 2 * size)]
    ).astype(ml_dtypes.bfloat16)


class LineSum:
    def __init__(self, kept, given):
        self.count = lax.axis_size("dp")
        self.chips = self.count // 2
        self.steps = self.chips - 1
        self.place = lax.axis_index("dp") // 2
        self.kept = kept
        self.swapped = lax.ppermute(
            given, "dp", [(d, d + 1 - 2 * (d % 2)) for d in range(self.count)]
        )
        self.arrived = None

    def own(self, index):
        index = jnp.clip(index, 0, self.chips - 1)
        return lax.dynamic_index_in_dim(self.kept, index, 0, False) + lax.dynamic_index_in_dim(
            self.swapped, index, 0, False
        )

    def prepare(self, step):
        up = self.own(self.chips - 1 - step + self.place)
        down = self.own(step - (self.chips - 1 - self.place))
        if step:
            up, down = up + self.arrived[0], down + self.arrived[1]
        return up, down

    def send(self, step, pair):
        last = self.chips - 1
        moves = [(z, c) for z in range(min(step + 1, last)) for c in range(2)]
        up = lax.ppermute(pair[0], "dp", [(2 * z + c, 2 * z + 2 + c) for z, c in moves])
        down = lax.ppermute(
            pair[1], "dp", [(2 * (last - z) + c, 2 * (last - z) - 2 + c) for z, c in moves]
        )
        self.arrived = lax.optimization_barrier((up, down))

    def result(self):
        total = self.own(self.place)
        if self.arrived is not None:
            total = total + self.arrived[0] + self.arrived[1]
        return total


def shards(clean, noise, stamps, enc_weight, dec_weight):
    sections = lax.axis_size("section")
    samples, height, breadth, channels = clean.shape
    pixels = height * breadth
    factor = 1.0 / math.sqrt(samples * lax.axis_size("dp") * pixels)
    ticks = make_schedule(sections, samples)

    levels = jnp.stack(noise_levels(stamps))
    wide = embed(stamps, 2 * channels)
    modulation = 1.0 + 0.5 * jnp.stack(
        [embed(stamps, channels), wide[:, :channels], wide[:, channels:]]
    )
    consts = {
        "modulation": modulation[:, :, None, :],
        "members": jnp.asarray(member_matrices(channels)),
        "enc_weight": enc_weight.reshape(9, channels, channels),
        "dec_weight": dec_weight.reshape(9, 2 * channels, channels),
        "levels": jnp.broadcast_to(levels[:, :, None, None], (2, samples, 1, channels)),
        "clean": clean.reshape(samples, pixels, channels),
        "noise": noise.reshape(samples, pixels, channels),
    }
    weights = (consts["enc_weight"], consts["dec_weight"])
    flipped = flip(1, *weights, None)
    consts["levels"], flipped = lax.optimization_barrier((consts["levels"], flipped))

    fresh = jax.ShapeDtypeStruct
    state = {
        "kept": fresh((samples, pixels, channels), F32),
        "side": fresh((samples, pixels, channels), F32),
        "normed": fresh((3, samples, pixels, channels), F32),
        "scale": fresh((3, samples, 1, channels), F32),
        "acts": fresh((3, samples, pixels, channels), BF16),
        "cots": fresh((2, samples, pixels, channels), BF16),
    }
    arriving = None
    dec_done = {
        sample: max(t for t, (work, _) in enumerate(ticks) if (DEC_BWD, sample) in work.values())
        for sample in range(samples)
    }
    early = list(range(samples - 1))
    last_dec = dec_done[samples - 1]
    dec_grad = dec_sum = None
    dec_step = 0
    for tick, (work, moves) in enumerate(ticks):
        ops = {op for op, _ in work.values()}
        leaving, state = call_stage(
            work, False, sections, breadth, factor, arriving, consts, state
        )
        if moves:
            arriving = lax.ppermute(leaving, "section", moves)
        if tick == 0:
            consts["flipped"] = flip(0, *weights, flipped)
        if ops & {ENC_FWD, DEC_BWD}:
            _, state = call_stage(work, True, sections, breadth, factor, None, consts, state)
        if early and tick == dec_done[samples - 2]:
            dec_grad = weight_grad(
                state["acts"], state["cots"], (1, 2), 1, early, None, breadth
            )
        if tick == last_dec:
            dec_grad = weight_grad(
                state["acts"], state["cots"], (1, 2), 1, [samples - 1], dec_grad, breadth
            )
            dec_sum = LineSum(*dec_grad)
        elif dec_sum is not None and (tick - last_dec) % 2 and dec_step < dec_sum.steps:
            pair = dec_sum.prepare(dec_step)
            state["scale"], pair = lax.optimization_barrier((state["scale"], pair))
            dec_sum.send(dec_step, pair)
            dec_step += 1
    enc_grad = weight_grad(
        state["acts"], state["cots"], (0,), 0, range(samples), None, breadth
    )
    enc_sum = LineSum(*enc_grad)
    enc_step = 0
    while enc_step < enc_sum.steps or dec_step < dec_sum.steps:
        pairs = {}
        if dec_step < dec_sum.steps:
            pairs["dec"] = dec_sum.prepare(dec_step)
        if enc_step < enc_sum.steps:
            pairs["enc"] = enc_sum.prepare(enc_step)
        pairs = lax.optimization_barrier(pairs)
        if "dec" in pairs:
            dec_sum.send(dec_step, pairs["dec"])
            dec_step += 1
        if "enc" in pairs:
            enc_sum.send(enc_step, pairs["enc"])
            enc_step += 1
    enc_share, dec_share = enc_sum.result(), dec_sum.result()
    return tuple(
        share.reshape((1, 3, 3) + share.shape[1:]) for share in (enc_share, dec_share)
    )


def solution(mesh):
    placed = (
        P("dp", None, None, None),
        P("dp", None, None, None),
        P("dp"),
        P("section", None, None, None, None),
        P("section", None, None, None, None),
    )
    return jax.shard_map(
        shards,
        mesh=mesh,
        in_specs=placed,
        out_specs=(P("section", None, None, "dp", None), P("section", None, None, "dp", None)),
        check_vma=False,
    )
```

```python
import functools
import math

import jax
import jax.numpy as jnp
import ml_dtypes
import numpy as np
from jax import lax
from jax.experimental import pallas as pl
from jax.experimental.pallas import tpu as pltpu
from jax.sharding import PartitionSpec as P

GROUPS = 32
F32 = jnp.float32
BF16 = jnp.bfloat16
ENC_FWD, DEC_FWD, DEC_BWD, ENC_BWD = 1, 2, 3, 4
STAGE_VMEM = 2 * 1024 * 1024
GRAD_VMEM = 8 * 1024 * 1024


def embed(stamps_in, channels):
    half_width = channels // 2
    frequency = jnp.exp(-math.log(10000.0) * jnp.arange(half_width, dtype=jnp.float32) / half_width)
    angles = stamps_in.astype(jnp.float32)[:, None] * frequency[None, :]
    return jnp.concatenate([jnp.sin(angles), jnp.cos(angles)], axis=1)


def noise_levels(stamps_in):
    phase = (stamps_in.astype(jnp.float32) / 1000.0 + 0.008) / 1.008 * (math.pi / 2.0)
    signal = jnp.cos(phase) ** 2
    return (jnp.sqrt(signal), jnp.sqrt(1.0 - signal))


def stage_of(position, sections):
    lap, step = divmod(position, sections)
    section = step if lap % 2 == 0 else sections - 1 - step
    return section, lap + 1


def make_schedule(sections, samples):
    stages = 4 * sections
    ticks = []
    for tick in range(stages + 2 * (samples - 1)):
        work, moves = {}, []
        for sample in range(samples):
            position = tick - 2 * sample
            if not 0 <= position < stages:
                continue
            section, op = stage_of(position, sections)
            assert section not in work
            work[section] = (op, sample)
            if position + 1 < stages:
                target, _ = stage_of(position + 1, sections)
                if target != section:
                    moves.append((section, target))
        ticks.append((work, moves))
    return ticks


def group_sums(vectors, members):
    channels = vectors[0].shape[1]
    row = lax.broadcasted_iota(jnp.int32, (16, channels), 0)
    stacked = jnp.zeros((16, channels), F32)
    for index, vector in enumerate(vectors):
        high = vector.astype(BF16).astype(F32)
        rest = vector - high
        middle = rest.astype(BF16).astype(F32)
        for part_index, part in enumerate((high, middle, rest - middle)):
            stacked = jnp.where(row == 3 * index + part_index, part, stacked)
    summed = jnp.dot(stacked.astype(BF16), members, preferred_element_type=F32)
    return [
        summed[3 * i : 3 * i + 1] + summed[3 * i + 1 : 3 * i + 2] + summed[3 * i + 2 : 3 * i + 3]
        for i in range(len(vectors))
    ]


def spread_columns(field, breadth, windows_ref):
    pixels, channels = field.shape
    column = lax.broadcasted_iota(jnp.int32, (pixels, channels), 0) & (breadth - 1)
    before = jnp.where(column == 0, 0.0, pltpu.roll(field, 1, 0))
    after = jnp.where(column == breadth - 1, 0.0, pltpu.roll(field, pixels - 1, 0))
    edge = jnp.zeros((breadth, channels), BF16)
    for index, shifted in enumerate((before, field, after)):
        lanes = slice(index * channels, (index + 1) * channels)
        windows_ref[0:breadth, lanes] = edge
        windows_ref[breadth : breadth + pixels, lanes] = shifted.astype(BF16)
        windows_ref[breadth + pixels : 2 * breadth + pixels, lanes] = edge


def convolve(windows_ref, weight_ref, first, pixels, breadth):
    outputs = weight_ref.shape[2]
    channels = windows_ref.shape[1] // 3
    total = None
    for row in range(3):
        part = jnp.dot(
            windows_ref[row * breadth : row * breadth + pixels, :],
            weight_ref[3 * row : 3 * row + 3, first : first + channels, :].reshape(
                3 * channels, outputs
            ),
            preferred_element_type=F32,
        )
        total = part if total is None else total + part
    return total


def chosen(index, values):
    result = jnp.int32(values[0])
    for position, value in enumerate(values):
        if value != values[0]:
            result = jnp.where(index == position, value, result)
    return result


def local_input(op, section, sections):
    return (op in (ENC_FWD, DEC_BWD) and section == 0) or (
        op in (DEC_FWD, ENC_BWD) and section == sections - 1
    )


def local_result(op, section, sections):
    return (
        op == ENC_FWD
        or (op == DEC_FWD and section == 0)
        or (op == DEC_BWD and section == sections - 1)
    )


STATE = ("kept", "side", "normed", "scale", "acts", "turned", "cots")


def stage_kernel(work, aside, core, sections, breadth, factor, refs):
    pixels, channels = refs["kept"].shape[1:]
    section = lax.axis_index("section")
    jobs = [work.get(s, (0, 0)) for s in range(sections)]
    ops = {op for op, _ in jobs}
    op = chosen(section, [job[0] for job in jobs])
    if core is not None:
        op = jnp.where(lax.axis_index("dp") % 2 == core, op, 0)
    slot = chosen(section, [job[1] for job in jobs])
    to_here = chosen(
        section, [int(local_result(job[0], s, sections)) for s, job in enumerate(jobs)]
    )
    kept, side, normed, scale = (refs[name] for name in ("kept", "side", "normed", "scale"))
    acts, turned, cots = (refs[name] for name in ("acts", "turned", "cots"))
    windows = refs["windows"]
    members, modulation = (refs[name] for name in ("members", "modulation"))
    group_size = channels // GROUPS
    fewer, more = 1.0 / (pixels * group_size), 1.0 / (pixels * 2 * group_size)

    def pick(is_dec):
        if aside:
            return 2, 1, F32(more)
        kind = jnp.where(is_dec, 1, 0)
        return kind, kind, jnp.where(is_dec, F32(more), F32(fewer))

    def load_input():
        leaving = refs["leaving"]
        cases = {}
        for s, (job_op, _) in enumerate(jobs):
            if job_op:
                local = local_input(job_op, s, sections)
                case = "noisy" if local and job_op == ENC_FWD else "kept" if local else "arriving"
                cases.setdefault(case, []).append(s)

        def fill(case):
            if case == "noisy":
                leaving[...] = refs["levels"][0, slot] * refs["clean"][slot].astype(F32) + refs[
                    "levels"
                ][1, slot] * refs["noise"][slot].astype(F32)
            elif case == "kept":
                leaving[...] = kept[slot]
            else:
                leaving[...] = refs["arriving"][...]

        for case, places in cases.items():
            here = functools.reduce(jnp.logical_or, [section == s for s in places])
            pl.when(here)(functools.partial(fill, case))
        return leaving[...]

    def forward():
        is_dec = op == DEC_FWD
        kind, which, inverse_count = pick(is_dec)
        x = kept[slot] if aside else load_input()
        total = jnp.sum(x, axis=0, keepdims=True)
        own_mean = total * (1.0 / pixels)
        own_dev = x - own_mean
        own_square = jnp.sum(own_dev * own_dev, axis=0, keepdims=True)
        (group_total,) = group_sums([total], members[which])
        mean = group_total * inverse_count
        apart = own_mean - mean
        (group_square,) = group_sums([own_square + pixels * (apart * apart)], members[which])
        inverse_std = lax.rsqrt(group_square * inverse_count + 1e-05)
        unit = (x - mean) * inverse_std
        value = unit * modulation[kind, slot]
        active = value / (1.0 + jnp.exp(-value))
        normed[kind, slot] = unit
        scale[kind, slot] = inverse_std
        spread_columns(active, breadth, windows)
        if aside:
            turned[0, slot] = acts[0, slot].astype(F32).T.astype(BF16)
            turned[2, slot] = active.T.astype(BF16)
            side[slot] = convolve(windows, refs["dec_weight"], channels, pixels, breadth)
            return
        acts[kind, slot] = active.astype(BF16)
        leaving = refs["leaving"]
        if ENC_FWD in ops:

            @pl.when(op == ENC_FWD)
            def _():
                leaving[...] += convolve(windows, refs["enc_weight"], 0, pixels, breadth)

        if DEC_FWD in ops:

            @pl.when(is_dec)
            def _():
                own = convolve(windows, refs["dec_weight"], 0, pixels, breadth)
                leaving[...] += own + side[slot]

                @pl.when(to_here == 1)
                def _():
                    leaving[...] = factor * (leaving[...] - refs["noise"][slot].astype(F32))

        keep_result()

    def keep_result():
        if any(local_result(job[0], s, sections) for s, job in enumerate(jobs)):

            @pl.when(to_here == 1)
            def _():
                kept[slot] = refs["leaving"][...]

    def backward():
        is_dec = op == DEC_BWD
        kind, which, inverse_count = pick(is_dec)
        if aside:
            given = cots.at[1, slot]
            turned[1, slot] = acts[1, slot].astype(F32).T.astype(BF16)
        else:
            given = cots.at[kind, slot]
            leaving = refs["leaving"]
            load_input()
            if ENC_BWD in ops:

                @pl.when(op == ENC_BWD)
                def _():
                    leaving[...] = leaving[...] + side[slot]

            spread_columns(leaving[...], breadth, given)
        down = convolve(given, refs["flipped"].at[kind], 0, pixels, breadth)
        unit = normed[kind, slot]
        mod = modulation[kind, slot]
        value = unit * mod
        gate = 1.0 / (1.0 + jnp.exp(-value))
        slope = gate * (1.0 + value * (1.0 - gate))
        d_unit = down * slope * mod
        sums = group_sums(
            [
                jnp.sum(d_unit, axis=0, keepdims=True),
                jnp.sum(d_unit * unit, axis=0, keepdims=True),
            ],
            members[which],
        )
        shift, stretch = sums[0] * inverse_count, sums[1] * inverse_count
        result = scale[kind, slot] * (d_unit - shift - unit * stretch)
        if aside:
            side[slot] = result
        else:
            leaving[...] = leaving[...] + result
            keep_result()

    if aside:
        if ENC_FWD in ops:
            pl.when(op == ENC_FWD)(forward)
        if DEC_BWD in ops:
            pl.when(op == DEC_BWD)(backward)
    else:
        if ops & {ENC_FWD, DEC_FWD}:
            pl.when(jnp.logical_or(op == ENC_FWD, op == DEC_FWD))(forward)
        if ops & {DEC_BWD, ENC_BWD}:
            pl.when(op >= DEC_BWD)(backward)


def call_stage(work, aside, core, sections, breadth, factor, arriving, consts, state):
    ops = {op for op, _ in work.values()}
    _, pixels, channels = state["kept"].shape
    vmem = pl.BlockSpec(memory_space=pltpu.VMEM)
    forward = ENC_FWD in ops if aside else bool(ops & {ENC_FWD, DEC_FWD})
    backward = DEC_BWD in ops if aside else bool(ops & {DEC_BWD, ENC_BWD})
    given = {name: consts[name] for name in ("modulation", "members")}
    if ENC_FWD in ops and not aside:
        given["enc_weight"] = consts["enc_weight"]
    if DEC_FWD in ops or (aside and forward):
        given["dec_weight"] = consts["dec_weight"]
    if backward:
        given["flipped"] = consts["flipped"]
    starting = not aside and work.get(0, (0, 0))[0] == ENC_FWD
    if starting:
        given["levels"] = consts["levels"]
        given["clean"] = consts["clean"]
    if starting or (DEC_FWD in ops and not aside):
        given["noise"] = consts["noise"]
    if not aside and any(not local_input(op, s, sections) for s, (op, _) in work.items()):
        given["arriving"] = arriving
    present = [n for n in STATE if not isinstance(state[n], jax.ShapeDtypeStruct)]
    out_shape = {} if aside else {"leaving": jax.ShapeDtypeStruct((pixels, channels), F32)}
    for name in STATE:
        out_shape[name] = jax.ShapeDtypeStruct(state[name].shape, state[name].dtype)
    out_names = list(out_shape)

    def kernel(*refs):
        named = dict(zip(given, refs))
        named.update(zip(out_names, refs[len(given) + len(present) :]))
        named["windows"] = refs[-1]
        stage_kernel(work, aside, core, sections, breadth, factor, named)

    outs = pl.pallas_call(
        kernel,
        out_shape=list(out_shape.values()),
        in_specs=[vmem] * (len(given) + len(present)),
        out_specs=[vmem] * len(out_shape),
        scratch_shapes=[pltpu.VMEM((pixels + 2 * breadth, 3 * channels), BF16)],
        input_output_aliases={
            len(given) + i: out_names.index(name) for i, name in enumerate(present)
        },
        compiler_params=pltpu.CompilerParams(vmem_limit_bytes=STAGE_VMEM),
        cost_estimate=pl.CostEstimate(flops=1000, bytes_accessed=1000, transcendentals=0),
    )(*given.values(), *[state[n] for n in present])
    named = dict(zip(out_names, outs))
    return named.pop("leaving", None), named


def flip_kernel(core, enc_weight, dec_weight, after, *refs):
    flipped = refs[-1]
    taps, channels, _ = enc_weight.shape

    @pl.when(lax.axis_index("dp") % 2 == core)
    def _():
        def one_tap(tap, carry):
            for kind, tile in enumerate(
                (
                    enc_weight[tap],
                    dec_weight[tap, 0:channels, :],
                    dec_weight[tap, channels : 2 * channels, :],
                )
            ):
                flipped[kind, taps - 1 - tap] = tile.astype(F32).T.astype(BF16)
            return carry

        lax.fori_loop(0, taps, one_tap, 0)


def flip(core, enc_weight, dec_weight, after, flipped):
    vmem = pl.BlockSpec(memory_space=pltpu.VMEM)
    return pl.pallas_call(
        functools.partial(flip_kernel, core),
        out_shape=jax.ShapeDtypeStruct((3,) + enc_weight.shape, BF16),
        in_specs=[vmem] * (3 if flipped is None else 4),
        out_specs=vmem,
        input_output_aliases={} if flipped is None else {3: 0},
        compiler_params=pltpu.CompilerParams(vmem_limit_bytes=STAGE_VMEM),
    )(enc_weight, dec_weight, after, *([] if flipped is None else [flipped]))


def weight_grad_kernel(breadth, kinds, which, group, chunks, turned, cots, *refs):
    outs, (ready, sems) = refs[0:2], refs[2:]
    _, samples, channels, pixels = turned.shape
    core = lax.axis_index("dp") % 2
    rows = len(kinds) * channels // chunks // 2
    places = [divmod(2 * chunk * rows, channels) for chunk in group]

    def store(tap, slot):
        return [
            pltpu.make_async_copy(ready.at[slot, i], outs[i].at[:, tap], sems.at[slot, i])
            for i in range(2)
        ]

    def one_tap(tap, carry):
        slot = lax.rem(tap, 2)
        row, col = tap // 3, lax.rem(tap, 3)
        start = pl.multiple_of((2 - row) * breadth, breadth)
        lane = pl.multiple_of((2 - col) * channels, 128)
        total = None
        for sample in range(samples):
            lines = [
                turned[kinds[half], sample, first : first + 2 * rows, :]
                for half, first in places
            ]
            part = jnp.dot(
                jnp.concatenate(lines, axis=0),
                cots[which, sample, pl.ds(start, pixels), pl.ds(lane, channels)],
                preferred_element_type=F32,
            )
            total = part if total is None else total + part

        @pl.when(tap >= 2)
        def _():
            for one in store(tap, slot):
                one.wait()

        pieces = total.reshape(len(group), 2, rows, channels)
        ready[slot, 0] = jnp.where(core == 0, pieces[:, 0], pieces[:, 1])
        ready[slot, 1] = jnp.where(core == 0, pieces[:, 1], pieces[:, 0])
        for one in store(tap, slot):
            one.start()
        return carry

    lax.fori_loop(0, 9, one_tap, 0)
    for tap in (7, 8):
        for one in store(tap, tap % 2):
            one.wait()


def weight_grad(turned, cots, kinds, which, group, breadth):
    _, _, channels, _ = turned.shape
    chunks = lax.axis_size("dp") // 2
    rows = len(kinds) * channels // chunks // 2
    vmem = pl.BlockSpec(memory_space=pltpu.VMEM)
    hbm = pl.BlockSpec(memory_space=pltpu.HBM)
    shape = jax.ShapeDtypeStruct((len(group), 9, rows, channels), F32)
    return pl.pallas_call(
        functools.partial(weight_grad_kernel, breadth, kinds, which, tuple(group), chunks),
        out_shape=[shape, shape],
        in_specs=[vmem, vmem],
        out_specs=[hbm, hbm],
        scratch_shapes=[
            pltpu.VMEM((2, 2, len(group), rows, channels), F32),
            pltpu.SemaphoreType.DMA((2, 2)),
        ],
        compiler_params=pltpu.CompilerParams(vmem_limit_bytes=GRAD_VMEM),
        cost_estimate=pl.CostEstimate(flops=1000, bytes_accessed=1000, transcendentals=0),
    )(turned, cots)


def member_matrices(channels):
    channel = np.arange(channels)
    size = channels // GROUPS
    return np.stack(
        [channel[:, None] // n == channel[None, :] // n for n in (size, 2 * size)]
    ).astype(ml_dtypes.bfloat16)


class LineSum:
    def __init__(self, make):
        self.count = lax.axis_size("dp")
        self.chips = self.count // 2
        self.steps = self.chips - 1
        self.place = lax.axis_index("dp") // 2
        self.arrived = None
        self.ends = self.swap(*make([0, self.chips - 1]))
        middle = list(range(1, self.chips - 1))
        self.middle = self.swap(*make(middle)) if middle else None

    def swap(self, kept, given):
        moves = [(d, d + 1 - 2 * (d % 2)) for d in range(self.count)]
        return kept, lax.ppermute(given, "dp", moves)

    def end(self, index):
        kept, swapped = self.ends
        return kept[index] + swapped[index]

    def between(self, chunk):
        index = jnp.clip(chunk - 1, 0, self.chips - 3)
        return sum(lax.dynamic_index_in_dim(part, index, 0, False) for part in self.middle)

    def prepare(self, step):
        up, down = self.end(1), self.end(0)
        if step:
            back = self.chips - 1 - self.place
            up = jnp.where(self.place == step, up, self.between(back - step + 2 * self.place))
            down = jnp.where(back == step, down, self.between(step - back))
            up, down = up + self.arrived[0], down + self.arrived[1]
        return up, down

    def send(self, step, pair):
        last = self.chips - 1
        moves = [(z, c) for z in range(min(step + 1, last)) for c in range(2)]
        up = lax.ppermute(pair[0], "dp", [(2 * z + c, 2 * z + 2 + c) for z, c in moves])
        down = lax.ppermute(
            pair[1], "dp", [(2 * (last - z) + c, 2 * (last - z) - 2 + c) for z, c in moves]
        )
        self.arrived = lax.optimization_barrier((up, down))

    def result(self):
        total = jnp.where(self.place == 0, self.end(0), self.end(1))
        if self.middle is not None:
            outer = jnp.logical_or(self.place == 0, self.place == self.chips - 1)
            total = jnp.where(outer, total, self.between(self.place))
        return total + self.arrived[0] + self.arrived[1]


def shards(clean, noise, stamps, enc_weight, dec_weight):
    sections = lax.axis_size("section")
    samples, height, breadth, channels = clean.shape
    pixels = height * breadth
    factor = 1.0 / math.sqrt(samples * lax.axis_size("dp") * pixels)
    ticks = make_schedule(sections, samples)

    levels = jnp.stack(noise_levels(stamps))
    wide = embed(stamps, 2 * channels)
    modulation = 1.0 + 0.5 * jnp.stack(
        [embed(stamps, channels), wide[:, :channels], wide[:, channels:]]
    )
    consts = {
        "modulation": modulation[:, :, None, :],
        "members": jnp.asarray(member_matrices(channels)),
        "enc_weight": enc_weight.reshape(9, channels, channels),
        "dec_weight": dec_weight.reshape(9, 2 * channels, channels),
        "levels": jnp.broadcast_to(levels[:, :, None, None], (2, samples, 1, channels)),
        "clean": clean.reshape(samples, pixels, channels),
        "noise": noise.reshape(samples, pixels, channels),
    }
    weights = (consts["enc_weight"], consts["dec_weight"])
    fresh = jax.ShapeDtypeStruct
    state = {
        "kept": fresh((samples, pixels, channels), F32),
        "side": fresh((samples, pixels, channels), F32),
        "normed": fresh((3, samples, pixels, channels), F32),
        "scale": fresh((3, samples, 1, channels), F32),
        "acts": fresh((2, samples, pixels, channels), BF16),
        "turned": fresh((3, samples, channels, pixels), BF16),
        "cots": fresh((2, samples, pixels + 2 * breadth, 3 * channels), BF16),
    }
    arriving = None
    last_dec = max(
        tick for tick, (work, _) in enumerate(ticks) if any(w[0] == DEC_BWD for w in work.values())
    )
    dec_sum = None
    dec_step = 0

    def gradient(kinds, which):
        return LineSum(
            lambda group: weight_grad(
                state["turned"], state["cots"], kinds, which, group, breadth
            )
        )

    def dec_advance(name):
        pair = dec_sum.prepare(dec_step)
        state[name], pair = lax.optimization_barrier((state[name], pair))
        dec_sum.send(dec_step, pair)

    for tick, (work, moves) in enumerate(ticks):
        ops = {op for op, _ in work.values()}
        leaving, state = call_stage(
            work, False, None, sections, breadth, factor, arriving, consts, state
        )
        later = None
        if tick == 0:
            _, state = call_stage(work, True, 1, sections, breadth, factor, None, consts, state)
            flipped = flip(1, *weights, state["scale"], None)
            leaving, flipped, state["scale"] = lax.optimization_barrier(
                (leaving, flipped, state["scale"])
            )
            consts["flipped"] = flip(0, *weights, state["scale"], flipped)
            later = 0
        if moves:
            arriving = lax.ppermute(leaving, "section", moves)
        if ops & {ENC_FWD, DEC_BWD}:
            _, state = call_stage(
                work, True, later, sections, breadth, factor, None, consts, state
            )
        if tick == last_dec:
            dec_sum = gradient((1, 2), 1)
        if tick >= last_dec and (tick - last_dec) % 3 == 0 and dec_step < dec_sum.steps:
            dec_advance("scale")
            dec_step += 1
    enc_sum = gradient((0,), 0)
    enc_step = 0
    while enc_step < enc_sum.steps or dec_step < dec_sum.steps:
        pairs = {}
        if dec_step < dec_sum.steps:
            pairs["dec"] = dec_sum.prepare(dec_step)
        if enc_step < enc_sum.steps:
            pairs["enc"] = enc_sum.prepare(enc_step)
        pairs = lax.optimization_barrier(pairs)
        if "dec" in pairs:
            dec_sum.send(dec_step, pairs["dec"])
            dec_step += 1
        if "enc" in pairs:
            enc_sum.send(enc_step, pairs["enc"])
            enc_step += 1
    enc_share, dec_share = enc_sum.result(), dec_sum.result()
    return tuple(
        share.reshape((1, 3, 3) + share.shape[1:]) for share in (enc_share, dec_share)
    )


def solution(mesh):
    placed = (
        P("dp", None, None, None),
        P("dp", None, None, None),
        P("dp"),
        P("section", None, None, None, None),
        P("section", None, None, None, None),
    )
    return jax.shard_map(
        shards,
        mesh=mesh,
        in_specs=placed,
        out_specs=(P("section", None, None, "dp", None), P("section", None, None, "dp", None)),
        check_vma=False,
    )
```

```python
import functools
import math

import jax
import jax.numpy as jnp
import ml_dtypes
import numpy as np
from jax import lax
from jax.experimental import pallas as pl
from jax.experimental.pallas import tpu as pltpu
from jax.sharding import PartitionSpec as P

GROUPS = 32
F32 = jnp.float32
BF16 = jnp.bfloat16
ENC_FWD, DEC_FWD, DEC_BWD, ENC_BWD = 1, 2, 3, 4
STAGE_VMEM = 2 * 1024 * 1024
GRAD_VMEM = 8 * 1024 * 1024


def embed(stamps_in, channels):
    half_width = channels // 2
    frequency = jnp.exp(-math.log(10000.0) * jnp.arange(half_width, dtype=jnp.float32) / half_width)
    angles = stamps_in.astype(jnp.float32)[:, None] * frequency[None, :]
    return jnp.concatenate([jnp.sin(angles), jnp.cos(angles)], axis=1)


def noise_levels(stamps_in):
    phase = (stamps_in.astype(jnp.float32) / 1000.0 + 0.008) / 1.008 * (math.pi / 2.0)
    signal = jnp.cos(phase) ** 2
    return (jnp.sqrt(signal), jnp.sqrt(1.0 - signal))


def stage_of(position, sections):
    lap, step = divmod(position, sections)
    section = step if lap % 2 == 0 else sections - 1 - step
    return section, lap + 1


def make_schedule(sections, samples):
    stages = 4 * sections
    ticks = []
    for tick in range(stages + 2 * (samples - 1)):
        work, moves = {}, []
        for sample in range(samples):
            position = tick - 2 * sample
            if not 0 <= position < stages:
                continue
            section, op = stage_of(position, sections)
            assert section not in work
            work[section] = (op, sample)
            if position + 1 < stages:
                target, _ = stage_of(position + 1, sections)
                if target != section:
                    moves.append((section, target))
        ticks.append((work, moves))
    return ticks


def group_sums(vectors, members):
    channels = vectors[0].shape[1]
    row = lax.broadcasted_iota(jnp.int32, (16, channels), 0)
    stacked = jnp.zeros((16, channels), F32)
    for index, vector in enumerate(vectors):
        high = vector.astype(BF16).astype(F32)
        rest = vector - high
        middle = rest.astype(BF16).astype(F32)
        for part_index, part in enumerate((high, middle, rest - middle)):
            stacked = jnp.where(row == 3 * index + part_index, part, stacked)
    summed = jnp.dot(stacked.astype(BF16), members, preferred_element_type=F32)
    return [
        summed[3 * i : 3 * i + 1] + summed[3 * i + 1 : 3 * i + 2] + summed[3 * i + 2 : 3 * i + 3]
        for i in range(len(vectors))
    ]


def spread_columns(field, breadth, windows_ref):
    pixels, channels = field.shape
    column = lax.broadcasted_iota(jnp.int32, (pixels, channels), 0) & (breadth - 1)
    before = jnp.where(column == 0, 0.0, pltpu.roll(field, 1, 0))
    after = jnp.where(column == breadth - 1, 0.0, pltpu.roll(field, pixels - 1, 0))
    edge = jnp.zeros((breadth, channels), BF16)
    for index, shifted in enumerate((before, field, after)):
        lanes = slice(index * channels, (index + 1) * channels)
        windows_ref[0:breadth, lanes] = edge
        windows_ref[breadth : breadth + pixels, lanes] = shifted.astype(BF16)
        windows_ref[breadth + pixels : 2 * breadth + pixels, lanes] = edge


def convolve(windows_ref, weight_ref, first, pixels, breadth):
    outputs = weight_ref.shape[2]
    channels = windows_ref.shape[1] // 3
    total = None
    for row in range(3):
        part = jnp.dot(
            windows_ref[row * breadth : row * breadth + pixels, :],
            weight_ref[3 * row : 3 * row + 3, first : first + channels, :].reshape(
                3 * channels, outputs
            ),
            preferred_element_type=F32,
        )
        total = part if total is None else total + part
    return total


def chosen(index, values):
    result = jnp.int32(values[0])
    for position, value in enumerate(values):
        if value != values[0]:
            result = jnp.where(index == position, value, result)
    return result


def local_input(op, section, sections):
    return (op in (ENC_FWD, DEC_BWD) and section == 0) or (
        op in (DEC_FWD, ENC_BWD) and section == sections - 1
    )


def local_result(op, section, sections):
    return (
        op == ENC_FWD
        or (op == DEC_FWD and section == 0)
        or (op == DEC_BWD and section == sections - 1)
    )


KINDS = ("enc", "dec", "skip")


def touched(work, aside):
    ops = {op for op, _ in work.values()}
    names = ["kept", "side"]
    if aside:
        if ENC_FWD in ops:
            names += ["normed_skip", "scale_skip", "acts_enc", "turned_enc", "turned_skip"]
        if DEC_BWD in ops:
            names += ["normed_skip", "scale_skip", "cots_dec", "acts_dec", "turned_dec"]
    else:
        for op, kind in ((ENC_FWD, "enc"), (DEC_FWD, "dec")):
            if op in ops:
                names += ["normed_" + kind, "scale_" + kind, "acts_" + kind]
        for op, kind in ((ENC_BWD, "enc"), (DEC_BWD, "dec")):
            if op in ops:
                names += ["normed_" + kind, "scale_" + kind, "cots_" + kind]
    return list(dict.fromkeys(names))


def stage_kernel(work, aside, core, sections, breadth, factor, refs):
    pixels, channels = refs["kept"].shape[1:]
    section = lax.axis_index("section")
    jobs = [work.get(s, (0, 0)) for s in range(sections)]
    ops = {op for op, _ in jobs}
    op = chosen(section, [job[0] for job in jobs])
    if core is not None:
        op = jnp.where(lax.axis_index("dp") % 2 == core, op, 0)
    slot = chosen(section, [job[1] for job in jobs])
    to_here = chosen(
        section, [int(local_result(job[0], s, sections)) for s, job in enumerate(jobs)]
    )
    kept, side = refs["kept"], refs["side"]
    group_size = channels // GROUPS

    def per_kind(kind):
        which = 0 if kind == "enc" else 1
        inverse_count = 1.0 / (pixels * group_size * (1 + which))
        modulation = refs["modulation"][KINDS.index(kind), slot]
        return refs["members"].at[which], inverse_count, modulation

    def load_input():
        leaving = refs["leaving"]
        cases = {}
        for s, (job_op, _) in enumerate(jobs):
            if job_op:
                local = local_input(job_op, s, sections)
                case = "noisy" if local and job_op == ENC_FWD else "kept" if local else "arriving"
                cases.setdefault(case, []).append(s)

        def fill(case):
            if case == "noisy":
                leaving[...] = refs["levels"][0, slot] * refs["clean"][slot].astype(F32) + refs[
                    "levels"
                ][1, slot] * refs["noise"][slot].astype(F32)
            elif case == "kept":
                leaving[...] = kept[slot]
            else:
                leaving[...] = refs["arriving"][...]

        for case, places in cases.items():
            here = functools.reduce(jnp.logical_or, [section == s for s in places])
            pl.when(here)(functools.partial(fill, case))
        return leaving[...]

    def forward(kind):
        members, inverse_count, modulation = per_kind(kind)
        windows = refs["windows"]
        x = kept[slot] if aside else load_input()
        total = jnp.sum(x, axis=0, keepdims=True)
        own_mean = total * (1.0 / pixels)
        own_dev = x - own_mean
        own_square = jnp.sum(own_dev * own_dev, axis=0, keepdims=True)
        (group_total,) = group_sums([total], members[...])
        mean = group_total * inverse_count
        apart = own_mean - mean
        (group_square,) = group_sums([own_square + pixels * (apart * apart)], members[...])
        inverse_std = lax.rsqrt(group_square * inverse_count + 1e-05)
        unit = (x - mean) * inverse_std
        value = unit * modulation
        active = value / (1.0 + jnp.exp(-value))
        refs["normed_" + kind][slot] = unit
        refs["scale_" + kind][slot] = inverse_std
        spread_columns(active, breadth, windows)
        if aside:
            side[slot] = convolve(windows, refs["dec_weight"], channels, pixels, breadth)
            refs["turned_enc"][slot] = refs["acts_enc"][slot].astype(F32).T.astype(BF16)
            refs["turned_skip"][slot] = active.T.astype(BF16)
            return
        refs["acts_" + kind][slot] = active.astype(BF16)
        leaving = refs["leaving"]
        if kind == "enc":
            leaving[...] += convolve(windows, refs["enc_weight"], 0, pixels, breadth)
        else:
            own = convolve(windows, refs["dec_weight"], 0, pixels, breadth)
            leaving[...] += own + side[slot]

            @pl.when(to_here == 1)
            def _():
                leaving[...] = factor * (leaving[...] - refs["noise"][slot].astype(F32))

        keep_result()

    def keep_result():
        if any(local_result(job[0], s, sections) for s, job in enumerate(jobs)):

            @pl.when(to_here == 1)
            def _():
                kept[slot] = refs["leaving"][...]

    def backward(kind):
        members, inverse_count, modulation = per_kind(kind)
        if aside:
            given = refs["cots_dec"].at[slot]
            refs["turned_dec"][slot] = refs["acts_dec"][slot].astype(F32).T.astype(BF16)
        else:
            given = refs["cots_" + kind].at[slot]
            leaving = refs["leaving"]
            load_input()
            if kind == "enc":
                leaving[...] = leaving[...] + side[slot]
            spread_columns(leaving[...], breadth, given)
        down = convolve(given, refs["flipped_" + kind], 0, pixels, breadth)
        unit = refs["normed_" + kind][slot]
        value = unit * modulation
        gate = 1.0 / (1.0 + jnp.exp(-value))
        slope = gate * (1.0 + value * (1.0 - gate))
        d_unit = down * slope * modulation
        sums = group_sums(
            [
                jnp.sum(d_unit, axis=0, keepdims=True),
                jnp.sum(d_unit * unit, axis=0, keepdims=True),
            ],
            members[...],
        )
        shift, stretch = sums[0] * inverse_count, sums[1] * inverse_count
        result = refs["scale_" + kind][slot] * (d_unit - shift - unit * stretch)
        if aside:
            side[slot] = result
        else:
            leaving[...] = leaving[...] + result
            keep_result()

    if aside:
        parts = ((ENC_FWD, forward, "skip"), (DEC_BWD, backward, "skip"))
    else:
        parts = (
            (ENC_FWD, forward, "enc"),
            (DEC_FWD, forward, "dec"),
            (DEC_BWD, backward, "dec"),
            (ENC_BWD, backward, "enc"),
        )
    for part_op, part, kind in parts:
        if part_op in ops:
            pl.when(op == part_op)(functools.partial(part, kind))


def call_stage(work, aside, core, sections, breadth, factor, arriving, consts, state):
    ops = {op for op, _ in work.values()}
    _, pixels, channels = state["kept"].shape
    vmem = pl.BlockSpec(memory_space=pltpu.VMEM)
    names = ["modulation", "members"]
    if ENC_FWD in ops and not aside:
        names.append("enc_weight")
    if (DEC_FWD in ops and not aside) or (ENC_FWD in ops and aside):
        names.append("dec_weight")
    if DEC_BWD in ops:
        names.append("flipped_skip" if aside else "flipped_dec")
    if ENC_BWD in ops and not aside:
        names.append("flipped_enc")
    starting = not aside and work.get(0, (0, 0))[0] == ENC_FWD
    if starting:
        names += ["levels", "clean"]
    if starting or (DEC_FWD in ops and not aside):
        names.append("noise")
    given = {name: consts[name] for name in names}
    if not aside and any(not local_input(op, s, sections) for s, (op, _) in work.items()):
        given["arriving"] = arriving
    used = touched(work, aside)
    present = [n for n in used if not isinstance(state[n], jax.ShapeDtypeStruct)]
    out_shape = {} if aside else {"leaving": jax.ShapeDtypeStruct((pixels, channels), F32)}
    for name in used:
        out_shape[name] = jax.ShapeDtypeStruct(state[name].shape, state[name].dtype)
    out_names = list(out_shape)

    def kernel(*refs):
        named = dict(zip(given, refs))
        named.update(zip(out_names, refs[len(given) + len(present) :]))
        named["windows"] = refs[-1]
        stage_kernel(work, aside, core, sections, breadth, factor, named)

    outs = pl.pallas_call(
        kernel,
        out_shape=list(out_shape.values()),
        in_specs=[vmem] * (len(given) + len(present)),
        out_specs=[vmem] * len(out_shape),
        scratch_shapes=[pltpu.VMEM((pixels + 2 * breadth, 3 * channels), BF16)],
        input_output_aliases={
            len(given) + i: out_names.index(name) for i, name in enumerate(present)
        },
        compiler_params=pltpu.CompilerParams(vmem_limit_bytes=STAGE_VMEM),
        cost_estimate=pl.CostEstimate(flops=1000, bytes_accessed=1000, transcendentals=0),
    )(*given.values(), *[state[n] for n in present])
    named = dict(zip(out_names, outs))
    leaving = named.pop("leaving", None)
    return leaving, {**state, **named}


def flip_kernel(core, enc_weight, dec_weight, after, *refs):
    taps, channels, _ = enc_weight.shape

    @pl.when(lax.axis_index("dp") % 2 == core)
    def _():
        def one_tap(tap, carry):
            tiles = (
                enc_weight[tap],
                dec_weight[tap, 0:channels, :],
                dec_weight[tap, channels : 2 * channels, :],
            )
            for tile, out in zip(tiles, refs[-3:]):
                out[taps - 1 - tap] = tile.astype(F32).T.astype(BF16)
            return carry

        lax.fori_loop(0, taps, one_tap, 0)


def flip(core, enc_weight, dec_weight, after, flipped):
    vmem = pl.BlockSpec(memory_space=pltpu.VMEM)
    return pl.pallas_call(
        functools.partial(flip_kernel, core),
        out_shape=[jax.ShapeDtypeStruct(enc_weight.shape, BF16)] * 3,
        in_specs=[vmem] * (3 + len(flipped)),
        out_specs=[vmem] * 3,
        input_output_aliases={3 + i: i for i in range(len(flipped))},
        compiler_params=pltpu.CompilerParams(vmem_limit_bytes=STAGE_VMEM),
    )(enc_weight, dec_weight, after, *flipped)


def weight_grad_kernel(breadth, halves, group, chunks, *refs):
    turned, cots, outs, (ready, sems) = refs[:halves], refs[halves], refs[-4:-2], refs[-2:]
    samples, channels, pixels = turned[0].shape
    core = lax.axis_index("dp") % 2
    rows = halves * channels // chunks // 2
    places = [divmod(2 * chunk * rows, channels) for chunk in group]

    def store(tap, slot):
        return [
            pltpu.make_async_copy(ready.at[slot, i], outs[i].at[:, tap], sems.at[slot, i])
            for i in range(2)
        ]

    def one_tap(tap, carry):
        slot = lax.rem(tap, 2)
        row, col = tap // 3, lax.rem(tap, 3)
        start = pl.multiple_of((2 - row) * breadth, breadth)
        lane = pl.multiple_of((2 - col) * channels, 128)
        total = None
        for sample in range(samples):
            lines = [
                turned[half][sample, first : first + 2 * rows, :]
                for half, first in places
            ]
            part = jnp.dot(
                jnp.concatenate(lines, axis=0),
                cots[sample, pl.ds(start, pixels), pl.ds(lane, channels)],
                preferred_element_type=F32,
            )
            total = part if total is None else total + part

        @pl.when(tap >= 2)
        def _():
            for one in store(tap, slot):
                one.wait()

        pieces = total.reshape(len(group), 2, rows, channels)
        ready[slot, 0] = jnp.where(core == 0, pieces[:, 0], pieces[:, 1])
        ready[slot, 1] = jnp.where(core == 0, pieces[:, 1], pieces[:, 0])
        for one in store(tap, slot):
            one.start()
        return carry

    lax.fori_loop(0, 9, one_tap, 0)
    for tap in (7, 8):
        for one in store(tap, tap % 2):
            one.wait()


def weight_grad(turned, cots, group, breadth):
    _, channels, _ = turned[0].shape
    chunks = lax.axis_size("dp") // 2
    rows = len(turned) * channels // chunks // 2
    vmem = pl.BlockSpec(memory_space=pltpu.VMEM)
    hbm = pl.BlockSpec(memory_space=pltpu.HBM)
    shape = jax.ShapeDtypeStruct((len(group), 9, rows, channels), F32)
    return pl.pallas_call(
        functools.partial(weight_grad_kernel, breadth, len(turned), tuple(group), chunks),
        out_shape=[shape, shape],
        in_specs=[vmem] * (len(turned) + 1),
        out_specs=[hbm, hbm],
        scratch_shapes=[
            pltpu.VMEM((2, 2, len(group), rows, channels), F32),
            pltpu.SemaphoreType.DMA((2, 2)),
        ],
        compiler_params=pltpu.CompilerParams(vmem_limit_bytes=GRAD_VMEM),
        cost_estimate=pl.CostEstimate(flops=1000, bytes_accessed=1000, transcendentals=0),
    )(*turned, cots)


def member_matrices(channels):
    channel = np.arange(channels)
    size = channels // GROUPS
    return np.stack(
        [channel[:, None] // n == channel[None, :] // n for n in (size, 2 * size)]
    ).astype(ml_dtypes.bfloat16)


class LineSum:
    def __init__(self, make):
        self.count = lax.axis_size("dp")
        self.chips = self.count // 2
        self.steps = self.chips - 1
        self.place = lax.axis_index("dp") // 2
        self.arrived = None
        self.ready = {}
        self.ends = self.swap(*make([0, self.chips - 1]))
        middle = list(range(1, self.chips - 1))
        self.middle = self.swap(*make(middle)) if middle else None

    def swap(self, kept, given):
        moves = [(d, d + 1 - 2 * (d % 2)) for d in range(self.count)]
        return kept, lax.ppermute(given, "dp", moves)

    def end(self, index):
        kept, swapped = self.ends
        return kept[index] + swapped[index]

    def between(self, chunk):
        index = jnp.clip(chunk - 1, 0, self.chips - 3)
        return sum(lax.dynamic_index_in_dim(part, index, 0, False) for part in self.middle)

    def own_pair(self, step):
        up, down = self.end(1), self.end(0)
        if step:
            back = self.chips - 1 - self.place
            up = jnp.where(self.place == step, up, self.between(back - step + 2 * self.place))
            down = jnp.where(back == step, down, self.between(step - back))
        return up, down

    def prepare(self, step):
        up, down = self.ready.pop(step) if step in self.ready else self.own_pair(step)
        if step:
            up, down = up + self.arrived[0], down + self.arrived[1]
        return up, down

    def send(self, step, pair):
        last = self.chips - 1
        moves = [(z, c) for z in range(min(step + 1, last)) for c in range(2)]
        up = lax.ppermute(pair[0], "dp", [(2 * z + c, 2 * z + 2 + c) for z, c in moves])
        down = lax.ppermute(
            pair[1], "dp", [(2 * (last - z) + c, 2 * (last - z) - 2 + c) for z, c in moves]
        )
        self.arrived = lax.optimization_barrier((up, down))

    def result(self):
        total = jnp.where(self.place == 0, self.end(0), self.end(1))
        if self.middle is not None:
            outer = jnp.logical_or(self.place == 0, self.place == self.chips - 1)
            total = jnp.where(outer, total, self.between(self.place))
        return total + self.arrived[0] + self.arrived[1]


def shards(clean, noise, stamps, enc_weight, dec_weight):
    sections = lax.axis_size("section")
    samples, height, breadth, channels = clean.shape
    pixels = height * breadth
    factor = 1.0 / math.sqrt(samples * lax.axis_size("dp") * pixels)
    ticks = make_schedule(sections, samples)

    levels = jnp.stack(noise_levels(stamps))
    wide = embed(stamps, 2 * channels)
    modulation = 1.0 + 0.5 * jnp.stack(
        [embed(stamps, channels), wide[:, :channels], wide[:, channels:]]
    )
    consts = {
        "modulation": modulation[:, :, None, :],
        "members": jnp.asarray(member_matrices(channels)),
        "enc_weight": enc_weight.reshape(9, channels, channels),
        "dec_weight": dec_weight.reshape(9, 2 * channels, channels),
        "levels": jnp.broadcast_to(levels[:, :, None, None], (2, samples, 1, channels)),
        "clean": clean.reshape(samples, pixels, channels),
        "noise": noise.reshape(samples, pixels, channels),
    }
    weights = (consts["enc_weight"], consts["dec_weight"])
    fresh = jax.ShapeDtypeStruct
    field = (samples, pixels, channels)
    state = {"kept": fresh(field, F32), "side": fresh(field, F32)}
    for kind in KINDS:
        state["normed_" + kind] = fresh(field, F32)
        state["scale_" + kind] = fresh((samples, 1, channels), F32)
        state["turned_" + kind] = fresh((samples, channels, pixels), BF16)
        if kind != "skip":
            state["acts_" + kind] = fresh(field, BF16)
            state["cots_" + kind] = fresh(
                (samples, pixels + 2 * breadth, 3 * channels), BF16
            )
    arriving = None
    last_dec = max(
        tick for tick, (work, _) in enumerate(ticks) if any(w[0] == DEC_BWD for w in work.values())
    )
    flip_tick = min(
        tick for tick, (work, _) in enumerate(ticks) if any(w[0] == DEC_BWD for w in work.values())
    ) - 2
    dec_sum = None
    dec_step = 0

    def gradient(kinds, cots):
        turned = [state["turned_" + kind] for kind in kinds]
        return LineSum(lambda group: weight_grad(turned, state[cots], group, breadth))

    def ahead_of(name, value):
        state[name], value = lax.optimization_barrier((state[name], value))
        return value

    for tick, (work, moves) in enumerate(ticks):
        ops = {op for op, _ in work.values()}
        leaving, state = call_stage(
            work, False, None, sections, breadth, factor, arriving, consts, state
        )
        later = None
        if tick == 0:
            _, state = call_stage(work, True, 1, sections, breadth, factor, None, consts, state)
            flipped = list(flip(1, *weights, state["scale_skip"], []))
            leaving, flipped[0] = lax.optimization_barrier((leaving, flipped[0]))
            later = 0
        if tick == flip_tick:
            flipped = flip(0, *weights, state["scale_skip"], flipped)
            consts.update(zip(["flipped_" + kind for kind in KINDS], flipped))
        if moves:
            arriving = lax.ppermute(leaving, "section", moves)
        if ops & {ENC_FWD, DEC_BWD}:
            _, state = call_stage(
                work, True, later, sections, breadth, factor, None, consts, state
            )
        if tick == last_dec:
            dec_sum = gradient(("dec", "skip"), "cots_dec")
        if dec_sum is not None and dec_step < dec_sum.steps:
            if tick - last_dec == (3 * dec_step + 1) // 2:
                dec_sum.send(dec_step, ahead_of("side", dec_sum.prepare(dec_step)))
                dec_step += 1
            elif dec_step not in dec_sum.ready:
                for step in range(dec_step, dec_sum.steps):
                    dec_sum.ready[step] = ahead_of("side", dec_sum.own_pair(step))
    enc_sum = gradient(("enc",), "cots_enc")
    enc_step = 0
    while enc_step < enc_sum.steps or dec_step < dec_sum.steps:
        pairs = {}
        if dec_step < dec_sum.steps:
            pairs["dec"] = dec_sum.prepare(dec_step)
        if enc_step < enc_sum.steps:
            pairs["enc"] = enc_sum.prepare(enc_step)
        pairs = lax.optimization_barrier(pairs)
        if "dec" in pairs:
            dec_sum.send(dec_step, pairs["dec"])
            dec_step += 1
        if "enc" in pairs:
            enc_sum.send(enc_step, pairs["enc"])
            enc_step += 1
    enc_share, dec_share = enc_sum.result(), dec_sum.result()
    return tuple(
        share.reshape((1, 3, 3) + share.shape[1:]) for share in (enc_share, dec_share)
    )


def solution(mesh):
    placed = (
        P("dp", None, None, None),
        P("dp", None, None, None),
        P("dp"),
        P("section", None, None, None, None),
        P("section", None, None, None, None),
    )
    return jax.shard_map(
        shards,
        mesh=mesh,
        in_specs=placed,
        out_specs=(P("section", None, None, "dp", None), P("section", None, None, "dp", None)),
        check_vma=False,
    )
```

```python
import functools
import math

import jax
import jax.numpy as jnp
import ml_dtypes
import numpy as np
from jax import lax
from jax.experimental import pallas as pl
from jax.experimental.pallas import tpu as pltpu
from jax.sharding import PartitionSpec as P

GROUPS = 32
F32 = jnp.float32
BF16 = jnp.bfloat16
ENC_FWD, DEC_FWD, DEC_BWD, ENC_BWD = 1, 2, 3, 4
STAGE_VMEM = 2 * 1024 * 1024
GRAD_VMEM = 8 * 1024 * 1024


def embed(stamps_in, channels):
    half_width = channels // 2
    frequency = jnp.exp(-math.log(10000.0) * jnp.arange(half_width, dtype=jnp.float32) / half_width)
    angles = stamps_in.astype(jnp.float32)[:, None] * frequency[None, :]
    return jnp.concatenate([jnp.sin(angles), jnp.cos(angles)], axis=1)


def noise_levels(stamps_in):
    phase = (stamps_in.astype(jnp.float32) / 1000.0 + 0.008) / 1.008 * (math.pi / 2.0)
    signal = jnp.cos(phase) ** 2
    return (jnp.sqrt(signal), jnp.sqrt(1.0 - signal))


def stage_of(position, sections):
    lap, step = divmod(position, sections)
    section = step if lap % 2 == 0 else sections - 1 - step
    return section, lap + 1


def make_schedule(sections, samples):
    stages = 4 * sections
    ticks = []
    for tick in range(stages + 2 * (samples - 1)):
        work, moves = {}, []
        for sample in range(samples):
            position = tick - 2 * sample
            if not 0 <= position < stages:
                continue
            section, op = stage_of(position, sections)
            assert section not in work
            work[section] = (op, sample)
            if position + 1 < stages:
                target, _ = stage_of(position + 1, sections)
                if target != section:
                    moves.append((section, target))
        ticks.append((work, moves))
    return ticks


def group_sums(vectors, members):
    channels = vectors[0].shape[1]
    row = lax.broadcasted_iota(jnp.int32, (16, channels), 0)
    stacked = jnp.zeros((16, channels), F32)
    for index, vector in enumerate(vectors):
        high = vector.astype(BF16).astype(F32)
        rest = vector - high
        middle = rest.astype(BF16).astype(F32)
        for part_index, part in enumerate((high, middle, rest - middle)):
            stacked = jnp.where(row == 3 * index + part_index, part, stacked)
    summed = jnp.dot(stacked.astype(BF16), members, preferred_element_type=F32)
    return [
        summed[3 * i : 3 * i + 1] + summed[3 * i + 1 : 3 * i + 2] + summed[3 * i + 2 : 3 * i + 3]
        for i in range(len(vectors))
    ]


def spread_columns(field, breadth, windows_ref):
    pixels, channels = field.shape
    column = lax.broadcasted_iota(jnp.int32, (pixels, channels), 0) & (breadth - 1)
    before = jnp.where(column == 0, 0.0, pltpu.roll(field, 1, 0))
    after = jnp.where(column == breadth - 1, 0.0, pltpu.roll(field, pixels - 1, 0))
    edge = jnp.zeros((breadth, channels), BF16)
    for index, shifted in enumerate((before, field, after)):
        lanes = slice(index * channels, (index + 1) * channels)
        windows_ref[0:breadth, lanes] = edge
        windows_ref[breadth : breadth + pixels, lanes] = shifted.astype(BF16)
        windows_ref[breadth + pixels : 2 * breadth + pixels, lanes] = edge


def convolve(windows_ref, weight_ref, first, pixels, breadth):
    outputs = weight_ref.shape[2]
    channels = windows_ref.shape[1] // 3
    total = None
    for row in range(3):
        part = jnp.dot(
            windows_ref[row * breadth : row * breadth + pixels, :],
            weight_ref[3 * row : 3 * row + 3, first : first + channels, :].reshape(
                3 * channels, outputs
            ),
            preferred_element_type=F32,
        )
        total = part if total is None else total + part
    return total


def chosen(index, values):
    result = jnp.int32(values[0])
    for position, value in enumerate(values):
        if value != values[0]:
            result = jnp.where(index == position, value, result)
    return result


def local_input(op, section, sections):
    return (op in (ENC_FWD, DEC_BWD) and section == 0) or (
        op in (DEC_FWD, ENC_BWD) and section == sections - 1
    )


def local_result(op, section, sections):
    return (
        op == ENC_FWD
        or (op == DEC_FWD and section == 0)
        or (op == DEC_BWD and section == sections - 1)
    )


KINDS = ("enc", "dec", "skip")


def touched(work, aside):
    ops = {op for op, _ in work.values()}
    names = ["kept", "side"]
    if aside:
        if ENC_FWD in ops:
            names += ["normed_skip", "scale_skip", "acts_enc", "turned_enc", "turned_skip"]
        if DEC_BWD in ops:
            names += ["normed_skip", "scale_skip", "cots_dec", "acts_dec", "turned_dec"]
    else:
        for op, kind in ((ENC_FWD, "enc"), (DEC_FWD, "dec")):
            if op in ops:
                names += ["normed_" + kind, "scale_" + kind, "acts_" + kind]
        for op, kind in ((ENC_BWD, "enc"), (DEC_BWD, "dec")):
            if op in ops:
                names += ["normed_" + kind, "scale_" + kind, "cots_" + kind]
    return list(dict.fromkeys(names))


def stage_kernel(work, aside, sections, breadth, factor, refs):
    pixels, channels = refs["kept"].shape[1:]
    section = lax.axis_index("section")
    jobs = [work.get(s, (0, 0)) for s in range(sections)]
    ops = {op for op, _ in jobs}
    op = chosen(section, [job[0] for job in jobs])
    slot = chosen(section, [job[1] for job in jobs])
    to_here = chosen(
        section, [int(local_result(job[0], s, sections)) for s, job in enumerate(jobs)]
    )
    kept, side = refs["kept"], refs["side"]
    group_size = channels // GROUPS

    def per_kind(kind):
        which = 0 if kind == "enc" else 1
        inverse_count = 1.0 / (pixels * group_size * (1 + which))
        modulation = refs["modulation"][KINDS.index(kind), slot]
        return refs["members"].at[which], inverse_count, modulation

    def load_input():
        leaving = refs["leaving"]
        cases = {}
        for s, (job_op, _) in enumerate(jobs):
            if job_op:
                local = local_input(job_op, s, sections)
                case = "noisy" if local and job_op == ENC_FWD else "kept" if local else "arriving"
                cases.setdefault(case, []).append(s)

        def fill(case):
            if case == "noisy":
                leaving[...] = refs["levels"][0, slot] * refs["clean"][slot].astype(F32) + refs[
                    "levels"
                ][1, slot] * refs["noise"][slot].astype(F32)
            elif case == "kept":
                leaving[...] = kept[slot]
            else:
                leaving[...] = refs["arriving"][...]

        for case, places in cases.items():
            here = functools.reduce(jnp.logical_or, [section == s for s in places])
            pl.when(here)(functools.partial(fill, case))
        return leaving[...]

    def forward(kind):
        members, inverse_count, modulation = per_kind(kind)
        windows = refs["windows"]
        x = kept[slot] if aside else load_input()
        total = jnp.sum(x, axis=0, keepdims=True)
        own_mean = total * (1.0 / pixels)
        own_dev = x - own_mean
        own_square = jnp.sum(own_dev * own_dev, axis=0, keepdims=True)
        (group_total,) = group_sums([total], members[...])
        mean = group_total * inverse_count
        apart = own_mean - mean
        (group_square,) = group_sums([own_square + pixels * (apart * apart)], members[...])
        inverse_std = lax.rsqrt(group_square * inverse_count + 1e-05)
        unit = (x - mean) * inverse_std
        value = unit * modulation
        active = value / (1.0 + jnp.exp(-value))
        refs["normed_" + kind][slot] = unit
        refs["scale_" + kind][slot] = inverse_std
        spread_columns(active, breadth, windows)
        if aside:
            side[slot] = convolve(windows, refs["dec_weight"], channels, pixels, breadth)
            refs["turned_enc"][slot] = refs["acts_enc"][slot].astype(F32).T.astype(BF16)
            refs["turned_skip"][slot] = active.T.astype(BF16)
            return
        refs["acts_" + kind][slot] = active.astype(BF16)
        leaving = refs["leaving"]
        if kind == "enc":
            leaving[...] += convolve(windows, refs["enc_weight"], 0, pixels, breadth)
        else:
            own = convolve(windows, refs["dec_weight"], 0, pixels, breadth)
            leaving[...] += own + side[slot]

            @pl.when(to_here == 1)
            def _():
                leaving[...] = factor * (leaving[...] - refs["noise"][slot].astype(F32))

        keep_result()

    def keep_result():
        if any(local_result(job[0], s, sections) for s, job in enumerate(jobs)):

            @pl.when(to_here == 1)
            def _():
                kept[slot] = refs["leaving"][...]

    def backward(kind):
        members, inverse_count, modulation = per_kind(kind)
        if aside:
            given = refs["cots_dec"].at[slot]
            refs["turned_dec"][slot] = refs["acts_dec"][slot].astype(F32).T.astype(BF16)
        else:
            given = refs["cots_" + kind].at[slot]
            leaving = refs["leaving"]
            load_input()
            if kind == "enc":
                leaving[...] = leaving[...] + side[slot]
            spread_columns(leaving[...], breadth, given)
        down = convolve(given, refs["flipped_" + kind], 0, pixels, breadth)
        unit = refs["normed_" + kind][slot]
        value = unit * modulation
        gate = 1.0 / (1.0 + jnp.exp(-value))
        slope = gate * (1.0 + value * (1.0 - gate))
        d_unit = down * slope * modulation
        sums = group_sums(
            [
                jnp.sum(d_unit, axis=0, keepdims=True),
                jnp.sum(d_unit * unit, axis=0, keepdims=True),
            ],
            members[...],
        )
        shift, stretch = sums[0] * inverse_count, sums[1] * inverse_count
        result = refs["scale_" + kind][slot] * (d_unit - shift - unit * stretch)
        if aside:
            side[slot] = result
        else:
            leaving[...] = leaving[...] + result
            keep_result()

    if aside:
        parts = ((ENC_FWD, forward, "skip"), (DEC_BWD, backward, "skip"))
    else:
        parts = (
            (ENC_FWD, forward, "enc"),
            (DEC_FWD, forward, "dec"),
            (DEC_BWD, backward, "dec"),
            (ENC_BWD, backward, "enc"),
        )
    for part_op, part, kind in parts:
        if part_op in ops:
            pl.when(op == part_op)(functools.partial(part, kind))


def call_stage(work, aside, sections, breadth, factor, arriving, consts, state):
    ops = {op for op, _ in work.values()}
    _, pixels, channels = state["kept"].shape
    vmem = pl.BlockSpec(memory_space=pltpu.VMEM)
    names = ["modulation", "members"]
    if ENC_FWD in ops and not aside:
        names.append("enc_weight")
    if (DEC_FWD in ops and not aside) or (ENC_FWD in ops and aside):
        names.append("dec_weight")
    if DEC_BWD in ops:
        names.append("flipped_skip" if aside else "flipped_dec")
    if ENC_BWD in ops and not aside:
        names.append("flipped_enc")
    starting = not aside and work.get(0, (0, 0))[0] == ENC_FWD
    if starting:
        names += ["levels", "clean"]
    if starting or (DEC_FWD in ops and not aside):
        names.append("noise")
    given = {name: consts[name] for name in names}
    if not aside and any(not local_input(op, s, sections) for s, (op, _) in work.items()):
        given["arriving"] = arriving
    used = touched(work, aside)
    present = [n for n in used if not isinstance(state[n], jax.ShapeDtypeStruct)]
    out_shape = {} if aside else {"leaving": jax.ShapeDtypeStruct((pixels, channels), F32)}
    for name in used:
        out_shape[name] = jax.ShapeDtypeStruct(state[name].shape, state[name].dtype)
    out_names = list(out_shape)

    def kernel(*refs):
        named = dict(zip(given, refs))
        named.update(zip(out_names, refs[len(given) + len(present) :]))
        named["windows"] = refs[-1]
        stage_kernel(work, aside, sections, breadth, factor, named)

    outs = pl.pallas_call(
        kernel,
        out_shape=list(out_shape.values()),
        in_specs=[vmem] * (len(given) + len(present)),
        out_specs=[vmem] * len(out_shape),
        scratch_shapes=[pltpu.VMEM((pixels + 2 * breadth, 3 * channels), BF16)],
        input_output_aliases={
            len(given) + i: out_names.index(name) for i, name in enumerate(present)
        },
        compiler_params=pltpu.CompilerParams(vmem_limit_bytes=STAGE_VMEM),
        cost_estimate=pl.CostEstimate(flops=1000, bytes_accessed=1000, transcendentals=0),
    )(*given.values(), *[state[n] for n in present])
    named = dict(zip(out_names, outs))
    leaving = named.pop("leaving", None)
    return leaving, {**state, **named}


def flip_kernel(enc_weight, dec_weight, after, *outs):
    taps, channels, _ = enc_weight.shape

    def one_tap(tap, carry):
        tiles = (
            enc_weight[tap],
            dec_weight[tap, 0:channels, :],
            dec_weight[tap, channels : 2 * channels, :],
        )
        for tile, out in zip(tiles, outs):
            out[taps - 1 - tap] = tile.astype(F32).T.astype(BF16)
        return carry

    lax.fori_loop(0, taps, one_tap, 0)


def flip(enc_weight, dec_weight, after):
    vmem = pl.BlockSpec(memory_space=pltpu.VMEM)
    return pl.pallas_call(
        flip_kernel,
        out_shape=[jax.ShapeDtypeStruct(enc_weight.shape, BF16)] * 3,
        in_specs=[vmem] * 3,
        out_specs=[vmem] * 3,
        compiler_params=pltpu.CompilerParams(vmem_limit_bytes=STAGE_VMEM),
    )(enc_weight, dec_weight, after)


def weight_grad_kernel(breadth, halves, group, chunks, *refs):
    turned, cots, outs, (ready, sems) = refs[:halves], refs[halves], refs[-4:-2], refs[-2:]
    samples, channels, pixels = turned[0].shape
    core = lax.axis_index("dp") % 2
    rows = halves * channels // chunks // 2
    places = [divmod(2 * chunk * rows, channels) for chunk in group]

    def store(tap, slot):
        return [
            pltpu.make_async_copy(ready.at[slot, i], outs[i].at[:, tap], sems.at[slot, i])
            for i in range(2)
        ]

    def one_tap(tap, carry):
        slot = lax.rem(tap, 2)
        row, col = tap // 3, lax.rem(tap, 3)
        start = pl.multiple_of((2 - row) * breadth, breadth)
        lane = pl.multiple_of((2 - col) * channels, 128)
        total = None
        for sample in range(samples):
            lines = [
                turned[half][sample, first : first + 2 * rows, :]
                for half, first in places
            ]
            part = jnp.dot(
                jnp.concatenate(lines, axis=0),
                cots[sample, pl.ds(start, pixels), pl.ds(lane, channels)],
                preferred_element_type=F32,
            )
            total = part if total is None else total + part

        @pl.when(tap >= 2)
        def _():
            for one in store(tap, slot):
                one.wait()

        pieces = total.reshape(len(group), 2, rows, channels)
        ready[slot, 0] = jnp.where(core == 0, pieces[:, 0], pieces[:, 1])
        ready[slot, 1] = jnp.where(core == 0, pieces[:, 1], pieces[:, 0])
        for one in store(tap, slot):
            one.start()
        return carry

    lax.fori_loop(0, 9, one_tap, 0)
    for tap in (7, 8):
        for one in store(tap, tap % 2):
            one.wait()


def weight_grad(turned, cots, group, breadth):
    _, channels, _ = turned[0].shape
    chunks = lax.axis_size("dp") // 2
    rows = len(turned) * channels // chunks // 2
    vmem = pl.BlockSpec(memory_space=pltpu.VMEM)
    hbm = pl.BlockSpec(memory_space=pltpu.HBM)
    shape = jax.ShapeDtypeStruct((len(group), 9, rows, channels), F32)
    return pl.pallas_call(
        functools.partial(weight_grad_kernel, breadth, len(turned), tuple(group), chunks),
        out_shape=[shape, shape],
        in_specs=[vmem] * (len(turned) + 1),
        out_specs=[hbm, hbm],
        scratch_shapes=[
            pltpu.VMEM((2, 2, len(group), rows, channels), F32),
            pltpu.SemaphoreType.DMA((2, 2)),
        ],
        compiler_params=pltpu.CompilerParams(vmem_limit_bytes=GRAD_VMEM),
        cost_estimate=pl.CostEstimate(flops=1000, bytes_accessed=1000, transcendentals=0),
    )(*turned, cots)


def member_matrices(channels):
    channel = np.arange(channels)
    size = channels // GROUPS
    return np.stack(
        [channel[:, None] // n == channel[None, :] // n for n in (size, 2 * size)]
    ).astype(ml_dtypes.bfloat16)


class LineSum:
    def __init__(self, make):
        self.count = lax.axis_size("dp")
        self.chips = self.count // 2
        self.steps = self.chips - 1
        self.place = lax.axis_index("dp") // 2
        self.arrived = None
        self.ends = self.swap(*make([0, self.chips - 1]))
        middle = list(range(1, self.chips - 1))
        self.middle = self.swap(*make(middle)) if middle else None

    def swap(self, kept, given):
        moves = [(d, d + 1 - 2 * (d % 2)) for d in range(self.count)]
        return kept, lax.ppermute(given, "dp", moves)

    def end(self, index):
        kept, swapped = self.ends
        return kept[index] + swapped[index]

    def between(self, chunk):
        index = jnp.clip(chunk - 1, 0, self.chips - 3)
        return sum(lax.dynamic_index_in_dim(part, index, 0, False) for part in self.middle)

    def own_pair(self, step):
        up, down = self.end(1), self.end(0)
        if step:
            back = self.chips - 1 - self.place
            up = jnp.where(self.place == step, up, self.between(back - step + 2 * self.place))
            down = jnp.where(back == step, down, self.between(step - back))
        return up, down

    def prepare(self, step):
        up, down = self.own_pair(step)
        if step:
            up, down = up + self.arrived[0], down + self.arrived[1]
        return up, down

    def send(self, step, pair):
        last = self.chips - 1
        moves = [(z, c) for z in range(min(step + 1, last)) for c in range(2)]
        up = lax.ppermute(pair[0], "dp", [(2 * z + c, 2 * z + 2 + c) for z, c in moves])
        down = lax.ppermute(
            pair[1], "dp", [(2 * (last - z) + c, 2 * (last - z) - 2 + c) for z, c in moves]
        )
        self.arrived = lax.optimization_barrier((up, down))

    def result(self):
        total = jnp.where(self.place == 0, self.end(0), self.end(1))
        if self.middle is not None:
            outer = jnp.logical_or(self.place == 0, self.place == self.chips - 1)
            total = jnp.where(outer, total, self.between(self.place))
        return total + self.arrived[0] + self.arrived[1]


def shards(clean, noise, stamps, enc_weight, dec_weight):
    sections = lax.axis_size("section")
    samples, height, breadth, channels = clean.shape
    pixels = height * breadth
    factor = 1.0 / math.sqrt(samples * lax.axis_size("dp") * pixels)
    ticks = make_schedule(sections, samples)

    levels = jnp.stack(noise_levels(stamps))
    wide = embed(stamps, 2 * channels)
    modulation = 1.0 + 0.5 * jnp.stack(
        [embed(stamps, channels), wide[:, :channels], wide[:, channels:]]
    )
    consts = {
        "modulation": modulation[:, :, None, :],
        "members": jnp.asarray(member_matrices(channels)),
        "enc_weight": enc_weight.reshape(9, channels, channels),
        "dec_weight": dec_weight.reshape(9, 2 * channels, channels),
        "levels": jnp.broadcast_to(levels[:, :, None, None], (2, samples, 1, channels)),
        "clean": clean.reshape(samples, pixels, channels),
        "noise": noise.reshape(samples, pixels, channels),
    }
    weights = (consts["enc_weight"], consts["dec_weight"])
    fresh = jax.ShapeDtypeStruct
    field = (samples, pixels, channels)
    state = {"kept": fresh(field, F32), "side": fresh(field, F32)}
    for kind in KINDS:
        state["normed_" + kind] = fresh(field, F32)
        state["scale_" + kind] = fresh((samples, 1, channels), F32)
        state["turned_" + kind] = fresh((samples, channels, pixels), BF16)
        if kind != "skip":
            state["acts_" + kind] = fresh(field, BF16)
            state["cots_" + kind] = fresh(
                (samples, pixels + 2 * breadth, 3 * channels), BF16
            )
    arriving = None
    last_dec = max(
        tick for tick, (work, _) in enumerate(ticks) if any(w[0] == DEC_BWD for w in work.values())
    )
    flip_tick = min(
        tick for tick, (work, _) in enumerate(ticks) if any(w[0] == DEC_BWD for w in work.values())
    ) - 2
    dec_sum = None
    dec_step = 0

    def gradient(kinds, cots):
        turned = [state["turned_" + kind] for kind in kinds]
        return LineSum(lambda group: weight_grad(turned, state[cots], group, breadth))

    def ahead_of(name, value):
        state[name], value = lax.optimization_barrier((state[name], value))
        return value

    for tick, (work, moves) in enumerate(ticks):
        ops = {op for op, _ in work.values()}
        leaving, state = call_stage(
            work, False, sections, breadth, factor, arriving, consts, state
        )
        if moves:
            arriving = lax.ppermute(leaving, "section", moves)
        if ops & {ENC_FWD, DEC_BWD}:
            _, state = call_stage(work, True, sections, breadth, factor, None, consts, state)
        if tick == flip_tick:
            flipped = flip(*weights, state["scale_skip"])
            consts.update(zip(["flipped_" + kind for kind in KINDS], flipped))
        if tick == last_dec:
            dec_sum = gradient(("dec", "skip"), "cots_dec")
        if dec_sum is not None and dec_step < dec_sum.steps and (tick - last_dec) % 2 == 0:
            if tick < len(ticks) - 1:
                dec_sum.send(dec_step, ahead_of("side", dec_sum.prepare(dec_step)))
                dec_step += 1
    enc_sum = gradient(("enc",), "cots_enc")
    enc_step = 0
    while enc_step < enc_sum.steps or dec_step < dec_sum.steps:
        pairs = {}
        if dec_step < dec_sum.steps:
            pairs["dec"] = dec_sum.prepare(dec_step)
        if enc_step < enc_sum.steps:
            pairs["enc"] = enc_sum.prepare(enc_step)
        pairs = lax.optimization_barrier(pairs)
        if "dec" in pairs:
            dec_sum.send(dec_step, pairs["dec"])
            dec_step += 1
        if "enc" in pairs:
            enc_sum.send(enc_step, pairs["enc"])
            enc_step += 1
    enc_share, dec_share = enc_sum.result(), dec_sum.result()
    return tuple(
        share.reshape((1, 3, 3) + share.shape[1:]) for share in (enc_share, dec_share)
    )


def solution(mesh):
    placed = (
        P("dp", None, None, None),
        P("dp", None, None, None),
        P("dp"),
        P("section", None, None, None, None),
        P("section", None, None, None, None),
    )
    return jax.shard_map(
        shards,
        mesh=mesh,
        in_specs=placed,
        out_specs=(P("section", None, None, "dp", None), P("section", None, None, "dp", None)),
        check_vma=False,
    )
```

```python
import functools
import math

import jax
import jax.numpy as jnp
import ml_dtypes
import numpy as np
from jax import lax
from jax.experimental import pallas as pl
from jax.experimental.pallas import tpu as pltpu
from jax.sharding import PartitionSpec as P

GROUPS = 32
F32 = jnp.float32
BF16 = jnp.bfloat16
ENC_FWD, DEC_FWD, DEC_BWD, ENC_BWD = 1, 2, 3, 4
STAGE_VMEM = 3 * 1024 * 1024
GRAD_VMEM = 8 * 1024 * 1024


def embed(stamps_in, channels):
    half_width = channels // 2
    frequency = jnp.exp(-math.log(10000.0) * jnp.arange(half_width, dtype=jnp.float32) / half_width)
    angles = stamps_in.astype(jnp.float32)[:, None] * frequency[None, :]
    return jnp.concatenate([jnp.sin(angles), jnp.cos(angles)], axis=1)


def noise_levels(stamps_in):
    phase = (stamps_in.astype(jnp.float32) / 1000.0 + 0.008) / 1.008 * (math.pi / 2.0)
    signal = jnp.cos(phase) ** 2
    return (jnp.sqrt(signal), jnp.sqrt(1.0 - signal))


def stage_of(position, sections):
    lap, step = divmod(position, sections)
    section = step if lap % 2 == 0 else sections - 1 - step
    return section, lap + 1


def make_schedule(sections, samples):
    stages = 4 * sections
    ticks = []
    for tick in range(stages + 2 * (samples - 1)):
        work, moves = {}, []
        for sample in range(samples):
            position = tick - 2 * sample
            if not 0 <= position < stages:
                continue
            section, op = stage_of(position, sections)
            assert section not in work
            work[section] = (op, sample)
            if position + 1 < stages:
                target, _ = stage_of(position + 1, sections)
                if target != section:
                    moves.append((section, target))
        ticks.append((work, moves))
    return ticks


def group_sums(vectors, members):
    channels = vectors[0].shape[1]
    row = lax.broadcasted_iota(jnp.int32, (16, channels), 0)
    stacked = jnp.zeros((16, channels), F32)
    for index, vector in enumerate(vectors):
        high = vector.astype(BF16).astype(F32)
        rest = vector - high
        middle = rest.astype(BF16).astype(F32)
        for part_index, part in enumerate((high, middle, rest - middle)):
            stacked = jnp.where(row == 3 * index + part_index, part, stacked)
    summed = jnp.dot(stacked.astype(BF16), members, preferred_element_type=F32)
    return [
        summed[3 * i : 3 * i + 1] + summed[3 * i + 1 : 3 * i + 2] + summed[3 * i + 2 : 3 * i + 3]
        for i in range(len(vectors))
    ]


def spread_columns(field, breadth, windows_ref):
    pixels, channels = field.shape
    column = lax.broadcasted_iota(jnp.int32, (pixels, channels), 0) & (breadth - 1)
    before = jnp.where(column == 0, 0.0, pltpu.roll(field, 1, 0))
    after = jnp.where(column == breadth - 1, 0.0, pltpu.roll(field, pixels - 1, 0))
    edge = jnp.zeros((breadth, channels), BF16)
    for index, shifted in enumerate((before, field, after)):
        lanes = slice(index * channels, (index + 1) * channels)
        windows_ref[0:breadth, lanes] = edge
        windows_ref[breadth : breadth + pixels, lanes] = shifted.astype(BF16)
        windows_ref[breadth + pixels : 2 * breadth + pixels, lanes] = edge


def add_convolution(total_ref, windows_ref, weight_ref, first, pixels, breadth):
    outputs = weight_ref.shape[2]
    channels = windows_ref.shape[1] // 3

    def one_row(row, carry):
        start = pl.multiple_of(row * breadth, breadth)
        total_ref[...] += jnp.dot(
            windows_ref[pl.ds(start, pixels), :],
            weight_ref[pl.ds(3 * row, 3), first : first + channels, :].reshape(
                3 * channels, outputs
            ),
            preferred_element_type=F32,
        )
        return carry

    lax.fori_loop(0, 3, one_row, 0)


def chosen(index, values):
    result = jnp.int32(values[0])
    for position, value in enumerate(values):
        if value != values[0]:
            result = jnp.where(index == position, value, result)
    return result


def local_input(op, section, sections):
    return (op in (ENC_FWD, DEC_BWD) and section == 0) or (
        op in (DEC_FWD, ENC_BWD) and section == sections - 1
    )


def local_result(op, section, sections):
    return (
        op == ENC_FWD
        or (op == DEC_FWD and section == 0)
        or (op == DEC_BWD and section == sections - 1)
    )


KINDS = ("enc", "dec", "skip")


def touched(work, aside):
    ops = {op for op, _ in work.values()}
    names = ["kept", "side"]
    if aside:
        if ENC_FWD in ops:
            names += ["normed_skip", "scale_skip", "acts_enc", "turned_enc", "turned_skip"]
        if DEC_BWD in ops:
            names += ["normed_skip", "scale_skip", "cots_dec", "acts_dec", "turned_dec"]
    else:
        for op, kind in ((ENC_FWD, "enc"), (DEC_FWD, "dec")):
            if op in ops:
                names += ["normed_" + kind, "scale_" + kind, "acts_" + kind]
        for op, kind in ((ENC_BWD, "enc"), (DEC_BWD, "dec")):
            if op in ops:
                names += ["normed_" + kind, "scale_" + kind, "cots_" + kind]
    return list(dict.fromkeys(names))


def stage_kernel(work, aside, sections, breadth, factor, refs):
    pixels, channels = refs["kept"].shape[1:]
    section = lax.axis_index("section")
    jobs = [work.get(s, (0, 0)) for s in range(sections)]
    ops = {op for op, _ in jobs}
    op = chosen(section, [job[0] for job in jobs])
    slot = chosen(section, [job[1] for job in jobs])
    to_here = chosen(
        section, [int(local_result(job[0], s, sections)) for s, job in enumerate(jobs)]
    )
    kept, side = refs["kept"], refs["side"]
    group_size = channels // GROUPS

    def per_kind(kind):
        which = 0 if kind == "enc" else 1
        inverse_count = 1.0 / (pixels * group_size * (1 + which))
        modulation = refs["modulation"][KINDS.index(kind), slot]
        return refs["members"].at[which], inverse_count, modulation

    def load_input():
        leaving = refs["leaving"]
        cases = {}
        for s, (job_op, _) in enumerate(jobs):
            if job_op:
                local = local_input(job_op, s, sections)
                case = "noisy" if local and job_op == ENC_FWD else "kept" if local else "arriving"
                cases.setdefault(case, []).append(s)

        def fill(case):
            if case == "noisy":
                leaving[...] = refs["levels"][0, slot] * refs["clean"][slot].astype(F32) + refs[
                    "levels"
                ][1, slot] * refs["noise"][slot].astype(F32)
            elif case == "kept":
                leaving[...] = kept[slot]
            else:
                leaving[...] = refs["arriving"][...]

        for case, places in cases.items():
            here = functools.reduce(jnp.logical_or, [section == s for s in places])
            pl.when(here)(functools.partial(fill, case))
        return leaving[...]

    def forward(kind):
        members, inverse_count, modulation = per_kind(kind)
        windows = refs["windows"]
        x = kept[slot] if aside else load_input()
        total = jnp.sum(x, axis=0, keepdims=True)
        own_mean = total * (1.0 / pixels)
        own_dev = x - own_mean
        own_square = jnp.sum(own_dev * own_dev, axis=0, keepdims=True)
        (group_total,) = group_sums([total], members[...])
        mean = group_total * inverse_count
        apart = own_mean - mean
        (group_square,) = group_sums([own_square + pixels * (apart * apart)], members[...])
        inverse_std = lax.rsqrt(group_square * inverse_count + 1e-05)
        unit = (x - mean) * inverse_std
        value = unit * modulation
        active = value / (1.0 + jnp.exp(-value))
        refs["normed_" + kind][slot] = unit
        refs["scale_" + kind][slot] = inverse_std
        spread_columns(active, breadth, windows)
        if aside:
            side[slot] = jnp.zeros((pixels, channels), F32)
            add_convolution(
                side.at[slot], windows, refs["dec_weight"], channels, pixels, breadth
            )
            refs["turned_enc"][slot] = refs["acts_enc"][slot].astype(F32).T.astype(BF16)
            refs["turned_skip"][slot] = active.T.astype(BF16)
            return
        refs["acts_" + kind][slot] = active.astype(BF16)
        leaving = refs["leaving"]
        if kind == "enc":
            add_convolution(leaving, windows, refs["enc_weight"], 0, pixels, breadth)
        else:
            leaving[...] += side[slot]
            add_convolution(leaving, windows, refs["dec_weight"], 0, pixels, breadth)

            @pl.when(to_here == 1)
            def _():
                leaving[...] = factor * (leaving[...] - refs["noise"][slot].astype(F32))

        keep_result()

    def keep_result():
        if any(local_result(job[0], s, sections) for s, job in enumerate(jobs)):

            @pl.when(to_here == 1)
            def _():
                kept[slot] = refs["leaving"][...]

    def backward(kind):
        members, inverse_count, modulation = per_kind(kind)
        if aside:
            given = refs["cots_dec"].at[slot]
            refs["turned_dec"][slot] = refs["acts_dec"][slot].astype(F32).T.astype(BF16)
        else:
            given = refs["cots_" + kind].at[slot]
            leaving = refs["leaving"]
            load_input()
            if kind == "enc":
                leaving[...] = leaving[...] + side[slot]
            spread_columns(leaving[...], breadth, given)
        down_ref = refs["down"]
        down_ref[...] = jnp.zeros((pixels, channels), F32)
        add_convolution(down_ref, given, refs["flipped_" + kind], 0, pixels, breadth)
        down = down_ref[...]
        unit = refs["normed_" + kind][slot]
        value = unit * modulation
        gate = 1.0 / (1.0 + jnp.exp(-value))
        slope = gate * (1.0 + value * (1.0 - gate))
        d_unit = down * slope * modulation
        sums = group_sums(
            [
                jnp.sum(d_unit, axis=0, keepdims=True),
                jnp.sum(d_unit * unit, axis=0, keepdims=True),
            ],
            members[...],
        )
        shift, stretch = sums[0] * inverse_count, sums[1] * inverse_count
        result = refs["scale_" + kind][slot] * (d_unit - shift - unit * stretch)
        if aside:
            side[slot] = result
        else:
            leaving[...] = leaving[...] + result
            keep_result()

    if aside:
        parts = ((ENC_FWD, forward, "skip"), (DEC_BWD, backward, "skip"))
    else:
        parts = (
            (ENC_FWD, forward, "enc"),
            (DEC_FWD, forward, "dec"),
            (DEC_BWD, backward, "dec"),
            (ENC_BWD, backward, "enc"),
        )
    for part_op, part, kind in parts:
        if part_op in ops:
            pl.when(op == part_op)(functools.partial(part, kind))


def call_stage(work, aside, sections, breadth, factor, arriving, consts, state):
    ops = {op for op, _ in work.values()}
    _, pixels, channels = state["kept"].shape
    vmem = pl.BlockSpec(memory_space=pltpu.VMEM)
    names = ["modulation", "members"]
    if ENC_FWD in ops and not aside:
        names.append("enc_weight")
    if (DEC_FWD in ops and not aside) or (ENC_FWD in ops and aside):
        names.append("dec_weight")
    if DEC_BWD in ops:
        names.append("flipped_skip" if aside else "flipped_dec")
    if ENC_BWD in ops and not aside:
        names.append("flipped_enc")
    starting = not aside and work.get(0, (0, 0))[0] == ENC_FWD
    if starting:
        names += ["levels", "clean"]
    if starting or (DEC_FWD in ops and not aside):
        names.append("noise")
    given = {name: consts[name] for name in names}
    if not aside and any(not local_input(op, s, sections) for s, (op, _) in work.items()):
        given["arriving"] = arriving
    used = touched(work, aside)
    present = [n for n in used if not isinstance(state[n], jax.ShapeDtypeStruct)]
    out_shape = {} if aside else {"leaving": jax.ShapeDtypeStruct((pixels, channels), F32)}
    for name in used:
        out_shape[name] = jax.ShapeDtypeStruct(state[name].shape, state[name].dtype)
    out_names = list(out_shape)

    def kernel(*refs):
        named = dict(zip(given, refs))
        named.update(zip(out_names, refs[len(given) + len(present) :]))
        named["windows"], named["down"] = refs[-2:]
        stage_kernel(work, aside, sections, breadth, factor, named)

    outs = pl.pallas_call(
        kernel,
        out_shape=list(out_shape.values()),
        in_specs=[vmem] * (len(given) + len(present)),
        out_specs=[vmem] * len(out_shape),
        scratch_shapes=[
            pltpu.VMEM((pixels + 2 * breadth, 3 * channels), BF16),
            pltpu.VMEM((pixels, channels), F32),
        ],
        input_output_aliases={
            len(given) + i: out_names.index(name) for i, name in enumerate(present)
        },
        compiler_params=pltpu.CompilerParams(vmem_limit_bytes=STAGE_VMEM),
        cost_estimate=pl.CostEstimate(flops=1000, bytes_accessed=1000, transcendentals=0),
    )(*given.values(), *[state[n] for n in present])
    named = dict(zip(out_names, outs))
    leaving = named.pop("leaving", None)
    return leaving, {**state, **named}


def flip_kernel(enc_weight, dec_weight, after, *outs):
    taps, channels, _ = enc_weight.shape

    def one_tap(tap, carry):
        tiles = (
            enc_weight[tap],
            dec_weight[tap, 0:channels, :],
            dec_weight[tap, channels : 2 * channels, :],
        )
        for tile, out in zip(tiles, outs):
            out[taps - 1 - tap] = tile.astype(F32).T.astype(BF16)
        return carry

    lax.fori_loop(0, taps, one_tap, 0)


def flip(enc_weight, dec_weight, after):
    vmem = pl.BlockSpec(memory_space=pltpu.VMEM)
    return pl.pallas_call(
        flip_kernel,
        out_shape=[jax.ShapeDtypeStruct(enc_weight.shape, BF16)] * 3,
        in_specs=[vmem] * 3,
        out_specs=[vmem] * 3,
        compiler_params=pltpu.CompilerParams(vmem_limit_bytes=STAGE_VMEM),
    )(enc_weight, dec_weight, after)


def weight_grad_kernel(breadth, halves, group, chunks, *refs):
    turned, cots, outs, (ready, sems) = refs[:halves], refs[halves], refs[-4:-2], refs[-2:]
    samples, channels, pixels = turned[0].shape
    core = lax.axis_index("dp") % 2
    rows = halves * channels // chunks // 2
    places = [divmod(2 * chunk * rows, channels) for chunk in group]

    def store(tap, slot):
        return [
            pltpu.make_async_copy(ready.at[slot, i], outs[i].at[:, tap], sems.at[slot, i])
            for i in range(2)
        ]

    def one_tap(tap, carry):
        slot = lax.rem(tap, 2)
        row, col = tap // 3, lax.rem(tap, 3)
        start = pl.multiple_of((2 - row) * breadth, breadth)
        lane = pl.multiple_of((2 - col) * channels, 128)
        total = None
        for sample in range(samples):
            lines = [
                turned[half][sample, first : first + 2 * rows, :]
                for half, first in places
            ]
            part = jnp.dot(
                jnp.concatenate(lines, axis=0),
                cots[sample, pl.ds(start, pixels), pl.ds(lane, channels)],
                preferred_element_type=F32,
            )
            total = part if total is None else total + part

        @pl.when(tap >= 2)
        def _():
            for one in store(tap, slot):
                one.wait()

        pieces = total.reshape(len(group), 2, rows, channels)
        ready[slot, 0] = jnp.where(core == 0, pieces[:, 0], pieces[:, 1])
        ready[slot, 1] = jnp.where(core == 0, pieces[:, 1], pieces[:, 0])
        for one in store(tap, slot):
            one.start()
        return carry

    lax.fori_loop(0, 9, one_tap, 0)
    for tap in (7, 8):
        for one in store(tap, tap % 2):
            one.wait()


def weight_grad(turned, cots, group, breadth):
    _, channels, _ = turned[0].shape
    chunks = lax.axis_size("dp") // 2
    rows = len(turned) * channels // chunks // 2
    vmem = pl.BlockSpec(memory_space=pltpu.VMEM)
    hbm = pl.BlockSpec(memory_space=pltpu.HBM)
    shape = jax.ShapeDtypeStruct((len(group), 9, rows, channels), F32)
    return pl.pallas_call(
        functools.partial(weight_grad_kernel, breadth, len(turned), tuple(group), chunks),
        out_shape=[shape, shape],
        in_specs=[vmem] * (len(turned) + 1),
        out_specs=[hbm, hbm],
        scratch_shapes=[
            pltpu.VMEM((2, 2, len(group), rows, channels), F32),
            pltpu.SemaphoreType.DMA((2, 2)),
        ],
        compiler_params=pltpu.CompilerParams(vmem_limit_bytes=GRAD_VMEM),
        cost_estimate=pl.CostEstimate(flops=1000, bytes_accessed=1000, transcendentals=0),
    )(*turned, cots)


def member_matrices(channels):
    channel = np.arange(channels)
    size = channels // GROUPS
    return np.stack(
        [channel[:, None] // n == channel[None, :] // n for n in (size, 2 * size)]
    ).astype(ml_dtypes.bfloat16)


class LineSum:
    def __init__(self, make):
        self.count = lax.axis_size("dp")
        self.chips = self.count // 2
        self.steps = self.chips - 1
        self.place = lax.axis_index("dp") // 2
        self.arrived = None
        self.ends = self.swap(*make([0, self.chips - 1]))
        middle = list(range(1, self.chips - 1))
        self.middle = self.swap(*make(middle)) if middle else None

    def swap(self, kept, given):
        moves = [(d, d + 1 - 2 * (d % 2)) for d in range(self.count)]
        return kept, lax.ppermute(given, "dp", moves)

    def end(self, index):
        kept, swapped = self.ends
        return kept[index] + swapped[index]

    def between(self, chunk):
        index = jnp.clip(chunk - 1, 0, self.chips - 3)
        return sum(lax.dynamic_index_in_dim(part, index, 0, False) for part in self.middle)

    def own_pair(self, step):
        up, down = self.end(1), self.end(0)
        if step:
            back = self.chips - 1 - self.place
            up = jnp.where(self.place == step, up, self.between(back - step + 2 * self.place))
            down = jnp.where(back == step, down, self.between(step - back))
        return up, down

    def prepare(self, step):
        up, down = self.own_pair(step)
        if step:
            up, down = up + self.arrived[0], down + self.arrived[1]
        return up, down

    def send(self, step, pair):
        last = self.chips - 1
        moves = [(z, c) for z in range(min(step + 1, last)) for c in range(2)]
        up = lax.ppermute(pair[0], "dp", [(2 * z + c, 2 * z + 2 + c) for z, c in moves])
        down = lax.ppermute(
            pair[1], "dp", [(2 * (last - z) + c, 2 * (last - z) - 2 + c) for z, c in moves]
        )
        self.arrived = lax.optimization_barrier((up, down))

    def result(self):
        total = jnp.where(self.place == 0, self.end(0), self.end(1))
        if self.middle is not None:
            outer = jnp.logical_or(self.place == 0, self.place == self.chips - 1)
            total = jnp.where(outer, total, self.between(self.place))
        return total + self.arrived[0] + self.arrived[1]


def shards(clean, noise, stamps, enc_weight, dec_weight):
    sections = lax.axis_size("section")
    samples, height, breadth, channels = clean.shape
    pixels = height * breadth
    factor = 1.0 / math.sqrt(samples * lax.axis_size("dp") * pixels)
    ticks = make_schedule(sections, samples)

    levels = jnp.stack(noise_levels(stamps))
    wide = embed(stamps, 2 * channels)
    modulation = 1.0 + 0.5 * jnp.stack(
        [embed(stamps, channels), wide[:, :channels], wide[:, channels:]]
    )
    consts = {
        "modulation": modulation[:, :, None, :],
        "members": jnp.asarray(member_matrices(channels)),
        "enc_weight": enc_weight.reshape(9, channels, channels),
        "dec_weight": dec_weight.reshape(9, 2 * channels, channels),
        "levels": jnp.broadcast_to(levels[:, :, None, None], (2, samples, 1, channels)),
        "clean": clean.reshape(samples, pixels, channels),
        "noise": noise.reshape(samples, pixels, channels),
    }
    weights = (consts["enc_weight"], consts["dec_weight"])
    fresh = jax.ShapeDtypeStruct
    field = (samples, pixels, channels)
    state = {"kept": fresh(field, F32), "side": fresh(field, F32)}
    for kind in KINDS:
        state["normed_" + kind] = fresh(field, F32)
        state["scale_" + kind] = fresh((samples, 1, channels), F32)
        state["turned_" + kind] = fresh((samples, channels, pixels), BF16)
        if kind != "skip":
            state["acts_" + kind] = fresh(field, BF16)
            state["cots_" + kind] = fresh(
                (samples, pixels + 2 * breadth, 3 * channels), BF16
            )
    arriving = None
    last_dec = max(
        tick for tick, (work, _) in enumerate(ticks) if any(w[0] == DEC_BWD for w in work.values())
    )
    flip_tick = min(
        tick for tick, (work, _) in enumerate(ticks) if any(w[0] == DEC_BWD for w in work.values())
    ) - 2
    dec_sum = None
    dec_step = 0

    def gradient(kinds, cots):
        turned = [state["turned_" + kind] for kind in kinds]
        return LineSum(lambda group: weight_grad(turned, state[cots], group, breadth))

    def ahead_of(name, value):
        state[name], value = lax.optimization_barrier((state[name], value))
        return value

    for tick, (work, moves) in enumerate(ticks):
        ops = {op for op, _ in work.values()}
        leaving, state = call_stage(
            work, False, sections, breadth, factor, arriving, consts, state
        )
        if moves:
            arriving = lax.ppermute(leaving, "section", moves)
        if ops & {ENC_FWD, DEC_BWD}:
            _, state = call_stage(work, True, sections, breadth, factor, None, consts, state)
        if tick == flip_tick:
            flipped = flip(*weights, state["scale_skip"])
            consts.update(zip(["flipped_" + kind for kind in KINDS], flipped))
        if tick == last_dec:
            dec_sum = gradient(("dec", "skip"), "cots_dec")
        if dec_sum is not None and dec_step < dec_sum.steps and tick < len(ticks) - 1:
            if tick - last_dec == 3 * dec_step // 2:
                if dec_step:
                    dec_sum.arrived, arriving = lax.optimization_barrier(
                        (dec_sum.arrived, arriving)
                    )
                dec_sum.send(dec_step, ahead_of("side", dec_sum.prepare(dec_step)))
                dec_step += 1
    enc_sum = gradient(("enc",), "cots_enc")
    for step in range(dec_step, dec_sum.steps):
        dec_sum.send(step, dec_sum.prepare(step))
    for step in range(enc_sum.steps):
        pair = enc_sum.prepare(step)
        if step == 0:
            pair, dec_sum.arrived = lax.optimization_barrier((pair, dec_sum.arrived))
        enc_sum.send(step, pair)
    enc_share, dec_share = enc_sum.result(), dec_sum.result()
    return tuple(
        share.reshape((1, 3, 3) + share.shape[1:]) for share in (enc_share, dec_share)
    )


def solution(mesh):
    placed = (
        P("dp", None, None, None),
        P("dp", None, None, None),
        P("dp"),
        P("section", None, None, None, None),
        P("section", None, None, None, None),
    )
    return jax.shard_map(
        shards,
        mesh=mesh,
        in_specs=placed,
        out_specs=(P("section", None, None, "dp", None), P("section", None, None, "dp", None)),
        check_vma=False,
    )
```

```python
import functools
import math

import jax
import jax.numpy as jnp
import ml_dtypes
import numpy as np
from jax import lax
from jax.experimental import pallas as pl
from jax.experimental.pallas import tpu as pltpu
from jax.sharding import PartitionSpec as P

GROUPS = 32
F32 = jnp.float32
BF16 = jnp.bfloat16
ENC_FWD, DEC_FWD, DEC_BWD, ENC_BWD = 1, 2, 3, 4
STAGE_VMEM = 3 * 1024 * 1024
GRAD_VMEM = 8 * 1024 * 1024


def embed(stamps_in, channels):
    half_width = channels // 2
    frequency = jnp.exp(-math.log(10000.0) * jnp.arange(half_width, dtype=jnp.float32) / half_width)
    angles = stamps_in.astype(jnp.float32)[:, None] * frequency[None, :]
    return jnp.concatenate([jnp.sin(angles), jnp.cos(angles)], axis=1)


def noise_levels(stamps_in):
    phase = (stamps_in.astype(jnp.float32) / 1000.0 + 0.008) / 1.008 * (math.pi / 2.0)
    signal = jnp.cos(phase) ** 2
    return (jnp.sqrt(signal), jnp.sqrt(1.0 - signal))


def stage_of(position, sections):
    lap, step = divmod(position, sections)
    section = step if lap % 2 == 0 else sections - 1 - step
    return section, lap + 1


def make_schedule(sections, samples):
    stages = 4 * sections
    ticks = []
    for tick in range(stages + 2 * (samples - 1)):
        work, moves = {}, []
        for sample in range(samples):
            position = tick - 2 * sample
            if not 0 <= position < stages:
                continue
            section, op = stage_of(position, sections)
            assert section not in work
            work[section] = (op, sample)
            if position + 1 < stages:
                target, _ = stage_of(position + 1, sections)
                if target != section:
                    moves.append((section, target))
        ticks.append((work, moves))
    return ticks


def group_sums(vectors, members):
    channels = vectors[0].shape[1]
    row = lax.broadcasted_iota(jnp.int32, (16, channels), 0)
    stacked = jnp.zeros((16, channels), F32)
    for index, vector in enumerate(vectors):
        high = vector.astype(BF16).astype(F32)
        rest = vector - high
        middle = rest.astype(BF16).astype(F32)
        for part_index, part in enumerate((high, middle, rest - middle)):
            stacked = jnp.where(row == 3 * index + part_index, part, stacked)
    summed = jnp.dot(stacked.astype(BF16), members, preferred_element_type=F32)
    return [
        summed[3 * i : 3 * i + 1] + summed[3 * i + 1 : 3 * i + 2] + summed[3 * i + 2 : 3 * i + 3]
        for i in range(len(vectors))
    ]


def spread_columns(field, breadth, windows_ref):
    pixels, channels = field.shape
    column = lax.broadcasted_iota(jnp.int32, (pixels, channels), 0) & (breadth - 1)
    before = jnp.where(column == 0, 0.0, pltpu.roll(field, 1, 0))
    after = jnp.where(column == breadth - 1, 0.0, pltpu.roll(field, pixels - 1, 0))
    edge = jnp.zeros((breadth, channels), BF16)
    for index, shifted in enumerate((before, field, after)):
        lanes = slice(index * channels, (index + 1) * channels)
        windows_ref[0:breadth, lanes] = edge
        windows_ref[breadth : breadth + pixels, lanes] = shifted.astype(BF16)
        windows_ref[breadth + pixels : 2 * breadth + pixels, lanes] = edge


def convolve(windows_ref, weight_ref, pixels, breadth):
    outputs = weight_ref.shape[2]
    channels = windows_ref.shape[1] // 3
    total = None
    for row in range(3):
        part = jnp.dot(
            windows_ref[row * breadth : row * breadth + pixels, :],
            weight_ref[3 * row : 3 * row + 3, 0:channels, :].reshape(3 * channels, outputs),
            preferred_element_type=F32,
        )
        total = part if total is None else total + part
    return total


def convolve_loop(total_ref, windows_ref, weight_ref, first, pixels, breadth):
    outputs = weight_ref.shape[2]
    channels = windows_ref.shape[1] // 3
    total_ref[...] = jnp.zeros((pixels, outputs), F32)

    def one_row(row, carry):
        start = pl.multiple_of(row * breadth, breadth)
        total_ref[...] += jnp.dot(
            windows_ref[pl.ds(start, pixels), :],
            weight_ref[pl.ds(3 * row, 3), first : first + channels, :].reshape(
                3 * channels, outputs
            ),
            preferred_element_type=F32,
        )
        return carry

    lax.fori_loop(0, 3, one_row, 0)


def chosen(index, values):
    result = jnp.int32(values[0])
    for position, value in enumerate(values):
        if value != values[0]:
            result = jnp.where(index == position, value, result)
    return result


def local_input(op, section, sections):
    return (op in (ENC_FWD, DEC_BWD) and section == 0) or (
        op in (DEC_FWD, ENC_BWD) and section == sections - 1
    )


def local_result(op, section, sections):
    return (
        op == ENC_FWD
        or (op == DEC_FWD and section == 0)
        or (op == DEC_BWD and section == sections - 1)
    )


KINDS = ("enc", "dec", "skip")


def touched(work, aside):
    ops = {op for op, _ in work.values()}
    names = ["kept", "side"]
    if aside:
        if ENC_FWD in ops:
            names += ["normed_skip", "scale_skip", "acts_enc", "turned_enc", "turned_skip"]
        if DEC_BWD in ops:
            names += ["normed_skip", "scale_skip", "cots_dec", "acts_dec", "turned_dec"]
    else:
        for op, kind in ((ENC_FWD, "enc"), (DEC_FWD, "dec")):
            if op in ops:
                names += ["normed_" + kind, "scale_" + kind, "acts_" + kind]
        for op, kind in ((ENC_BWD, "enc"), (DEC_BWD, "dec")):
            if op in ops:
                names += ["normed_" + kind, "scale_" + kind, "cots_" + kind]
    return list(dict.fromkeys(names))


def stage_kernel(work, aside, sections, breadth, factor, refs):
    pixels, channels = refs["kept"].shape[1:]
    section = lax.axis_index("section")
    jobs = [work.get(s, (0, 0)) for s in range(sections)]
    ops = {op for op, _ in jobs}
    op = chosen(section, [job[0] for job in jobs])
    slot = chosen(section, [job[1] for job in jobs])
    to_here = chosen(
        section, [int(local_result(job[0], s, sections)) for s, job in enumerate(jobs)]
    )
    lanes = pl.ds(pl.multiple_of(slot * pixels, 128), pixels)
    kept, side = refs["kept"], refs["side"]
    group_size = channels // GROUPS

    def per_kind(kind):
        which = 0 if kind == "enc" else 1
        inverse_count = 1.0 / (pixels * group_size * (1 + which))
        modulation = refs["modulation"][KINDS.index(kind), slot]
        return refs["members"].at[which], inverse_count, modulation

    def load_input():
        leaving = refs["leaving"]
        cases = {}
        for s, (job_op, _) in enumerate(jobs):
            if job_op:
                local = local_input(job_op, s, sections)
                case = "noisy" if local and job_op == ENC_FWD else "kept" if local else "arriving"
                cases.setdefault(case, []).append(s)

        def fill(case):
            if case == "noisy":
                leaving[...] = refs["levels"][0, slot] * refs["clean"][slot].astype(F32) + refs[
                    "levels"
                ][1, slot] * refs["noise"][slot].astype(F32)
            elif case == "kept":
                leaving[...] = kept[slot]
            else:
                leaving[...] = refs["arriving"][...]

        for case, places in cases.items():
            here = functools.reduce(jnp.logical_or, [section == s for s in places])
            pl.when(here)(functools.partial(fill, case))
        return leaving[...]

    def forward(kind):
        members, inverse_count, modulation = per_kind(kind)
        windows = refs["windows"]
        x = kept[slot] if aside else load_input()
        total = jnp.sum(x, axis=0, keepdims=True)
        own_mean = total * (1.0 / pixels)
        own_dev = x - own_mean
        own_square = jnp.sum(own_dev * own_dev, axis=0, keepdims=True)
        (group_total,) = group_sums([total], members[...])
        mean = group_total * inverse_count
        apart = own_mean - mean
        (group_square,) = group_sums([own_square + pixels * (apart * apart)], members[...])
        inverse_std = lax.rsqrt(group_square * inverse_count + 1e-05)
        unit = (x - mean) * inverse_std
        value = unit * modulation
        active = value / (1.0 + jnp.exp(-value))
        refs["normed_" + kind][slot] = unit
        refs["scale_" + kind][slot] = inverse_std
        spread_columns(active, breadth, windows)
        if aside:
            convolve_loop(side.at[slot], windows, refs["dec_weight"], channels, pixels, breadth)
            refs["turned_enc"][:, lanes] = refs["acts_enc"][slot].astype(F32).T.astype(BF16)
            refs["turned_skip"][:, lanes] = active.T.astype(BF16)
            return
        refs["acts_" + kind][slot] = active.astype(BF16)
        leaving = refs["leaving"]
        if kind == "enc":
            leaving[...] += convolve(windows, refs["enc_weight"], pixels, breadth)
        else:
            own = convolve(windows, refs["dec_weight"], pixels, breadth)
            leaving[...] += own + side[slot]

            @pl.when(to_here == 1)
            def _():
                leaving[...] = factor * (leaving[...] - refs["noise"][slot].astype(F32))

        keep_result()

    def keep_result():
        if any(local_result(job[0], s, sections) for s, job in enumerate(jobs)):

            @pl.when(to_here == 1)
            def _():
                kept[slot] = refs["leaving"][...]

    def backward(kind):
        members, inverse_count, modulation = per_kind(kind)
        if aside:
            given = refs["cots_dec"].at[slot]
            refs["turned_dec"][:, lanes] = refs["acts_dec"][slot].astype(F32).T.astype(BF16)
        else:
            given = refs["cots_" + kind].at[slot]
            leaving = refs["leaving"]
            load_input()
            if kind == "enc":
                leaving[...] = leaving[...] + side[slot]
            spread_columns(leaving[...], breadth, given)
        if aside:
            convolve_loop(refs["down"], given, refs["flipped_skip"], 0, pixels, breadth)
            down = refs["down"][...]
        else:
            down = convolve(given, refs["flipped_" + kind], pixels, breadth)
        unit = refs["normed_" + kind][slot]
        value = unit * modulation
        gate = 1.0 / (1.0 + jnp.exp(-value))
        slope = gate * (1.0 + value * (1.0 - gate))
        d_unit = down * slope * modulation
        sums = group_sums(
            [
                jnp.sum(d_unit, axis=0, keepdims=True),
                jnp.sum(d_unit * unit, axis=0, keepdims=True),
            ],
            members[...],
        )
        shift, stretch = sums[0] * inverse_count, sums[1] * inverse_count
        result = refs["scale_" + kind][slot] * (d_unit - shift - unit * stretch)
        if aside:
            side[slot] = result
        else:
            leaving[...] = leaving[...] + result
            keep_result()

    if aside:
        parts = ((ENC_FWD, forward, "skip"), (DEC_BWD, backward, "skip"))
    else:
        parts = (
            (ENC_FWD, forward, "enc"),
            (DEC_FWD, forward, "dec"),
            (DEC_BWD, backward, "dec"),
            (ENC_BWD, backward, "enc"),
        )
    for part_op, part, kind in parts:
        if part_op in ops:
            pl.when(op == part_op)(functools.partial(part, kind))


def call_stage(work, aside, sections, breadth, factor, arriving, consts, state):
    ops = {op for op, _ in work.values()}
    _, pixels, channels = state["kept"].shape
    vmem = pl.BlockSpec(memory_space=pltpu.VMEM)
    names = ["modulation", "members"]
    if ENC_FWD in ops and not aside:
        names.append("enc_weight")
    if (DEC_FWD in ops and not aside) or (ENC_FWD in ops and aside):
        names.append("dec_weight")
    if DEC_BWD in ops:
        names.append("flipped_skip" if aside else "flipped_dec")
    if ENC_BWD in ops and not aside:
        names.append("flipped_enc")
    starting = not aside and work.get(0, (0, 0))[0] == ENC_FWD
    if starting:
        names += ["levels", "clean"]
    if starting or (DEC_FWD in ops and not aside):
        names.append("noise")
    given = {name: consts[name] for name in names}
    if not aside and any(not local_input(op, s, sections) for s, (op, _) in work.items()):
        given["arriving"] = arriving
    used = touched(work, aside)
    present = [n for n in used if not isinstance(state[n], jax.ShapeDtypeStruct)]
    out_shape = {} if aside else {"leaving": jax.ShapeDtypeStruct((pixels, channels), F32)}
    for name in used:
        out_shape[name] = jax.ShapeDtypeStruct(state[name].shape, state[name].dtype)
    out_names = list(out_shape)

    def kernel(*refs):
        named = dict(zip(given, refs))
        named.update(zip(out_names, refs[len(given) + len(present) :]))
        named["windows"], named["down"] = refs[-2:]
        stage_kernel(work, aside, sections, breadth, factor, named)

    outs = pl.pallas_call(
        kernel,
        out_shape=list(out_shape.values()),
        in_specs=[vmem] * (len(given) + len(present)),
        out_specs=[vmem] * len(out_shape),
        scratch_shapes=[
            pltpu.VMEM((pixels + 2 * breadth, 3 * channels), BF16),
            pltpu.VMEM((pixels, channels), F32),
        ],
        input_output_aliases={
            len(given) + i: out_names.index(name) for i, name in enumerate(present)
        },
        compiler_params=pltpu.CompilerParams(vmem_limit_bytes=STAGE_VMEM),
        cost_estimate=pl.CostEstimate(flops=1000, bytes_accessed=1000, transcendentals=0),
    )(*given.values(), *[state[n] for n in present])
    named = dict(zip(out_names, outs))
    leaving = named.pop("leaving", None)
    return leaving, {**state, **named}


def flip_kernel(enc_weight, dec_weight, after, *outs):
    taps, channels, _ = enc_weight.shape

    def one_tap(tap, carry):
        tiles = (
            enc_weight[tap],
            dec_weight[tap, 0:channels, :],
            dec_weight[tap, channels : 2 * channels, :],
        )
        for tile, out in zip(tiles, outs):
            out[taps - 1 - tap] = tile.astype(F32).T.astype(BF16)
        return carry

    lax.fori_loop(0, taps, one_tap, 0)


def flip(enc_weight, dec_weight, after):
    vmem = pl.BlockSpec(memory_space=pltpu.VMEM)
    return pl.pallas_call(
        flip_kernel,
        out_shape=[jax.ShapeDtypeStruct(enc_weight.shape, BF16)] * 3,
        in_specs=[vmem] * 3,
        out_specs=[vmem] * 3,
        compiler_params=pltpu.CompilerParams(vmem_limit_bytes=STAGE_VMEM),
    )(enc_weight, dec_weight, after)


def weight_grad_kernel(breadth, halves, group, chunks, *refs):
    turned, cots, outs, (ready, sems) = refs[:halves], refs[halves], refs[-4:-2], refs[-2:]
    channels = turned[0].shape[0]
    samples = cots.shape[0]
    pixels = turned[0].shape[1] // samples
    core = lax.axis_index("dp") % 2
    rows = halves * channels // chunks // 2
    places = [divmod(2 * chunk * rows, channels) for chunk in group]

    def store(tap, slot):
        return [
            pltpu.make_async_copy(ready.at[slot, i], outs[i].at[:, tap], sems.at[slot, i])
            for i in range(2)
        ]

    def one_tap(tap, carry):
        slot = lax.rem(tap, 2)
        row, col = tap // 3, lax.rem(tap, 3)
        start = pl.multiple_of((2 - row) * breadth, breadth)
        lane = pl.multiple_of((2 - col) * channels, 128)
        lines = [turned[half][first : first + 2 * rows, :] for half, first in places]
        fields = [
            cots[sample, pl.ds(start, pixels), pl.ds(lane, channels)] for sample in range(samples)
        ]
        total = jnp.dot(
            jnp.concatenate(lines, axis=0),
            jnp.concatenate(fields, axis=0),
            preferred_element_type=F32,
        )

        @pl.when(tap >= 2)
        def _():
            for one in store(tap, slot):
                one.wait()

        pieces = total.reshape(len(group), 2, rows, channels)
        ready[slot, 0] = jnp.where(core == 0, pieces[:, 0], pieces[:, 1])
        ready[slot, 1] = jnp.where(core == 0, pieces[:, 1], pieces[:, 0])
        for one in store(tap, slot):
            one.start()
        return carry

    lax.fori_loop(0, 9, one_tap, 0)
    for tap in (7, 8):
        for one in store(tap, tap % 2):
            one.wait()


def weight_grad(turned, cots, group, breadth):
    channels = turned[0].shape[0]
    chunks = lax.axis_size("dp") // 2
    rows = len(turned) * channels // chunks // 2
    vmem = pl.BlockSpec(memory_space=pltpu.VMEM)
    hbm = pl.BlockSpec(memory_space=pltpu.HBM)
    shape = jax.ShapeDtypeStruct((len(group), 9, rows, channels), F32)
    return pl.pallas_call(
        functools.partial(weight_grad_kernel, breadth, len(turned), tuple(group), chunks),
        out_shape=[shape, shape],
        in_specs=[vmem] * (len(turned) + 1),
        out_specs=[hbm, hbm],
        scratch_shapes=[
            pltpu.VMEM((2, 2, len(group), rows, channels), F32),
            pltpu.SemaphoreType.DMA((2, 2)),
        ],
        compiler_params=pltpu.CompilerParams(vmem_limit_bytes=GRAD_VMEM),
        cost_estimate=pl.CostEstimate(flops=1000, bytes_accessed=1000, transcendentals=0),
    )(*turned, cots)


def member_matrices(channels):
    channel = np.arange(channels)
    size = channels // GROUPS
    return np.stack(
        [channel[:, None] // n == channel[None, :] // n for n in (size, 2 * size)]
    ).astype(ml_dtypes.bfloat16)


class LineSum:
    def __init__(self, make):
        self.count = lax.axis_size("dp")
        self.chips = self.count // 2
        self.steps = self.chips - 1
        self.place = lax.axis_index("dp") // 2
        self.arrived = None
        self.ends = self.swap(*make([0, self.chips - 1]))
        middle = list(range(1, self.chips - 1))
        self.middle = self.swap(*make(middle)) if middle else None

    def swap(self, kept, given):
        moves = [(d, d + 1 - 2 * (d % 2)) for d in range(self.count)]
        return kept, lax.ppermute(given, "dp", moves)

    def end(self, index):
        kept, swapped = self.ends
        return kept[index] + swapped[index]

    def between(self, chunk):
        index = jnp.clip(chunk - 1, 0, self.chips - 3)
        return sum(lax.dynamic_index_in_dim(part, index, 0, False) for part in self.middle)

    def own_pair(self, step):
        up, down = self.end(1), self.end(0)
        if step:
            back = self.chips - 1 - self.place
            up = jnp.where(self.place == step, up, self.between(back - step + 2 * self.place))
            down = jnp.where(back == step, down, self.between(step - back))
        return up, down

    def prepare(self, step):
        up, down = self.own_pair(step)
        if step:
            up, down = up + self.arrived[0], down + self.arrived[1]
        return up, down

    def send(self, step, pair):
        last = self.chips - 1
        moves = [(z, c) for z in range(min(step + 1, last)) for c in range(2)]
        up = lax.ppermute(pair[0], "dp", [(2 * z + c, 2 * z + 2 + c) for z, c in moves])
        down = lax.ppermute(
            pair[1], "dp", [(2 * (last - z) + c, 2 * (last - z) - 2 + c) for z, c in moves]
        )
        self.arrived = lax.optimization_barrier((up, down))

    def result(self):
        total = jnp.where(self.place == 0, self.end(0), self.end(1))
        if self.middle is not None:
            outer = jnp.logical_or(self.place == 0, self.place == self.chips - 1)
            total = jnp.where(outer, total, self.between(self.place))
        return total + self.arrived[0] + self.arrived[1]


def shards(clean, noise, stamps, enc_weight, dec_weight):
    sections = lax.axis_size("section")
    samples, height, breadth, channels = clean.shape
    pixels = height * breadth
    factor = 1.0 / math.sqrt(samples * lax.axis_size("dp") * pixels)
    ticks = make_schedule(sections, samples)

    levels = jnp.stack(noise_levels(stamps))
    wide = embed(stamps, 2 * channels)
    modulation = 1.0 + 0.5 * jnp.stack(
        [embed(stamps, channels), wide[:, :channels], wide[:, channels:]]
    )
    consts = {
        "modulation": modulation[:, :, None, :],
        "members": jnp.asarray(member_matrices(channels)),
        "enc_weight": enc_weight.reshape(9, channels, channels),
        "dec_weight": dec_weight.reshape(9, 2 * channels, channels),
        "levels": jnp.broadcast_to(levels[:, :, None, None], (2, samples, 1, channels)),
        "clean": clean.reshape(samples, pixels, channels),
        "noise": noise.reshape(samples, pixels, channels),
    }
    weights = (consts["enc_weight"], consts["dec_weight"])
    fresh = jax.ShapeDtypeStruct
    field = (samples, pixels, channels)
    state = {"kept": fresh(field, F32), "side": fresh(field, F32)}
    for kind in KINDS:
        state["normed_" + kind] = fresh(field, F32)
        state["scale_" + kind] = fresh((samples, 1, channels), F32)
        state["turned_" + kind] = fresh((channels, samples * pixels), BF16)
        if kind != "skip":
            state["acts_" + kind] = fresh(field, BF16)
            state["cots_" + kind] = fresh(
                (samples, pixels + 2 * breadth, 3 * channels), BF16
            )
    arriving = None
    last_dec = max(
        tick for tick, (work, _) in enumerate(ticks) if any(w[0] == DEC_BWD for w in work.values())
    )
    flip_tick = min(
        tick for tick, (work, _) in enumerate(ticks) if any(w[0] == DEC_BWD for w in work.values())
    ) - 2
    dec_sum = None
    dec_step = 0

    def gradient(kinds, cots):
        turned = [state["turned_" + kind] for kind in kinds]
        return LineSum(lambda group: weight_grad(turned, state[cots], group, breadth))

    def ahead_of(name, value):
        state[name], value = lax.optimization_barrier((state[name], value))
        return value

    for tick, (work, moves) in enumerate(ticks):
        ops = {op for op, _ in work.values()}
        leaving, state = call_stage(
            work, False, sections, breadth, factor, arriving, consts, state
        )
        if moves:
            arriving = lax.ppermute(leaving, "section", moves)
        if ops & {ENC_FWD, DEC_BWD}:
            _, state = call_stage(work, True, sections, breadth, factor, None, consts, state)
        if tick == flip_tick:
            flipped = flip(*weights, state["scale_skip"])
            consts.update(zip(["flipped_" + kind for kind in KINDS], flipped))
        if tick == last_dec:
            dec_sum = gradient(("dec", "skip"), "cots_dec")
        if dec_sum is not None and dec_step < dec_sum.steps and tick < len(ticks) - 1:
            if tick - last_dec == 3 * dec_step // 2:
                if dec_step:
                    dec_sum.arrived, arriving = lax.optimization_barrier(
                        (dec_sum.arrived, arriving)
                    )
                dec_sum.send(dec_step, ahead_of("side", dec_sum.prepare(dec_step)))
                dec_step += 1
    enc_sum = gradient(("enc",), "cots_enc")
    for step in range(dec_step, dec_sum.steps):
        dec_sum.send(step, dec_sum.prepare(step))
    for step in range(enc_sum.steps):
        pair = enc_sum.prepare(step)
        if step == 0:
            pair, dec_sum.arrived = lax.optimization_barrier((pair, dec_sum.arrived))
        enc_sum.send(step, pair)
    enc_share, dec_share = enc_sum.result(), dec_sum.result()
    return tuple(
        share.reshape((1, 3, 3) + share.shape[1:]) for share in (enc_share, dec_share)
    )


def solution(mesh):
    placed = (
        P("dp", None, None, None),
        P("dp", None, None, None),
        P("dp"),
        P("section", None, None, None, None),
        P("section", None, None, None, None),
    )
    return jax.shard_map(
        shards,
        mesh=mesh,
        in_specs=placed,
        out_specs=(P("section", None, None, "dp", None), P("section", None, None, "dp", None)),
        check_vma=False,
    )
```

```python
import functools
import math

import jax
import jax.numpy as jnp
import ml_dtypes
import numpy as np
from jax import lax
from jax.experimental import pallas as pl
from jax.experimental.pallas import tpu as pltpu
from jax.sharding import PartitionSpec as P

GROUPS = 32
F32 = jnp.float32
BF16 = jnp.bfloat16
ENC_FWD, DEC_FWD, DEC_BWD, ENC_BWD = 1, 2, 3, 4
STAGE_VMEM = 3 * 1024 * 1024
GRAD_VMEM = 8 * 1024 * 1024


def embed(stamps_in, channels):
    half_width = channels // 2
    frequency = jnp.exp(-math.log(10000.0) * jnp.arange(half_width, dtype=jnp.float32) / half_width)
    angles = stamps_in.astype(jnp.float32)[:, None] * frequency[None, :]
    return jnp.concatenate([jnp.sin(angles), jnp.cos(angles)], axis=1)


def noise_levels(stamps_in):
    phase = (stamps_in.astype(jnp.float32) / 1000.0 + 0.008) / 1.008 * (math.pi / 2.0)
    signal = jnp.cos(phase) ** 2
    return (jnp.sqrt(signal), jnp.sqrt(1.0 - signal))


def stage_of(position, sections):
    lap, step = divmod(position, sections)
    section = step if lap % 2 == 0 else sections - 1 - step
    return section, lap + 1


def make_schedule(sections, samples):
    stages = 4 * sections
    ticks = []
    for tick in range(stages + 2 * (samples - 1)):
        work, moves = {}, []
        for sample in range(samples):
            position = tick - 2 * sample
            if not 0 <= position < stages:
                continue
            section, op = stage_of(position, sections)
            assert section not in work
            work[section] = (op, sample)
            if position + 1 < stages:
                target, _ = stage_of(position + 1, sections)
                if target != section:
                    moves.append((section, target))
        ticks.append((work, moves))
    return ticks


def group_sums(vectors, members):
    channels = vectors[0].shape[1]
    row = lax.broadcasted_iota(jnp.int32, (16, channels), 0)
    stacked = jnp.zeros((16, channels), F32)
    for index, vector in enumerate(vectors):
        high = vector.astype(BF16).astype(F32)
        rest = vector - high
        middle = rest.astype(BF16).astype(F32)
        for part_index, part in enumerate((high, middle, rest - middle)):
            stacked = jnp.where(row == 3 * index + part_index, part, stacked)
    summed = jnp.dot(stacked.astype(BF16), members, preferred_element_type=F32)
    return [
        summed[3 * i : 3 * i + 1] + summed[3 * i + 1 : 3 * i + 2] + summed[3 * i + 2 : 3 * i + 3]
        for i in range(len(vectors))
    ]


def spread_columns(field, breadth, windows_ref):
    pixels, channels = field.shape
    column = lax.broadcasted_iota(jnp.int32, (pixels, channels), 0) & (breadth - 1)
    before = jnp.where(column == 0, 0.0, pltpu.roll(field, 1, 0))
    after = jnp.where(column == breadth - 1, 0.0, pltpu.roll(field, pixels - 1, 0))
    edge = jnp.zeros((breadth, channels), BF16)
    for index, shifted in enumerate((before, field, after)):
        lanes = slice(index * channels, (index + 1) * channels)
        windows_ref[0:breadth, lanes] = edge
        windows_ref[breadth : breadth + pixels, lanes] = shifted.astype(BF16)
        windows_ref[breadth + pixels : 2 * breadth + pixels, lanes] = edge


def convolve(windows_ref, weight_ref, pixels, breadth):
    outputs = weight_ref.shape[2]
    channels = windows_ref.shape[1] // 3
    total = None
    for row in range(3):
        part = jnp.dot(
            windows_ref[row * breadth : row * breadth + pixels, :],
            weight_ref[3 * row : 3 * row + 3, 0:channels, :].reshape(3 * channels, outputs),
            preferred_element_type=F32,
        )
        total = part if total is None else total + part
    return total


def convolve_loop(total_ref, windows_ref, weight_ref, first, pixels, breadth):
    outputs = weight_ref.shape[2]
    channels = windows_ref.shape[1] // 3
    total_ref[...] = jnp.zeros((pixels, outputs), F32)

    def one_row(row, carry):
        start = pl.multiple_of(row * breadth, breadth)
        total_ref[...] += jnp.dot(
            windows_ref[pl.ds(start, pixels), :],
            weight_ref[pl.ds(3 * row, 3), first : first + channels, :].reshape(
                3 * channels, outputs
            ),
            preferred_element_type=F32,
        )
        return carry

    lax.fori_loop(0, 3, one_row, 0)


def chosen(index, values):
    result = jnp.int32(values[0])
    for position, value in enumerate(values):
        if value != values[0]:
            result = jnp.where(index == position, value, result)
    return result


def local_input(op, section, sections):
    return (op in (ENC_FWD, DEC_BWD) and section == 0) or (
        op in (DEC_FWD, ENC_BWD) and section == sections - 1
    )


def local_result(op, section, sections):
    return (
        op == ENC_FWD
        or (op == DEC_FWD and section == 0)
        or (op == DEC_BWD and section == sections - 1)
    )


KINDS = ("enc", "dec", "skip")


def touched(work, aside):
    ops = {op for op, _ in work.values()}
    names = ["kept", "side"]
    if aside:
        if ENC_FWD in ops:
            names += ["normed_skip", "scale_skip", "acts_enc", "turned_enc", "turned_skip"]
        if DEC_BWD in ops:
            names += ["normed_skip", "scale_skip", "cots_dec", "acts_dec", "turned_dec"]
    else:
        for op, kind in ((ENC_FWD, "enc"), (DEC_FWD, "dec")):
            if op in ops:
                names += ["normed_" + kind, "scale_" + kind, "acts_" + kind]
        for op, kind in ((ENC_BWD, "enc"), (DEC_BWD, "dec")):
            if op in ops:
                names += ["normed_" + kind, "scale_" + kind, "cots_" + kind]
    return list(dict.fromkeys(names))


def stage_kernel(work, aside, sections, breadth, factor, refs):
    pixels, channels = refs["kept"].shape[1:]
    section = lax.axis_index("section")
    jobs = [work.get(s, (0, 0)) for s in range(sections)]
    ops = {op for op, _ in jobs}
    op = chosen(section, [job[0] for job in jobs])
    slot = chosen(section, [job[1] for job in jobs])
    to_here = chosen(
        section, [int(local_result(job[0], s, sections)) for s, job in enumerate(jobs)]
    )
    lanes = pl.ds(pl.multiple_of(slot * pixels, 128), pixels)
    kept, side = refs["kept"], refs["side"]
    group_size = channels // GROUPS

    def per_kind(kind):
        which = 0 if kind == "enc" else 1
        inverse_count = 1.0 / (pixels * group_size * (1 + which))
        modulation = refs["modulation"][KINDS.index(kind), slot]
        return refs["members"].at[which], inverse_count, modulation

    def load_input():
        leaving = refs["leaving"]
        cases = {}
        for s, (job_op, _) in enumerate(jobs):
            if job_op:
                local = local_input(job_op, s, sections)
                case = "noisy" if local and job_op == ENC_FWD else "kept" if local else "arriving"
                cases.setdefault(case, []).append(s)

        def fill(case):
            if case == "noisy":
                leaving[...] = refs["levels"][0, slot] * refs["clean"][slot].astype(F32) + refs[
                    "levels"
                ][1, slot] * refs["noise"][slot].astype(F32)
            elif case == "kept":
                leaving[...] = kept[slot]
            else:
                leaving[...] = refs["arriving"][...]

        for case, places in cases.items():
            here = functools.reduce(jnp.logical_or, [section == s for s in places])
            pl.when(here)(functools.partial(fill, case))
        return leaving[...]

    def forward(kind):
        members, inverse_count, modulation = per_kind(kind)
        windows = refs["windows"]
        x = kept[slot] if aside else load_input()
        total = jnp.sum(x, axis=0, keepdims=True)
        own_mean = total * (1.0 / pixels)
        own_dev = x - own_mean
        own_square = jnp.sum(own_dev * own_dev, axis=0, keepdims=True)
        (group_total,) = group_sums([total], members[...])
        mean = group_total * inverse_count
        apart = own_mean - mean
        (group_square,) = group_sums([own_square + pixels * (apart * apart)], members[...])
        inverse_std = lax.rsqrt(group_square * inverse_count + 1e-05)
        unit = (x - mean) * inverse_std
        value = unit * modulation
        active = value / (1.0 + jnp.exp(-value))
        refs["normed_" + kind][slot] = unit
        refs["scale_" + kind][slot] = inverse_std
        spread_columns(active, breadth, windows)
        if aside:
            convolve_loop(side.at[slot], windows, refs["dec_weight"], channels, pixels, breadth)
            refs["turned_enc"][:, lanes] = refs["acts_enc"][slot].astype(F32).T.astype(BF16)
            refs["turned_skip"][:, lanes] = active.T.astype(BF16)
            return
        refs["acts_" + kind][slot] = active.astype(BF16)
        leaving = refs["leaving"]
        if kind == "enc":
            leaving[...] += convolve(windows, refs["enc_weight"], pixels, breadth)
        else:
            own = convolve(windows, refs["dec_weight"], pixels, breadth)
            leaving[...] += own + side[slot]

            @pl.when(to_here == 1)
            def _():
                leaving[...] = factor * (leaving[...] - refs["noise"][slot].astype(F32))

        keep_result()

    def keep_result():
        if any(local_result(job[0], s, sections) for s, job in enumerate(jobs)):

            @pl.when(to_here == 1)
            def _():
                kept[slot] = refs["leaving"][...]

    def backward(kind):
        members, inverse_count, modulation = per_kind(kind)
        if aside:
            given = refs["cots_dec"].at[slot]
            refs["turned_dec"][:, lanes] = refs["acts_dec"][slot].astype(F32).T.astype(BF16)
        else:
            given = refs["cots_" + kind].at[slot]
            leaving = refs["leaving"]
            load_input()
            if kind == "enc":
                leaving[...] = leaving[...] + side[slot]
            spread_columns(leaving[...], breadth, given)
        if aside:
            convolve_loop(refs["down"], given, refs["flipped_skip"], 0, pixels, breadth)
            down = refs["down"][...]
        else:
            down = convolve(given, refs["flipped_" + kind], pixels, breadth)
        unit = refs["normed_" + kind][slot]
        value = unit * modulation
        gate = 1.0 / (1.0 + jnp.exp(-value))
        slope = gate * (1.0 + value * (1.0 - gate))
        d_unit = down * slope * modulation
        sums = group_sums(
            [
                jnp.sum(d_unit, axis=0, keepdims=True),
                jnp.sum(d_unit * unit, axis=0, keepdims=True),
            ],
            members[...],
        )
        shift, stretch = sums[0] * inverse_count, sums[1] * inverse_count
        result = refs["scale_" + kind][slot] * (d_unit - shift - unit * stretch)
        if aside:
            side[slot] = result
        else:
            leaving[...] = leaving[...] + result
            keep_result()

    if aside:
        parts = ((ENC_FWD, forward, "skip"), (DEC_BWD, backward, "skip"))
    else:
        parts = (
            (ENC_FWD, forward, "enc"),
            (DEC_FWD, forward, "dec"),
            (DEC_BWD, backward, "dec"),
            (ENC_BWD, backward, "enc"),
        )
    for part_op, part, kind in parts:
        if part_op in ops:
            pl.when(op == part_op)(functools.partial(part, kind))


def call_stage(work, aside, sections, breadth, factor, arriving, consts, state):
    ops = {op for op, _ in work.values()}
    _, pixels, channels = state["kept"].shape
    vmem = pl.BlockSpec(memory_space=pltpu.VMEM)
    names = ["modulation", "members"]
    if ENC_FWD in ops and not aside:
        names.append("enc_weight")
    if (DEC_FWD in ops and not aside) or (ENC_FWD in ops and aside):
        names.append("dec_weight")
    if DEC_BWD in ops:
        names.append("flipped_skip" if aside else "flipped_dec")
    if ENC_BWD in ops and not aside:
        names.append("flipped_enc")
    starting = not aside and work.get(0, (0, 0))[0] == ENC_FWD
    if starting:
        names += ["levels", "clean"]
    if starting or (DEC_FWD in ops and not aside):
        names.append("noise")
    given = {name: consts[name] for name in names}
    if not aside and any(not local_input(op, s, sections) for s, (op, _) in work.items()):
        given["arriving"] = arriving
    used = touched(work, aside)
    present = [n for n in used if not isinstance(state[n], jax.ShapeDtypeStruct)]
    out_shape = {} if aside else {"leaving": jax.ShapeDtypeStruct((pixels, channels), F32)}
    for name in used:
        out_shape[name] = jax.ShapeDtypeStruct(state[name].shape, state[name].dtype)
    out_names = list(out_shape)

    def kernel(*refs):
        named = dict(zip(given, refs))
        named.update(zip(out_names, refs[len(given) + len(present) :]))
        named["windows"], named["down"] = refs[-2:]
        stage_kernel(work, aside, sections, breadth, factor, named)

    outs = pl.pallas_call(
        kernel,
        out_shape=list(out_shape.values()),
        in_specs=[vmem] * (len(given) + len(present)),
        out_specs=[vmem] * len(out_shape),
        scratch_shapes=[
            pltpu.VMEM((pixels + 2 * breadth, 3 * channels), BF16),
            pltpu.VMEM((pixels, channels), F32),
        ],
        input_output_aliases={
            len(given) + i: out_names.index(name) for i, name in enumerate(present)
        },
        compiler_params=pltpu.CompilerParams(vmem_limit_bytes=STAGE_VMEM),
        cost_estimate=pl.CostEstimate(flops=1000, bytes_accessed=1000, transcendentals=0),
    )(*given.values(), *[state[n] for n in present])
    named = dict(zip(out_names, outs))
    leaving = named.pop("leaving", None)
    return leaving, {**state, **named}


def flip_kernel(enc_weight, dec_weight, after, *outs):
    taps, channels, _ = enc_weight.shape

    def one_tap(tap, carry):
        tiles = (
            enc_weight[tap],
            dec_weight[tap, 0:channels, :],
            dec_weight[tap, channels : 2 * channels, :],
        )
        for tile, out in zip(tiles, outs):
            out[taps - 1 - tap] = tile.astype(F32).T.astype(BF16)
        return carry

    lax.fori_loop(0, taps, one_tap, 0)


def flip(enc_weight, dec_weight, after):
    vmem = pl.BlockSpec(memory_space=pltpu.VMEM)
    return pl.pallas_call(
        flip_kernel,
        out_shape=[jax.ShapeDtypeStruct(enc_weight.shape, BF16)] * 3,
        in_specs=[vmem] * 3,
        out_specs=[vmem] * 3,
        compiler_params=pltpu.CompilerParams(vmem_limit_bytes=STAGE_VMEM),
    )(enc_weight, dec_weight, after)


def weight_grad_kernel(breadth, halves, group, chunks, *refs):
    turned, cots, outs, (ready, sems) = refs[:halves], refs[halves], refs[-4:-2], refs[-2:]
    channels = turned[0].shape[0]
    samples = cots.shape[0]
    pixels = turned[0].shape[1] // samples
    core = lax.axis_index("dp") % 2
    rows = halves * channels // chunks // 2
    places = [divmod(2 * chunk * rows, channels) for chunk in group]

    def store(tap, slot):
        return [
            pltpu.make_async_copy(ready.at[slot, i], outs[i].at[:, tap], sems.at[slot, i])
            for i in range(2)
        ]

    def one_tap(tap, carry):
        slot = lax.rem(tap, 2)
        row, col = tap // 3, lax.rem(tap, 3)
        start = pl.multiple_of((2 - row) * breadth, breadth)
        lane = pl.multiple_of((2 - col) * channels, 128)
        lines = [turned[half][first : first + 2 * rows, :] for half, first in places]
        fields = [
            cots[sample, pl.ds(start, pixels), pl.ds(lane, channels)] for sample in range(samples)
        ]
        total = jnp.dot(
            jnp.concatenate(lines, axis=0),
            jnp.concatenate(fields, axis=0),
            preferred_element_type=F32,
        )

        @pl.when(tap >= 2)
        def _():
            for one in store(tap, slot):
                one.wait()

        pieces = total.reshape(len(group), 2, rows, channels)
        ready[slot, 0] = jnp.where(core == 0, pieces[:, 0], pieces[:, 1])
        ready[slot, 1] = jnp.where(core == 0, pieces[:, 1], pieces[:, 0])
        for one in store(tap, slot):
            one.start()
        return carry

    lax.fori_loop(0, 9, one_tap, 0)
    for tap in (7, 8):
        for one in store(tap, tap % 2):
            one.wait()


def weight_grad(turned, cots, group, breadth):
    channels = turned[0].shape[0]
    chunks = lax.axis_size("dp") // 2
    rows = len(turned) * channels // chunks // 2
    vmem = pl.BlockSpec(memory_space=pltpu.VMEM)
    hbm = pl.BlockSpec(memory_space=pltpu.HBM)
    shape = jax.ShapeDtypeStruct((len(group), 9, rows, channels), F32)
    return pl.pallas_call(
        functools.partial(weight_grad_kernel, breadth, len(turned), tuple(group), chunks),
        out_shape=[shape, shape],
        in_specs=[vmem] * (len(turned) + 1),
        out_specs=[hbm, hbm],
        scratch_shapes=[
            pltpu.VMEM((2, 2, len(group), rows, channels), F32),
            pltpu.SemaphoreType.DMA((2, 2)),
        ],
        compiler_params=pltpu.CompilerParams(vmem_limit_bytes=GRAD_VMEM),
        cost_estimate=pl.CostEstimate(flops=1000, bytes_accessed=1000, transcendentals=0),
    )(*turned, cots)


def member_matrices(channels):
    channel = np.arange(channels)
    size = channels // GROUPS
    return np.stack(
        [channel[:, None] // n == channel[None, :] // n for n in (size, 2 * size)]
    ).astype(ml_dtypes.bfloat16)


class LineSum:
    def __init__(self, make):
        self.count = lax.axis_size("dp")
        self.chips = self.count // 2
        self.steps = self.chips - 1
        self.place = lax.axis_index("dp") // 2
        self.arrived = None
        self.ends = self.swap(*make([0, self.chips - 1]))
        middle = list(range(1, self.chips - 1))
        self.middle = self.swap(*make(middle)) if middle else None

    def swap(self, kept, given):
        moves = [(d, d + 1 - 2 * (d % 2)) for d in range(self.count)]
        return kept, lax.ppermute(given, "dp", moves)

    def end(self, index):
        kept, swapped = self.ends
        return kept[index] + swapped[index]

    def between(self, chunk):
        index = jnp.clip(chunk - 1, 0, self.chips - 3)
        return sum(lax.dynamic_index_in_dim(part, index, 0, False) for part in self.middle)

    def own_pair(self, step):
        up, down = self.end(1), self.end(0)
        if step:
            back = self.chips - 1 - self.place
            up = jnp.where(self.place == step, up, self.between(back - step + 2 * self.place))
            down = jnp.where(back == step, down, self.between(step - back))
        return up, down

    def prepare(self, step):
        up, down = self.own_pair(step)
        if step:
            up, down = up + self.arrived[0], down + self.arrived[1]
        return up, down

    def send(self, step, pair):
        last = self.chips - 1
        moves = [(z, c) for z in range(min(step + 1, last)) for c in range(2)]
        up = lax.ppermute(pair[0], "dp", [(2 * z + c, 2 * z + 2 + c) for z, c in moves])
        down = lax.ppermute(
            pair[1], "dp", [(2 * (last - z) + c, 2 * (last - z) - 2 + c) for z, c in moves]
        )
        self.arrived = lax.optimization_barrier((up, down))

    def result(self):
        total = jnp.where(self.place == 0, self.end(0), self.end(1))
        if self.middle is not None:
            outer = jnp.logical_or(self.place == 0, self.place == self.chips - 1)
            total = jnp.where(outer, total, self.between(self.place))
        return total + self.arrived[0] + self.arrived[1]


def shards(clean, noise, stamps, enc_weight, dec_weight):
    sections = lax.axis_size("section")
    samples, height, breadth, channels = clean.shape
    pixels = height * breadth
    factor = 1.0 / math.sqrt(samples * lax.axis_size("dp") * pixels)
    ticks = make_schedule(sections, samples)

    levels = jnp.stack(noise_levels(stamps))
    wide = embed(stamps, 2 * channels)
    modulation = 1.0 + 0.5 * jnp.stack(
        [embed(stamps, channels), wide[:, :channels], wide[:, channels:]]
    )
    consts = {
        "modulation": modulation[:, :, None, :],
        "members": jnp.asarray(member_matrices(channels)),
        "enc_weight": enc_weight.reshape(9, channels, channels),
        "dec_weight": dec_weight.reshape(9, 2 * channels, channels),
        "levels": jnp.broadcast_to(levels[:, :, None, None], (2, samples, 1, channels)),
        "clean": clean.reshape(samples, pixels, channels),
        "noise": noise.reshape(samples, pixels, channels),
    }
    weights = (consts["enc_weight"], consts["dec_weight"])
    fresh = jax.ShapeDtypeStruct
    field = (samples, pixels, channels)
    state = {"kept": fresh(field, F32), "side": fresh(field, F32)}
    for kind in KINDS:
        state["normed_" + kind] = fresh(field, F32)
        state["scale_" + kind] = fresh((samples, 1, channels), F32)
        state["turned_" + kind] = fresh((channels, samples * pixels), BF16)
        if kind != "skip":
            state["acts_" + kind] = fresh(field, BF16)
            state["cots_" + kind] = fresh(
                (samples, pixels + 2 * breadth, 3 * channels), BF16
            )
    arriving = None
    last_dec = max(
        tick for tick, (work, _) in enumerate(ticks) if any(w[0] == DEC_BWD for w in work.values())
    )
    flip_tick = min(
        tick for tick, (work, _) in enumerate(ticks) if any(w[0] == DEC_BWD for w in work.values())
    ) - 2
    dec_sum = None
    dec_step = 0

    def gradient(kinds, cots):
        turned = [state["turned_" + kind] for kind in kinds]
        return LineSum(lambda group: weight_grad(turned, state[cots], group, breadth))

    def ahead_of(name, value):
        state[name], value = lax.optimization_barrier((state[name], value))
        return value

    for tick, (work, moves) in enumerate(ticks):
        ops = {op for op, _ in work.values()}
        leaving, state = call_stage(
            work, False, sections, breadth, factor, arriving, consts, state
        )
        if moves:
            arriving = lax.ppermute(leaving, "section", moves)
        if ops & {ENC_FWD, DEC_BWD}:
            _, state = call_stage(work, True, sections, breadth, factor, None, consts, state)
        if tick == flip_tick:
            flipped = flip(*weights, state["scale_skip"])
            consts.update(zip(["flipped_" + kind for kind in KINDS], flipped))
        if tick == last_dec:
            dec_sum = gradient(("dec", "skip"), "cots_dec")
        if dec_sum is not None and dec_step < dec_sum.steps and tick < len(ticks) - 1:
            if tick - last_dec == 3 * dec_step // 2:
                if dec_step == 1:
                    dec_sum.arrived, arriving = lax.optimization_barrier(
                        (dec_sum.arrived, arriving)
                    )
                dec_sum.send(dec_step, ahead_of("side", dec_sum.prepare(dec_step)))
                dec_step += 1
    enc_sum = gradient(("enc",), "cots_enc")
    for step in range(dec_step, dec_sum.steps):
        dec_sum.send(step, dec_sum.prepare(step))
    for step in range(enc_sum.steps):
        pair = enc_sum.prepare(step)
        if step == 0:
            pair, dec_sum.arrived = lax.optimization_barrier((pair, dec_sum.arrived))
        enc_sum.send(step, pair)
    enc_share, dec_share = enc_sum.result(), dec_sum.result()
    return tuple(
        share.reshape((1, 3, 3) + share.shape[1:]) for share in (enc_share, dec_share)
    )


def solution(mesh):
    placed = (
        P("dp", None, None, None),
        P("dp", None, None, None),
        P("dp"),
        P("section", None, None, None, None),
        P("section", None, None, None, None),
    )
    return jax.shard_map(
        shards,
        mesh=mesh,
        in_specs=placed,
        out_specs=(P("section", None, None, "dp", None), P("section", None, None, "dp", None)),
        check_vma=False,
    )
```

```python
import functools
import math

import jax
import jax.numpy as jnp
import ml_dtypes
import numpy as np
from jax import lax
from jax.experimental import pallas as pl
from jax.experimental.pallas import tpu as pltpu
from jax.sharding import PartitionSpec as P

GROUPS = 32
F32 = jnp.float32
BF16 = jnp.bfloat16
ENC_FWD, DEC_FWD, DEC_BWD, ENC_BWD = 1, 2, 3, 4
STAGE_VMEM = 3 * 1024 * 1024
GRAD_VMEM = 8 * 1024 * 1024


def embed(stamps_in, channels):
    half_width = channels // 2
    frequency = jnp.exp(-math.log(10000.0) * jnp.arange(half_width, dtype=jnp.float32) / half_width)
    angles = stamps_in.astype(jnp.float32)[:, None] * frequency[None, :]
    return jnp.concatenate([jnp.sin(angles), jnp.cos(angles)], axis=1)


def noise_levels(stamps_in):
    phase = (stamps_in.astype(jnp.float32) / 1000.0 + 0.008) / 1.008 * (math.pi / 2.0)
    signal = jnp.cos(phase) ** 2
    return (jnp.sqrt(signal), jnp.sqrt(1.0 - signal))


def stage_of(position, sections):
    lap, step = divmod(position, sections)
    section = step if lap % 2 == 0 else sections - 1 - step
    return section, lap + 1


def make_schedule(sections, samples):
    stages = 4 * sections
    ticks = []
    for tick in range(stages + 2 * (samples - 1)):
        work, moves = {}, []
        for sample in range(samples):
            position = tick - 2 * sample
            if not 0 <= position < stages:
                continue
            section, op = stage_of(position, sections)
            assert section not in work
            work[section] = (op, sample)
            if position + 1 < stages:
                target, _ = stage_of(position + 1, sections)
                if target != section:
                    moves.append((section, target))
        ticks.append((work, moves))
    return ticks


def group_sums(vectors, members):
    channels = vectors[0].shape[1]
    row = lax.broadcasted_iota(jnp.int32, (16, channels), 0)
    stacked = jnp.zeros((16, channels), F32)
    for index, vector in enumerate(vectors):
        high = vector.astype(BF16).astype(F32)
        rest = vector - high
        middle = rest.astype(BF16).astype(F32)
        for part_index, part in enumerate((high, middle, rest - middle)):
            stacked = jnp.where(row == 3 * index + part_index, part, stacked)
    summed = jnp.dot(stacked.astype(BF16), members, preferred_element_type=F32)
    return [
        summed[3 * i : 3 * i + 1] + summed[3 * i + 1 : 3 * i + 2] + summed[3 * i + 2 : 3 * i + 3]
        for i in range(len(vectors))
    ]


def spread_columns(field, breadth, windows_ref):
    pixels, channels = field.shape
    column = lax.broadcasted_iota(jnp.int32, (pixels, channels), 0) & (breadth - 1)
    before = jnp.where(column == 0, 0.0, pltpu.roll(field, 1, 0))
    after = jnp.where(column == breadth - 1, 0.0, pltpu.roll(field, pixels - 1, 0))
    edge = jnp.zeros((breadth, channels), BF16)
    for index, shifted in enumerate((before, field, after)):
        lanes = slice(index * channels, (index + 1) * channels)
        windows_ref[0:breadth, lanes] = edge
        windows_ref[breadth : breadth + pixels, lanes] = shifted.astype(BF16)
        windows_ref[breadth + pixels : 2 * breadth + pixels, lanes] = edge


def convolve(windows_ref, weight_ref, pixels, breadth):
    outputs = weight_ref.shape[2]
    channels = windows_ref.shape[1] // 3
    total = None
    for row in range(3):
        part = jnp.dot(
            windows_ref[row * breadth : row * breadth + pixels, :],
            weight_ref[3 * row : 3 * row + 3, 0:channels, :].reshape(3 * channels, outputs),
            preferred_element_type=F32,
        )
        total = part if total is None else total + part
    return total


def convolve_loop(total_ref, windows_ref, weight_ref, first, pixels, breadth):
    outputs = weight_ref.shape[2]
    channels = windows_ref.shape[1] // 3
    total_ref[...] = jnp.zeros((pixels, outputs), F32)

    def one_row(row, carry):
        start = pl.multiple_of(row * breadth, breadth)
        total_ref[...] += jnp.dot(
            windows_ref[pl.ds(start, pixels), :],
            weight_ref[pl.ds(3 * row, 3), first : first + channels, :].reshape(
                3 * channels, outputs
            ),
            preferred_element_type=F32,
        )
        return carry

    lax.fori_loop(0, 3, one_row, 0)


def chosen(index, values):
    result = jnp.int32(values[0])
    for position, value in enumerate(values):
        if value != values[0]:
            result = jnp.where(index == position, value, result)
    return result


def local_input(op, section, sections):
    return (op in (ENC_FWD, DEC_BWD) and section == 0) or (
        op in (DEC_FWD, ENC_BWD) and section == sections - 1
    )


def local_result(op, section, sections):
    return (
        op == ENC_FWD
        or (op == DEC_FWD and section == 0)
        or (op == DEC_BWD and section == sections - 1)
    )


KINDS = ("enc", "dec", "skip")


def touched(work, aside):
    ops = {op for op, _ in work.values()}
    names = ["kept", "side"]
    if aside:
        if ENC_FWD in ops:
            names += ["normed_skip", "scale_skip", "acts_enc", "turned_enc", "turned_skip"]
        if DEC_BWD in ops:
            names += ["normed_skip", "scale_skip", "cots_dec", "acts_dec", "turned_dec"]
    else:
        for op, kind in ((ENC_FWD, "enc"), (DEC_FWD, "dec")):
            if op in ops:
                names += ["normed_" + kind, "scale_" + kind, "acts_" + kind]
        for op, kind in ((ENC_BWD, "enc"), (DEC_BWD, "dec")):
            if op in ops:
                names += ["normed_" + kind, "scale_" + kind, "cots_" + kind]
    return list(dict.fromkeys(names))


def stage_kernel(work, aside, sections, breadth, factor, refs):
    pixels, channels = refs["kept"].shape[1:]
    section = lax.axis_index("section")
    jobs = [work.get(s, (0, 0)) for s in range(sections)]
    ops = {op for op, _ in jobs}
    op = chosen(section, [job[0] for job in jobs])
    slot = chosen(section, [job[1] for job in jobs])
    to_here = chosen(
        section, [int(local_result(job[0], s, sections)) for s, job in enumerate(jobs)]
    )
    lanes = pl.ds(pl.multiple_of(slot * pixels, 128), pixels)
    kept, side = refs["kept"], refs["side"]
    group_size = channels // GROUPS

    def per_kind(kind):
        which = 0 if kind == "enc" else 1
        inverse_count = 1.0 / (pixels * group_size * (1 + which))
        modulation = refs["modulation"][KINDS.index(kind), slot]
        return refs["members"].at[which], inverse_count, modulation

    def load_input():
        leaving = refs["leaving"]
        cases = {}
        for s, (job_op, _) in enumerate(jobs):
            if job_op:
                local = local_input(job_op, s, sections)
                case = "noisy" if local and job_op == ENC_FWD else "kept" if local else "arriving"
                cases.setdefault(case, []).append(s)

        def fill(case):
            if case == "noisy":
                leaving[...] = refs["levels"][0, slot] * refs["clean"][slot].astype(F32) + refs[
                    "levels"
                ][1, slot] * refs["noise"][slot].astype(F32)
            elif case == "kept":
                leaving[...] = kept[slot]
            else:
                leaving[...] = refs["arriving"][...]

        for case, places in cases.items():
            here = functools.reduce(jnp.logical_or, [section == s for s in places])
            pl.when(here)(functools.partial(fill, case))
        return leaving[...]

    def forward(kind):
        members, inverse_count, modulation = per_kind(kind)
        windows = refs["windows"]
        x = kept[slot] if aside else load_input()
        total = jnp.sum(x, axis=0, keepdims=True)
        own_mean = total * (1.0 / pixels)
        own_dev = x - own_mean
        own_square = jnp.sum(own_dev * own_dev, axis=0, keepdims=True)
        (group_total,) = group_sums([total], members[...])
        mean = group_total * inverse_count
        apart = own_mean - mean
        (group_square,) = group_sums([own_square + pixels * (apart * apart)], members[...])
        inverse_std = lax.rsqrt(group_square * inverse_count + 1e-05)
        unit = (x - mean) * inverse_std
        value = unit * modulation
        active = value / (1.0 + jnp.exp(-value))
        refs["normed_" + kind][slot] = unit
        refs["scale_" + kind][slot] = inverse_std
        spread_columns(active, breadth, windows)
        if aside:
            convolve_loop(side.at[slot], windows, refs["dec_weight"], channels, pixels, breadth)
            refs["turned_enc"][:, lanes] = refs["acts_enc"][slot].astype(F32).T.astype(BF16)
            refs["turned_skip"][:, lanes] = active.T.astype(BF16)
            return
        refs["acts_" + kind][slot] = active.astype(BF16)
        leaving = refs["leaving"]
        if kind == "enc":
            leaving[...] += convolve(windows, refs["enc_weight"], pixels, breadth)
        else:
            own = convolve(windows, refs["dec_weight"], pixels, breadth)
            leaving[...] += own + side[slot]

            @pl.when(to_here == 1)
            def _():
                leaving[...] = factor * (leaving[...] - refs["noise"][slot].astype(F32))

        keep_result()

    def keep_result():
        if any(local_result(job[0], s, sections) for s, job in enumerate(jobs)):

            @pl.when(to_here == 1)
            def _():
                kept[slot] = refs["leaving"][...]

    def backward(kind):
        members, inverse_count, modulation = per_kind(kind)
        if aside:
            given = refs["cots_dec"].at[slot]
            refs["turned_dec"][:, lanes] = refs["acts_dec"][slot].astype(F32).T.astype(BF16)
        else:
            given = refs["cots_" + kind].at[slot]
            leaving = refs["leaving"]
            load_input()
            if kind == "enc":
                leaving[...] = leaving[...] + side[slot]
            spread_columns(leaving[...], breadth, given)
        if aside:
            convolve_loop(refs["down"], given, refs["flipped_skip"], 0, pixels, breadth)
            down = refs["down"][...]
        else:
            down = convolve(given, refs["flipped_" + kind], pixels, breadth)
        unit = refs["normed_" + kind][slot]
        value = unit * modulation
        gate = 1.0 / (1.0 + jnp.exp(-value))
        slope = gate * (1.0 + value * (1.0 - gate))
        d_unit = down * slope * modulation
        sums = group_sums(
            [
                jnp.sum(d_unit, axis=0, keepdims=True),
                jnp.sum(d_unit * unit, axis=0, keepdims=True),
            ],
            members[...],
        )
        shift, stretch = sums[0] * inverse_count, sums[1] * inverse_count
        result = refs["scale_" + kind][slot] * (d_unit - shift - unit * stretch)
        if aside:
            side[slot] = result
        else:
            leaving[...] = leaving[...] + result
            keep_result()

    if aside:
        parts = ((ENC_FWD, forward, "skip"), (DEC_BWD, backward, "skip"))
    else:
        parts = (
            (ENC_FWD, forward, "enc"),
            (DEC_FWD, forward, "dec"),
            (DEC_BWD, backward, "dec"),
            (ENC_BWD, backward, "enc"),
        )
    for part_op, part, kind in parts:
        if part_op in ops:
            pl.when(op == part_op)(functools.partial(part, kind))


def call_stage(work, aside, sections, breadth, factor, arriving, consts, state):
    ops = {op for op, _ in work.values()}
    _, pixels, channels = state["kept"].shape
    vmem = pl.BlockSpec(memory_space=pltpu.VMEM)
    names = ["modulation", "members"]
    if ENC_FWD in ops and not aside:
        names.append("enc_weight")
    if (DEC_FWD in ops and not aside) or (ENC_FWD in ops and aside):
        names.append("dec_weight")
    if DEC_BWD in ops:
        names.append("flipped_skip" if aside else "flipped_dec")
    if ENC_BWD in ops and not aside:
        names.append("flipped_enc")
    starting = not aside and work.get(0, (0, 0))[0] == ENC_FWD
    if starting:
        names += ["levels", "clean"]
    if starting or (DEC_FWD in ops and not aside):
        names.append("noise")
    given = {name: consts[name] for name in names}
    if not aside and any(not local_input(op, s, sections) for s, (op, _) in work.items()):
        given["arriving"] = arriving
    used = touched(work, aside)
    present = [n for n in used if not isinstance(state[n], jax.ShapeDtypeStruct)]
    out_shape = {} if aside else {"leaving": jax.ShapeDtypeStruct((pixels, channels), F32)}
    for name in used:
        out_shape[name] = jax.ShapeDtypeStruct(state[name].shape, state[name].dtype)
    out_names = list(out_shape)

    def kernel(*refs):
        named = dict(zip(given, refs))
        named.update(zip(out_names, refs[len(given) + len(present) :]))
        named["windows"], named["down"] = refs[-2:]
        stage_kernel(work, aside, sections, breadth, factor, named)

    outs = pl.pallas_call(
        kernel,
        out_shape=list(out_shape.values()),
        in_specs=[vmem] * (len(given) + len(present)),
        out_specs=[vmem] * len(out_shape),
        scratch_shapes=[
            pltpu.VMEM((pixels + 2 * breadth, 3 * channels), BF16),
            pltpu.VMEM((pixels, channels), F32),
        ],
        input_output_aliases={
            len(given) + i: out_names.index(name) for i, name in enumerate(present)
        },
        compiler_params=pltpu.CompilerParams(vmem_limit_bytes=STAGE_VMEM),
        cost_estimate=pl.CostEstimate(flops=1000, bytes_accessed=1000, transcendentals=0),
    )(*given.values(), *[state[n] for n in present])
    named = dict(zip(out_names, outs))
    leaving = named.pop("leaving", None)
    return leaving, {**state, **named}


def flip_kernel(enc_weight, dec_weight, after, *outs):
    taps, channels, _ = enc_weight.shape

    def one_tap(tap, carry):
        tiles = (
            enc_weight[tap],
            dec_weight[tap, 0:channels, :],
            dec_weight[tap, channels : 2 * channels, :],
        )
        for tile, out in zip(tiles, outs):
            out[taps - 1 - tap] = tile.astype(F32).T.astype(BF16)
        return carry

    lax.fori_loop(0, taps, one_tap, 0)


def flip(enc_weight, dec_weight, after):
    vmem = pl.BlockSpec(memory_space=pltpu.VMEM)
    return pl.pallas_call(
        flip_kernel,
        out_shape=[jax.ShapeDtypeStruct(enc_weight.shape, BF16)] * 3,
        in_specs=[vmem] * 3,
        out_specs=[vmem] * 3,
        compiler_params=pltpu.CompilerParams(vmem_limit_bytes=STAGE_VMEM),
    )(enc_weight, dec_weight, after)


def weight_grad_kernel(breadth, halves, group, chunks, *refs):
    turned, cots, outs, (ready, sems) = refs[:halves], refs[halves], refs[-4:-2], refs[-2:]
    channels = turned[0].shape[0]
    samples = cots.shape[0]
    pixels = turned[0].shape[1] // samples
    core = lax.axis_index("dp") % 2
    rows = halves * channels // chunks // 2
    places = [divmod(2 * chunk * rows, channels) for chunk in group]

    def store(tap, slot):
        return [
            pltpu.make_async_copy(ready.at[slot, i], outs[i].at[:, tap], sems.at[slot, i])
            for i in range(2)
        ]

    def one_tap(tap, carry):
        slot = lax.rem(tap, 2)
        row, col = tap // 3, lax.rem(tap, 3)
        start = pl.multiple_of((2 - row) * breadth, breadth)
        lane = pl.multiple_of((2 - col) * channels, 128)
        lines = [turned[half][first : first + 2 * rows, :] for half, first in places]
        fields = [
            cots[sample, pl.ds(start, pixels), pl.ds(lane, channels)] for sample in range(samples)
        ]
        total = jnp.dot(
            jnp.concatenate(lines, axis=0),
            jnp.concatenate(fields, axis=0),
            preferred_element_type=F32,
        )

        @pl.when(tap >= 2)
        def _():
            for one in store(tap, slot):
                one.wait()

        pieces = total.reshape(len(group), 2, rows, channels)
        ready[slot, 0] = jnp.where(core == 0, pieces[:, 0], pieces[:, 1])
        ready[slot, 1] = jnp.where(core == 0, pieces[:, 1], pieces[:, 0])
        for one in store(tap, slot):
            one.start()
        return carry

    lax.fori_loop(0, 9, one_tap, 0)
    for tap in (7, 8):
        for one in store(tap, tap % 2):
            one.wait()


def weight_grad(turned, cots, group, breadth):
    channels = turned[0].shape[0]
    chunks = lax.axis_size("dp") // 2
    rows = len(turned) * channels // chunks // 2
    vmem = pl.BlockSpec(memory_space=pltpu.VMEM)
    hbm = pl.BlockSpec(memory_space=pltpu.HBM)
    shape = jax.ShapeDtypeStruct((len(group), 9, rows, channels), F32)
    return pl.pallas_call(
        functools.partial(weight_grad_kernel, breadth, len(turned), tuple(group), chunks),
        out_shape=[shape, shape],
        in_specs=[vmem] * (len(turned) + 1),
        out_specs=[hbm, hbm],
        scratch_shapes=[
            pltpu.VMEM((2, 2, len(group), rows, channels), F32),
            pltpu.SemaphoreType.DMA((2, 2)),
        ],
        compiler_params=pltpu.CompilerParams(vmem_limit_bytes=GRAD_VMEM),
        cost_estimate=pl.CostEstimate(flops=1000, bytes_accessed=1000, transcendentals=0),
    )(*turned, cots)


def member_matrices(channels):
    channel = np.arange(channels)
    size = channels // GROUPS
    return np.stack(
        [channel[:, None] // n == channel[None, :] // n for n in (size, 2 * size)]
    ).astype(ml_dtypes.bfloat16)


class LineSum:
    def __init__(self, make):
        self.count = lax.axis_size("dp")
        self.chips = self.count // 2
        self.steps = self.chips - 1
        self.place = lax.axis_index("dp") // 2
        self.arrived = None
        self.ends = self.swap(*make([0, self.chips - 1]))
        middle = list(range(1, self.chips - 1))
        self.middle = self.swap(*make(middle)) if middle else None

    def swap(self, kept, given):
        moves = [(d, d + 1 - 2 * (d % 2)) for d in range(self.count)]
        return kept, lax.ppermute(given, "dp", moves)

    def end(self, index):
        kept, swapped = self.ends
        return kept[index] + swapped[index]

    def between(self, chunk):
        index = jnp.clip(chunk - 1, 0, self.chips - 3)
        return sum(lax.dynamic_index_in_dim(part, index, 0, False) for part in self.middle)

    def own_pair(self, step):
        up, down = self.end(1), self.end(0)
        if step:
            back = self.chips - 1 - self.place
            up = jnp.where(self.place == step, up, self.between(back - step + 2 * self.place))
            down = jnp.where(back == step, down, self.between(step - back))
        return up, down

    def prepare(self, step):
        up, down = self.own_pair(step)
        if step:
            up, down = up + self.arrived[0], down + self.arrived[1]
        return up, down

    def send(self, step, pair):
        last = self.chips - 1
        moves = [(z, c) for z in range(min(step + 1, last)) for c in range(2)]
        up = lax.ppermute(pair[0], "dp", [(2 * z + c, 2 * z + 2 + c) for z, c in moves])
        down = lax.ppermute(
            pair[1], "dp", [(2 * (last - z) + c, 2 * (last - z) - 2 + c) for z, c in moves]
        )
        self.arrived = lax.optimization_barrier((up, down))

    def result(self):
        total = jnp.where(self.place == 0, self.end(0), self.end(1))
        if self.middle is not None:
            outer = jnp.logical_or(self.place == 0, self.place == self.chips - 1)
            total = jnp.where(outer, total, self.between(self.place))
        return total + self.arrived[0] + self.arrived[1]


def shards(clean, noise, stamps, enc_weight, dec_weight):
    sections = lax.axis_size("section")
    samples, height, breadth, channels = clean.shape
    pixels = height * breadth
    factor = 1.0 / math.sqrt(samples * lax.axis_size("dp") * pixels)
    ticks = make_schedule(sections, samples)

    levels = jnp.stack(noise_levels(stamps))
    wide = embed(stamps, 2 * channels)
    modulation = 1.0 + 0.5 * jnp.stack(
        [embed(stamps, channels), wide[:, :channels], wide[:, channels:]]
    )
    consts = {
        "modulation": modulation[:, :, None, :],
        "members": jnp.asarray(member_matrices(channels)),
        "enc_weight": enc_weight.reshape(9, channels, channels),
        "dec_weight": dec_weight.reshape(9, 2 * channels, channels),
        "levels": jnp.broadcast_to(levels[:, :, None, None], (2, samples, 1, channels)),
        "clean": clean.reshape(samples, pixels, channels),
        "noise": noise.reshape(samples, pixels, channels),
    }
    weights = (consts["enc_weight"], consts["dec_weight"])
    fresh = jax.ShapeDtypeStruct
    field = (samples, pixels, channels)
    state = {"kept": fresh(field, F32), "side": fresh(field, F32)}
    for kind in KINDS:
        state["normed_" + kind] = fresh(field, F32)
        state["scale_" + kind] = fresh((samples, 1, channels), F32)
        state["turned_" + kind] = fresh((channels, samples * pixels), BF16)
        if kind != "skip":
            state["acts_" + kind] = fresh(field, BF16)
            state["cots_" + kind] = fresh(
                (samples, pixels + 2 * breadth, 3 * channels), BF16
            )
    arriving = None
    last_dec = max(
        tick for tick, (work, _) in enumerate(ticks) if any(w[0] == DEC_BWD for w in work.values())
    )
    flip_tick = 1
    dec_sum = None
    dec_step = 0

    def gradient(kinds, cots):
        turned = [state["turned_" + kind] for kind in kinds]
        return LineSum(lambda group: weight_grad(turned, state[cots], group, breadth))

    def ahead_of(name, value):
        state[name], value = lax.optimization_barrier((state[name], value))
        return value

    for tick, (work, moves) in enumerate(ticks):
        ops = {op for op, _ in work.values()}
        leaving, state = call_stage(
            work, False, sections, breadth, factor, arriving, consts, state
        )
        if moves:
            arriving = lax.ppermute(leaving, "section", moves)
        if ops & {ENC_FWD, DEC_BWD}:
            _, state = call_stage(work, True, sections, breadth, factor, None, consts, state)
        if tick == flip_tick:
            flipped = flip(*weights, state["scale_skip"])
            flipped = ahead_of("side", flipped)
            consts.update(zip(["flipped_" + kind for kind in KINDS], flipped))
        if tick == last_dec:
            dec_sum = gradient(("dec", "skip"), "cots_dec")
        if dec_sum is not None and dec_step < dec_sum.steps and tick < len(ticks) - 1:
            if tick - last_dec == 3 * dec_step // 2:
                if dec_step == 1:
                    dec_sum.arrived, arriving = lax.optimization_barrier(
                        (dec_sum.arrived, arriving)
                    )
                dec_sum.send(dec_step, ahead_of("side", dec_sum.prepare(dec_step)))
                dec_step += 1
    enc_sum = gradient(("enc",), "cots_enc")
    for step in range(dec_step, dec_sum.steps):
        dec_sum.send(step, dec_sum.prepare(step))
    for step in range(enc_sum.steps):
        pair = enc_sum.prepare(step)
        if step == 0:
            pair, dec_sum.arrived = lax.optimization_barrier((pair, dec_sum.arrived))
        enc_sum.send(step, pair)
    enc_share, dec_share = enc_sum.result(), dec_sum.result()
    return tuple(
        share.reshape((1, 3, 3) + share.shape[1:]) for share in (enc_share, dec_share)
    )


def solution(mesh):
    placed = (
        P("dp", None, None, None),
        P("dp", None, None, None),
        P("dp"),
        P("section", None, None, None, None),
        P("section", None, None, None, None),
    )
    return jax.shard_map(
        shards,
        mesh=mesh,
        in_specs=placed,
        out_specs=(P("section", None, None, "dp", None), P("section", None, None, "dp", None)),
        check_vma=False,
    )
```

```python
import functools
import math

import jax
import jax.numpy as jnp
import ml_dtypes
import numpy as np
from jax import lax
from jax.experimental import pallas as pl
from jax.experimental.pallas import tpu as pltpu
from jax.sharding import PartitionSpec as P

GROUPS = 32
F32 = jnp.float32
BF16 = jnp.bfloat16
ENC_FWD, DEC_FWD, DEC_BWD, ENC_BWD = 1, 2, 3, 4
STAGE_VMEM = 3 * 1024 * 1024
GRAD_VMEM = 8 * 1024 * 1024


def embed(stamps_in, channels):
    half_width = channels // 2
    frequency = jnp.exp(-math.log(10000.0) * jnp.arange(half_width, dtype=jnp.float32) / half_width)
    angles = stamps_in.astype(jnp.float32)[:, None] * frequency[None, :]
    return jnp.concatenate([jnp.sin(angles), jnp.cos(angles)], axis=1)


def noise_levels(stamps_in):
    phase = (stamps_in.astype(jnp.float32) / 1000.0 + 0.008) / 1.008 * (math.pi / 2.0)
    signal = jnp.cos(phase) ** 2
    return (jnp.sqrt(signal), jnp.sqrt(1.0 - signal))


def stage_of(position, sections):
    lap, step = divmod(position, sections)
    section = step if lap % 2 == 0 else sections - 1 - step
    return section, lap + 1


def make_schedule(sections, samples):
    stages = 4 * sections
    ticks = []
    for tick in range(stages + 2 * (samples - 1)):
        work, moves = {}, []
        for sample in range(samples):
            position = tick - 2 * sample
            if not 0 <= position < stages:
                continue
            section, op = stage_of(position, sections)
            assert section not in work
            work[section] = (op, sample)
            if position + 1 < stages:
                target, _ = stage_of(position + 1, sections)
                if target != section:
                    moves.append((section, target))
        ticks.append((work, moves))
    return ticks


def group_sums(vectors, members):
    channels = vectors[0].shape[1]
    row = lax.broadcasted_iota(jnp.int32, (16, channels), 0)
    stacked = jnp.zeros((16, channels), F32)
    for index, vector in enumerate(vectors):
        high = vector.astype(BF16).astype(F32)
        rest = vector - high
        middle = rest.astype(BF16).astype(F32)
        for part_index, part in enumerate((high, middle, rest - middle)):
            stacked = jnp.where(row == 3 * index + part_index, part, stacked)
    summed = jnp.dot(stacked.astype(BF16), members, preferred_element_type=F32)
    return [
        summed[3 * i : 3 * i + 1] + summed[3 * i + 1 : 3 * i + 2] + summed[3 * i + 2 : 3 * i + 3]
        for i in range(len(vectors))
    ]


def spread_columns(field, breadth, windows_ref):
    pixels, channels = field.shape
    column = lax.broadcasted_iota(jnp.int32, (pixels, channels), 0) & (breadth - 1)
    before = jnp.where(column == 0, 0.0, pltpu.roll(field, 1, 0))
    after = jnp.where(column == breadth - 1, 0.0, pltpu.roll(field, pixels - 1, 0))
    edge = jnp.zeros((breadth, channels), BF16)
    for index, shifted in enumerate((before, field, after)):
        lanes = slice(index * channels, (index + 1) * channels)
        windows_ref[0:breadth, lanes] = edge
        windows_ref[breadth : breadth + pixels, lanes] = shifted.astype(BF16)
        windows_ref[breadth + pixels : 2 * breadth + pixels, lanes] = edge


def convolve(windows_ref, weight_ref, pixels, breadth):
    outputs = weight_ref.shape[2]
    channels = windows_ref.shape[1] // 3
    total = None
    for row in range(3):
        part = jnp.dot(
            windows_ref[row * breadth : row * breadth + pixels, :],
            weight_ref[3 * row : 3 * row + 3, 0:channels, :].reshape(3 * channels, outputs),
            preferred_element_type=F32,
        )
        total = part if total is None else total + part
    return total


def convolve_loop(total_ref, windows_ref, weight_ref, first, pixels, breadth):
    outputs = weight_ref.shape[2]
    channels = windows_ref.shape[1] // 3
    total_ref[...] = jnp.zeros((pixels, outputs), F32)

    def one_row(row, carry):
        start = pl.multiple_of(row * breadth, breadth)
        total_ref[...] += jnp.dot(
            windows_ref[pl.ds(start, pixels), :],
            weight_ref[pl.ds(3 * row, 3), first : first + channels, :].reshape(
                3 * channels, outputs
            ),
            preferred_element_type=F32,
        )
        return carry

    lax.fori_loop(0, 3, one_row, 0)


def chosen(index, values):
    result = jnp.int32(values[0])
    for position, value in enumerate(values):
        if value != values[0]:
            result = jnp.where(index == position, value, result)
    return result


def local_input(op, section, sections):
    return (op in (ENC_FWD, DEC_BWD) and section == 0) or (
        op in (DEC_FWD, ENC_BWD) and section == sections - 1
    )


def local_result(op, section, sections):
    return (
        op == ENC_FWD
        or (op == DEC_FWD and section == 0)
        or (op == DEC_BWD and section == sections - 1)
    )


KINDS = ("enc", "dec", "skip")


def touched(work, aside):
    ops = {op for op, _ in work.values()}
    names = ["kept", "side"]
    if aside:
        if ENC_FWD in ops:
            names += ["normed_skip", "scale_skip", "acts_enc", "turned_enc", "turned_skip"]
        if DEC_BWD in ops:
            names += ["normed_skip", "scale_skip", "cots_dec", "acts_dec", "turned_dec"]
    else:
        for op, kind in ((ENC_FWD, "enc"), (DEC_FWD, "dec")):
            if op in ops:
                names += ["normed_" + kind, "scale_" + kind, "acts_" + kind]
        for op, kind in ((ENC_BWD, "enc"), (DEC_BWD, "dec")):
            if op in ops:
                names += ["normed_" + kind, "scale_" + kind, "cots_" + kind]
    return list(dict.fromkeys(names))


def stage_kernel(work, aside, sections, breadth, factor, refs):
    pixels, channels = refs["kept"].shape[1:]
    section = lax.axis_index("section")
    jobs = [work.get(s, (0, 0)) for s in range(sections)]
    ops = {op for op, _ in jobs}
    op = chosen(section, [job[0] for job in jobs])
    slot = chosen(section, [job[1] for job in jobs])
    to_here = chosen(
        section, [int(local_result(job[0], s, sections)) for s, job in enumerate(jobs)]
    )
    lanes = pl.ds(pl.multiple_of(slot * pixels, 128), pixels)
    kept, side = refs["kept"], refs["side"]
    group_size = channels // GROUPS

    def per_kind(kind):
        which = 0 if kind == "enc" else 1
        inverse_count = 1.0 / (pixels * group_size * (1 + which))
        modulation = refs["modulation"][KINDS.index(kind), slot]
        return refs["members"].at[which], inverse_count, modulation

    def load_input():
        leaving = refs["leaving"]
        cases = {}
        for s, (job_op, _) in enumerate(jobs):
            if job_op:
                local = local_input(job_op, s, sections)
                case = "noisy" if local and job_op == ENC_FWD else "kept" if local else "arriving"
                cases.setdefault(case, []).append(s)

        def fill(case):
            if case == "noisy":
                leaving[...] = refs["levels"][0, slot] * refs["clean"][slot].astype(F32) + refs[
                    "levels"
                ][1, slot] * refs["noise"][slot].astype(F32)
            elif case == "kept":
                leaving[...] = kept[slot]
            else:
                leaving[...] = refs["arriving"][...]

        for case, places in cases.items():
            here = functools.reduce(jnp.logical_or, [section == s for s in places])
            pl.when(here)(functools.partial(fill, case))
        return leaving[...]

    def forward(kind):
        members, inverse_count, modulation = per_kind(kind)
        windows = refs["windows"]
        x = kept[slot] if aside else load_input()
        total = jnp.sum(x, axis=0, keepdims=True)
        own_mean = total * (1.0 / pixels)
        own_dev = x - own_mean
        own_square = jnp.sum(own_dev * own_dev, axis=0, keepdims=True)
        (group_total,) = group_sums([total], members[...])
        mean = group_total * inverse_count
        apart = own_mean - mean
        (group_square,) = group_sums([own_square + pixels * (apart * apart)], members[...])
        inverse_std = lax.rsqrt(group_square * inverse_count + 1e-05)
        unit = (x - mean) * inverse_std
        value = unit * modulation
        active = value / (1.0 + jnp.exp(-value))
        refs["normed_" + kind][slot] = unit
        refs["scale_" + kind][slot] = inverse_std
        spread_columns(active, breadth, windows)
        if aside:
            convolve_loop(side.at[slot], windows, refs["dec_weight"], channels, pixels, breadth)
            refs["turned_enc"][:, lanes] = refs["acts_enc"][slot].astype(F32).T.astype(BF16)
            refs["turned_skip"][:, lanes] = active.T.astype(BF16)
            return
        refs["acts_" + kind][slot] = active.astype(BF16)
        leaving = refs["leaving"]
        if kind == "enc":
            leaving[...] += convolve(windows, refs["enc_weight"], pixels, breadth)
        else:
            own = convolve(windows, refs["dec_weight"], pixels, breadth)
            leaving[...] += own + side[slot]

            @pl.when(to_here == 1)
            def _():
                leaving[...] = factor * (leaving[...] - refs["noise"][slot].astype(F32))

        keep_result()

    def keep_result():
        if any(local_result(job[0], s, sections) for s, job in enumerate(jobs)):

            @pl.when(to_here == 1)
            def _():
                kept[slot] = refs["leaving"][...]

    def backward(kind):
        members, inverse_count, modulation = per_kind(kind)
        if aside:
            given = refs["cots_dec"].at[slot]
            refs["turned_dec"][:, lanes] = refs["acts_dec"][slot].astype(F32).T.astype(BF16)
        else:
            given = refs["cots_" + kind].at[slot]
            leaving = refs["leaving"]
            load_input()
            if kind == "enc":
                leaving[...] = leaving[...] + side[slot]
            spread_columns(leaving[...], breadth, given)
        if aside:
            convolve_loop(refs["down"], given, refs["flipped_skip"], 0, pixels, breadth)
            down = refs["down"][...]
        else:
            down = convolve(given, refs["flipped_" + kind], pixels, breadth)
        unit = refs["normed_" + kind][slot]
        value = unit * modulation
        gate = 1.0 / (1.0 + jnp.exp(-value))
        slope = gate * (1.0 + value * (1.0 - gate))
        d_unit = down * slope * modulation
        sums = group_sums(
            [
                jnp.sum(d_unit, axis=0, keepdims=True),
                jnp.sum(d_unit * unit, axis=0, keepdims=True),
            ],
            members[...],
        )
        shift, stretch = sums[0] * inverse_count, sums[1] * inverse_count
        result = refs["scale_" + kind][slot] * (d_unit - shift - unit * stretch)
        if aside:
            side[slot] = result
        else:
            leaving[...] = leaving[...] + result
            keep_result()

    if aside:
        parts = ((ENC_FWD, forward, "skip"), (DEC_BWD, backward, "skip"))
    else:
        parts = (
            (ENC_FWD, forward, "enc"),
            (DEC_FWD, forward, "dec"),
            (DEC_BWD, backward, "dec"),
            (ENC_BWD, backward, "enc"),
        )
    for part_op, part, kind in parts:
        if part_op in ops:
            pl.when(op == part_op)(functools.partial(part, kind))


def call_stage(work, aside, sections, breadth, factor, arriving, consts, state):
    ops = {op for op, _ in work.values()}
    _, pixels, channels = state["kept"].shape
    vmem = pl.BlockSpec(memory_space=pltpu.VMEM)
    names = ["modulation", "members"]
    if ENC_FWD in ops and not aside:
        names.append("enc_weight")
    if (DEC_FWD in ops and not aside) or (ENC_FWD in ops and aside):
        names.append("dec_weight")
    if DEC_BWD in ops:
        names.append("flipped_skip" if aside else "flipped_dec")
    if ENC_BWD in ops and not aside:
        names.append("flipped_enc")
    starting = not aside and work.get(0, (0, 0))[0] == ENC_FWD
    if starting:
        names += ["levels", "clean"]
    if starting or (DEC_FWD in ops and not aside):
        names.append("noise")
    given = {name: consts[name] for name in names}
    if not aside and any(not local_input(op, s, sections) for s, (op, _) in work.items()):
        given["arriving"] = arriving
    used = touched(work, aside)
    present = [n for n in used if not isinstance(state[n], jax.ShapeDtypeStruct)]
    out_shape = {} if aside else {"leaving": jax.ShapeDtypeStruct((pixels, channels), F32)}
    for name in used:
        out_shape[name] = jax.ShapeDtypeStruct(state[name].shape, state[name].dtype)
    out_names = list(out_shape)

    def kernel(*refs):
        named = dict(zip(given, refs))
        named.update(zip(out_names, refs[len(given) + len(present) :]))
        named["windows"], named["down"] = refs[-2:]
        stage_kernel(work, aside, sections, breadth, factor, named)

    outs = pl.pallas_call(
        kernel,
        out_shape=list(out_shape.values()),
        in_specs=[vmem] * (len(given) + len(present)),
        out_specs=[vmem] * len(out_shape),
        scratch_shapes=[
            pltpu.VMEM((pixels + 2 * breadth, 3 * channels), BF16),
            pltpu.VMEM((pixels, channels), F32),
        ],
        input_output_aliases={
            len(given) + i: out_names.index(name) for i, name in enumerate(present)
        },
        compiler_params=pltpu.CompilerParams(vmem_limit_bytes=STAGE_VMEM),
        cost_estimate=pl.CostEstimate(flops=1000, bytes_accessed=1000, transcendentals=0),
    )(*given.values(), *[state[n] for n in present])
    named = dict(zip(out_names, outs))
    leaving = named.pop("leaving", None)
    return leaving, {**state, **named}


def flip_kernel(enc_weight, dec_weight, after, *outs):
    taps, channels, _ = enc_weight.shape

    def one_tap(tap, carry):
        tiles = (
            enc_weight[tap],
            dec_weight[tap, 0:channels, :],
            dec_weight[tap, channels : 2 * channels, :],
        )
        for tile, out in zip(tiles, outs):
            out[taps - 1 - tap] = tile.astype(F32).T.astype(BF16)
        return carry

    lax.fori_loop(0, taps, one_tap, 0)


def flip(enc_weight, dec_weight, after):
    vmem = pl.BlockSpec(memory_space=pltpu.VMEM)
    return pl.pallas_call(
        flip_kernel,
        out_shape=[jax.ShapeDtypeStruct(enc_weight.shape, BF16)] * 3,
        in_specs=[vmem] * 3,
        out_specs=[vmem] * 3,
        compiler_params=pltpu.CompilerParams(vmem_limit_bytes=STAGE_VMEM),
    )(enc_weight, dec_weight, after)


def weight_grad_kernel(breadth, halves, group, chunks, *refs):
    turned, cots, outs, (ready, sems) = refs[:halves], refs[halves], refs[-4:-2], refs[-2:]
    channels = turned[0].shape[0]
    samples = cots.shape[0]
    pixels = turned[0].shape[1] // samples
    core = lax.axis_index("dp") % 2
    rows = halves * channels // chunks // 2
    places = [divmod(2 * chunk * rows, channels) for chunk in group]

    def store(tap, slot):
        return [
            pltpu.make_async_copy(ready.at[slot, i], outs[i].at[:, tap], sems.at[slot, i])
            for i in range(2)
        ]

    def one_tap(row, col):
        tap = 3 * row + col
        slot = lax.rem(tap, 2)
        start = pl.multiple_of((2 - row) * breadth, breadth)
        lane = (2 - col) * channels
        lines = [turned[half][first : first + 2 * rows, :] for half, first in places]
        fields = [
            cots[sample, pl.ds(start, pixels), lane : lane + channels] for sample in range(samples)
        ]
        total = jnp.dot(
            jnp.concatenate(lines, axis=0),
            jnp.concatenate(fields, axis=0),
            preferred_element_type=F32,
        )

        @pl.when(tap >= 2)
        def _():
            for one in store(tap, slot):
                one.wait()

        pieces = total.reshape(len(group), 2, rows, channels)
        ready[slot, 0] = jnp.where(core == 0, pieces[:, 0], pieces[:, 1])
        ready[slot, 1] = jnp.where(core == 0, pieces[:, 1], pieces[:, 0])
        for one in store(tap, slot):
            one.start()

    def one_row(row, carry):
        for col in range(3):
            one_tap(row, col)
        return carry

    lax.fori_loop(0, 3, one_row, 0)
    for tap in (7, 8):
        for one in store(tap, tap % 2):
            one.wait()


def weight_grad(turned, cots, group, breadth):
    channels = turned[0].shape[0]
    chunks = lax.axis_size("dp") // 2
    rows = len(turned) * channels // chunks // 2
    vmem = pl.BlockSpec(memory_space=pltpu.VMEM)
    hbm = pl.BlockSpec(memory_space=pltpu.HBM)
    shape = jax.ShapeDtypeStruct((len(group), 9, rows, channels), F32)
    return pl.pallas_call(
        functools.partial(weight_grad_kernel, breadth, len(turned), tuple(group), chunks),
        out_shape=[shape, shape],
        in_specs=[vmem] * (len(turned) + 1),
        out_specs=[hbm, hbm],
        scratch_shapes=[
            pltpu.VMEM((2, 2, len(group), rows, channels), F32),
            pltpu.SemaphoreType.DMA((2, 2)),
        ],
        compiler_params=pltpu.CompilerParams(vmem_limit_bytes=GRAD_VMEM),
        cost_estimate=pl.CostEstimate(flops=1000, bytes_accessed=1000, transcendentals=0),
    )(*turned, cots)


def member_matrices(channels):
    channel = np.arange(channels)
    size = channels // GROUPS
    return np.stack(
        [channel[:, None] // n == channel[None, :] // n for n in (size, 2 * size)]
    ).astype(ml_dtypes.bfloat16)


class LineSum:
    def __init__(self, make):
        self.count = lax.axis_size("dp")
        self.chips = self.count // 2
        self.steps = self.chips - 1
        self.place = lax.axis_index("dp") // 2
        self.arrived = None
        self.ends = self.swap(*make([0, self.chips - 1]))
        middle = list(range(1, self.chips - 1))
        self.middle = self.swap(*make(middle)) if middle else None

    def swap(self, kept, given):
        moves = [(d, d + 1 - 2 * (d % 2)) for d in range(self.count)]
        return kept, lax.ppermute(given, "dp", moves)

    def end(self, index):
        kept, swapped = self.ends
        return kept[index] + swapped[index]

    def between(self, chunk):
        index = jnp.clip(chunk - 1, 0, self.chips - 3)
        return sum(lax.dynamic_index_in_dim(part, index, 0, False) for part in self.middle)

    def own_pair(self, step):
        up, down = self.end(1), self.end(0)
        if step:
            back = self.chips - 1 - self.place
            up = jnp.where(self.place == step, up, self.between(back - step + 2 * self.place))
            down = jnp.where(back == step, down, self.between(step - back))
        return up, down

    def prepare(self, step):
        up, down = self.own_pair(step)
        if step:
            up, down = up + self.arrived[0], down + self.arrived[1]
        return up, down

    def send(self, step, pair):
        last = self.chips - 1
        moves = [(z, c) for z in range(min(step + 1, last)) for c in range(2)]
        up = lax.ppermute(pair[0], "dp", [(2 * z + c, 2 * z + 2 + c) for z, c in moves])
        down = lax.ppermute(
            pair[1], "dp", [(2 * (last - z) + c, 2 * (last - z) - 2 + c) for z, c in moves]
        )
        self.arrived = lax.optimization_barrier((up, down))

    def result(self):
        total = jnp.where(self.place == 0, self.end(0), self.end(1))
        if self.middle is not None:
            outer = jnp.logical_or(self.place == 0, self.place == self.chips - 1)
            total = jnp.where(outer, total, self.between(self.place))
        return total + self.arrived[0] + self.arrived[1]


def shards(clean, noise, stamps, enc_weight, dec_weight):
    sections = lax.axis_size("section")
    samples, height, breadth, channels = clean.shape
    pixels = height * breadth
    factor = 1.0 / math.sqrt(samples * lax.axis_size("dp") * pixels)
    ticks = make_schedule(sections, samples)

    levels = jnp.stack(noise_levels(stamps))
    wide = embed(stamps, 2 * channels)
    modulation = 1.0 + 0.5 * jnp.stack(
        [embed(stamps, channels), wide[:, :channels], wide[:, channels:]]
    )
    consts = {
        "modulation": modulation[:, :, None, :],
        "members": jnp.asarray(member_matrices(channels)),
        "enc_weight": enc_weight.reshape(9, channels, channels),
        "dec_weight": dec_weight.reshape(9, 2 * channels, channels),
        "levels": jnp.broadcast_to(levels[:, :, None, None], (2, samples, 1, channels)),
        "clean": clean.reshape(samples, pixels, channels),
        "noise": noise.reshape(samples, pixels, channels),
    }
    weights = (consts["enc_weight"], consts["dec_weight"])
    fresh = jax.ShapeDtypeStruct
    field = (samples, pixels, channels)
    state = {"kept": fresh(field, F32), "side": fresh(field, F32)}
    for kind in KINDS:
        state["normed_" + kind] = fresh(field, F32)
        state["scale_" + kind] = fresh((samples, 1, channels), F32)
        state["turned_" + kind] = fresh((channels, samples * pixels), BF16)
        if kind != "skip":
            state["acts_" + kind] = fresh(field, BF16)
            state["cots_" + kind] = fresh(
                (samples, pixels + 2 * breadth, 3 * channels), BF16
            )
    arriving = None
    last_dec = max(
        tick for tick, (work, _) in enumerate(ticks) if any(w[0] == DEC_BWD for w in work.values())
    )
    flip_tick = min(
        tick for tick, (work, _) in enumerate(ticks) if any(w[0] == DEC_BWD for w in work.values())
    ) - 2
    dec_sum = None
    dec_step = 0

    def gradient(kinds, cots):
        turned = [state["turned_" + kind] for kind in kinds]
        return LineSum(lambda group: weight_grad(turned, state[cots], group, breadth))

    def ahead_of(name, value):
        state[name], value = lax.optimization_barrier((state[name], value))
        return value

    for tick, (work, moves) in enumerate(ticks):
        ops = {op for op, _ in work.values()}
        leaving, state = call_stage(
            work, False, sections, breadth, factor, arriving, consts, state
        )
        if moves:
            arriving = lax.ppermute(leaving, "section", moves)
        if ops & {ENC_FWD, DEC_BWD}:
            _, state = call_stage(work, True, sections, breadth, factor, None, consts, state)
        if tick == flip_tick:
            flipped = flip(*weights, state["scale_skip"])
            consts.update(zip(["flipped_" + kind for kind in KINDS], flipped))
        if tick == last_dec:
            dec_sum = gradient(("dec", "skip"), "cots_dec")
        if dec_sum is not None and dec_step < dec_sum.steps and tick < len(ticks) - 1:
            if tick - last_dec == 3 * dec_step // 2:
                if dec_step:
                    dec_sum.arrived, arriving = lax.optimization_barrier(
                        (dec_sum.arrived, arriving)
                    )
                dec_sum.send(dec_step, ahead_of("side", dec_sum.prepare(dec_step)))
                dec_step += 1
    enc_sum = gradient(("enc",), "cots_enc")
    for step in range(dec_step, dec_sum.steps):
        dec_sum.send(step, dec_sum.prepare(step))
    for step in range(enc_sum.steps):
        pair = enc_sum.prepare(step)
        if step == 0:
            pair, dec_sum.arrived = lax.optimization_barrier((pair, dec_sum.arrived))
        enc_sum.send(step, pair)
    enc_share, dec_share = enc_sum.result(), dec_sum.result()
    return tuple(
        share.reshape((1, 3, 3) + share.shape[1:]) for share in (enc_share, dec_share)
    )


def solution(mesh):
    placed = (
        P("dp", None, None, None),
        P("dp", None, None, None),
        P("dp"),
        P("section", None, None, None, None),
        P("section", None, None, None, None),
    )
    return jax.shard_map(
        shards,
        mesh=mesh,
        in_specs=placed,
        out_specs=(P("section", None, None, "dp", None), P("section", None, None, "dp", None)),
        check_vma=False,
    )
```
